32 devices in a mesh: rows: 16 (over z, y, core), cols: 2 (over x).
Axes of the slice: x: 2, y: 2, z: 4, core: 2. Of those that a mesh axis runs over, the one named last changes fastest.
Arguments:
- residual: bfloat16 [2, 8192, 8192], P(None, 'rows', 'cols'), may hold values from -6 to 6
- field_slopes: bfloat16 [4, 8192, 8192], P(None, 'rows', 'cols'), may hold values from -6 to 6
- source_tile: int32 [2, 8192, 64], P(None, 'rows', 'cols'), may hold values from 0 to 31
- row_shift: int32 [2, 8192, 64], P(None, 'rows', 'cols'), may hold values from -8 to 8
- pixel_shift: int32 [2, 8192, 64], P(None, 'rows', 'cols'), may hold values from -2 to 2
- fraction: float32 [2, 8192, 64], P(None, 'rows', 'cols'), may hold values from 0 to 1
Outputs:
- potential_step: float32 [8192, 8192], P('rows', 'cols')
The draws below stay inside these ranges and needn't reach their ends.
Inputs may be any that keep to these rules, and one draw needn't show every extreme that they name: `source_tile`: a tile number inside the group of 32 tiles that holds the destination tile.
All inputs are finite; a program needn't handle non-finite values.
Results may differ from the reference program's by a relative error of at most 0.0003.
Values may be sent and summed in bfloat16 or wider, within the bound.
No kernel may reach another device: no remote copies, remote signals or barrier semaphores. Data moves between devices by JAX's collectives and lax.ppermute only.
A program may use at most 256 MiB of HBM per device.

```python
import math
from functools import partial
import jax
import jax.numpy as jnp
from jax import lax

N = 8192
TILE = 128
PAIRS = 2
HALO = 8
SHIFT = 2
TILES = 64
N_ROWS = 16
N_COLS = 2


def set_ends(entries, stream_key, smallest, high):
    longest = entries.shape.index(max(entries.shape))
    spots = []
    for shift in (0, 1):
        where = [jax.random.randint(jax.random.fold_in(stream_key, axis), (), 0, length) for axis, length in enumerate(entries.shape)]
        where[longest] = (where[longest] + shift) % entries.shape[longest]
        spots.append(tuple(where))
    return entries.at[spots[0]].set(smallest).at[spots[1]].set(high)


def levels(own_key, dims, shards, low, high):
    def one(position, blocks):
        steps = jax.random.uniform(jax.random.fold_in(jax.random.fold_in(own_key, 6), position), (blocks,), jnp.float32, low / len(shards), high / len(shards))
        return jnp.repeat(jnp.exp(steps), dims[position] // blocks).reshape((-1,) + (1,) * (len(dims) - position - 1))

    factor_of = one(*shards[0])
    for cut in shards[1:]:
        factor_of = factor_of * one(*cut)
    return factor_of


def bell_draw(rng, dims, scale, bound, cuts=(), kind=jnp.bfloat16):
    values = jax.random.normal(rng, dims, jnp.float32) * scale
    if len(cuts) > 0:
        values = levels(rng, dims, cuts, -0.22, 0.18) * values
    return jnp.clip(values, min=-bound, max=bound).astype(kind)


def setup_inputs(seed: int = 0) -> dict:
    keys = jax.random.split(jax.random.key(seed), 7)
    return {
        "residual": bell_draw(keys[0], (2, N, N), 1.0, 6.0, ((1, 16), (2, 2))),
        "field_slopes": bell_draw(keys[1], (4, N, N), 1.0, 6.0, ((1, 16), (2, 2))),
        "source_tile": set_ends(jax.random.randint(keys[2], (PAIRS, N, TILES), 0, N // N_COLS // TILE), jax.random.fold_in(keys[2], 1), 0, (N // N_COLS // TILE) - 1).astype(jnp.int32),
        "row_shift": set_ends(jax.random.randint(keys[3], (PAIRS, N, TILES), -HALO, HALO + 1), jax.random.fold_in(keys[3], 1), -HALO, HALO).astype(jnp.int32),
        "pixel_shift": set_ends(jax.random.randint(keys[4], (PAIRS, N, TILES), -SHIFT, SHIFT + 1), jax.random.fold_in(keys[4], 1), -SHIFT, SHIFT).astype(jnp.int32),
        "fraction": jnp.clip(1.0 * jax.random.uniform(keys[5], (PAIRS, N, TILES), jnp.float32) ** levels(keys[5], (PAIRS, N, TILES), ((1, 16), (2, 2)), -0.2, 0.2), 0.0, 1.0),
    }


local_weight = 0.5


def signed_wave(counter):
    middle = N // 2
    shifted = jnp.where(counter > middle, counter - N, counter)
    shifted = jnp.where(counter == middle, 0, shifted)
    return shifted.astype(jnp.float32) * (2.0 * math.pi / N)


def sample_tile(picked, spots):
    inside = (spots >= 0) & (spots < TILE)
    clipped = jnp.clip(spots, 0, TILE - 1)
    values = jnp.take_along_axis(picked, jnp.broadcast_to(clipped[None], picked.shape), axis=4)
    return jnp.where(inside[None], values, 0.0)


def band_flow(band_index, padded, field_slopes, source_tile, row_shift, pixel_shift, fraction):
    rows_dev = N // N_ROWS
    tiles_all = N // TILE
    tiles_dev = N // N_COLS // TILE
    first_row = band_index * rows_dev
    tile_rows = lax.dynamic_slice_in_dim(padded, first_row, rows_dev + 2 * HALO, 1)
    tile_rows = tile_rows.reshape(2, (rows_dev + 2 * HALO) * tiles_all, TILE)
    sources = lax.dynamic_slice_in_dim(source_tile, first_row, rows_dev, 1)
    shifts = lax.dynamic_slice_in_dim(row_shift, first_row, rows_dev, 1)
    offsets = lax.dynamic_slice_in_dim(pixel_shift, first_row, rows_dev, 1)
    blends = lax.dynamic_slice_in_dim(fraction, first_row, rows_dev, 1)
    row_index = jnp.arange(rows_dev, dtype=jnp.int32)[None, :, None]
    tile_index = jnp.arange(tiles_all, dtype=jnp.int32)[None, None, :]
    chosen = tile_index // tiles_dev * tiles_dev + sources
    flat_index = ((row_index + HALO + shifts) * tiles_all + chosen).astype(jnp.int32)
    picked = jnp.take(tile_rows, flat_index.reshape(-1), axis=1)
    picked = picked.reshape(2, PAIRS, rows_dev, tiles_all, TILE).astype(jnp.float32)
    spots = jnp.arange(TILE, dtype=jnp.int32) + offsets[..., None]
    lower = sample_tile(picked, spots)
    upper = sample_tile(picked, spots + 1)
    blend_four = blends[None, :, :, :, None]
    pulled = jnp.sum((1.0 - blend_four) * lower + blend_four * upper, axis=1).reshape(2, rows_dev, N)
    slopes = lax.dynamic_slice_in_dim(field_slopes, first_row, rows_dev, 1).astype(jnp.float32)
    flow_across = -(pulled[0] * slopes[0] + pulled[1] * slopes[1])
    downward_flow = -(pulled[0] * slopes[2] + pulled[1] * slopes[3])
    return jnp.stack([flow_across, downward_flow])


def reference(residual, field_slopes, source_tile, row_shift, pixel_shift, fraction):
    padded = jnp.pad(residual, ((0, 0), (HALO, HALO), (0, 0)))
    bands = jnp.arange(N_ROWS, dtype=jnp.int32)
    patch_worker = partial(band_flow, padded=padded, field_slopes=field_slopes, source_tile=source_tile,
                     row_shift=row_shift, pixel_shift=pixel_shift, fraction=fraction)
    flow_maps = lax.map(patch_worker, bands)
    flow_maps = jnp.transpose(flow_maps, (1, 0, 2, 3)).reshape(2, N, N)
    spectrum_across = jnp.fft.rfft2(flow_maps[0])
    spectrum_down = jnp.fft.rfft2(flow_maps[1])
    wave_rows = signed_wave(jnp.arange(N, dtype=jnp.int32))[:, None]
    wave_cols = signed_wave(jnp.arange(N // 2 + 1, dtype=jnp.int32))[None, :]
    floored_wavenumber = 8.0 * math.pi / N
    weight = local_weight + 1.0 / (wave_rows * wave_rows + wave_cols * wave_cols + floored_wavenumber * floored_wavenumber)
    combined = (weight * wave_cols) * spectrum_across + (weight * wave_rows) * spectrum_down
    return jnp.fft.irfft2(-1j * combined, s=(N, N)).astype(jnp.float32)
```

```python
import math
from functools import partial

import jax
import jax.numpy as jnp
import ml_dtypes
import numpy as np
from jax import lax
from jax.experimental import pallas as pl
from jax.experimental.pallas import tpu as pltpu
from jax.sharding import PartitionSpec as P

TILE = 128
PAIRS = 2
HALO = 8
SHIFT = 2


local_weight = 0.5
highest = lax.Precision.HIGHEST


def with_halo(x, sides, width):
    for axis, dim in sides:
        peers, length = (lax.axis_size(axis), x.shape[dim])
        up = [(i, (i + 1) % peers) for i in range(peers - 1)]
        down = [(j, i) for i, j in up]
        last = lax.slice_in_dim(x, length - width, length, axis=dim)
        first = lax.slice_in_dim(x, 0, width, axis=dim)
        before = lax.ppermute(last, axis, up)
        after = lax.ppermute(first, axis, down)
        x = jnp.concatenate([before, x, after], axis=dim)
    return x


def phase_pair(phases, length, direction):
    angles = phases.astype(jnp.float32) * (direction * 2.0 * math.pi / length)
    return (jnp.cos(angles), jnp.sin(angles))


def fourier_matrix(length, direction):
    counter = jnp.arange(length, dtype=jnp.int32)
    cosine, sine_part = phase_pair(counter[:, None] * counter[None, :] % length, length, direction)
    return jnp.stack([jnp.stack([cosine, sine_part], 1), jnp.stack([-sine_part, cosine], 1)], 0)


def rotate(values, cosine, sine_part):
    real_part = values[0] * cosine - values[1] * sine_part
    imag_part = values[0] * sine_part + values[1] * cosine
    return jnp.stack([real_part, imag_part])


def contract_indices(formula, values, matrix):
    return jnp.einsum(
        formula, values, matrix, precision=highest, preferred_element_type=jnp.float32
    )


def signed_wave(counter, n):
    middle = n // 2
    shifted = jnp.where(counter > middle, counter - n, counter)
    shifted = jnp.where(counter == middle, 0, shifted)
    return shifted.astype(jnp.float32) * (2.0 * math.pi / n)


def across_columns(values):
    return lax.all_to_all(values, "cols", split_axis=1, concat_axis=2, tiled=True)


def across_rows(values):
    return lax.all_to_all(values, "rows", split_axis=3, concat_axis=1, tiled=True)


def remap_tiles(padded, source_tile, row_shift, pixel_shift, fraction):
    rows_dev = padded.shape[1] - 2 * HALO
    tiles_dev = padded.shape[2] // TILE
    tile_rows = padded.reshape(2, (rows_dev + 2 * HALO) * tiles_dev, TILE)
    row_index = jnp.arange(rows_dev, dtype=jnp.int32)[None, :, None]
    flat_index = (row_index + HALO + row_shift) * tiles_dev + source_tile
    picked = jnp.take(tile_rows, flat_index.reshape(-1), axis=1)
    picked = picked.reshape(2, PAIRS, rows_dev, tiles_dev, TILE)
    widened = jnp.pad(picked, ((0, 0), (0, 0), (0, 0), (0, 0), (SHIFT + 1, SHIFT + 1)))
    pulled = jnp.zeros((2, rows_dev, tiles_dev, TILE), jnp.float32)
    for offset in range(-SHIFT, SHIFT + 2):
        weights = jnp.where(pixel_shift == offset, 1.0 - fraction, 0.0)
        weights = weights + jnp.where(pixel_shift + 1 == offset, fraction, 0.0)
        start_at = SHIFT + 1 + offset
        window = widened[..., start_at : start_at + TILE].astype(jnp.float32)
        pulled = pulled + jnp.sum(window * weights[None, :, :, :, None], axis=1)
    return pulled.reshape(2, rows_dev, tiles_dev * TILE)


def weigh_spectra(power_spectra, row_wave, col_wave, n):
    floored_wavenumber = 8.0 * math.pi / n
    weight = local_weight + 1.0 / (
        row_wave * row_wave + col_wave * col_wave + floored_wavenumber * floored_wavenumber
    )
    real_part = weight * (col_wave * power_spectra[1, 0] - row_wave * power_spectra[0, 0])
    imag_part = -weight * (col_wave * power_spectra[0, 0] + row_wave * power_spectra[1, 0])
    return jnp.stack([real_part, imag_part])


GROUP = 16
SLICES = 4
STEPS = tuple(range(-SHIFT, SHIFT + 2))
VMEM_LIMIT = 48 * 2**20


def turn(x, numerator, denominator):
    numerator %= denominator
    re, im = x
    if numerator == 0:
        return x
    if 4 * numerator == denominator:
        return (-im, re)
    if 2 * numerator == denominator:
        return (-re, -im)
    if 4 * numerator == 3 * denominator:
        return (im, -re)
    if 8 * numerator % denominator == 0:
        half = math.sqrt(0.5)
        a, b = half * re, half * im
        return {1: (a - b, a + b), 3: (-a - b, a - b), 5: (b - a, -a - b), 7: (a + b, b - a)}[
            8 * numerator // denominator
        ]
    angle = 2.0 * math.pi * numerator / denominator
    c, s = math.cos(angle), math.sin(angle)
    return (re * c - im * s, re * s + im * c)


def dft(xs, sign):
    n = len(xs)
    if n == 1:
        return xs
    even, odd = dft(xs[0::2], sign), dft(xs[1::2], sign)
    odd = [turn(x, sign * k, n) for k, x in enumerate(odd)]
    first = [(e[0] + o[0], e[1] + o[1]) for e, o in zip(even, odd)]
    second = [(e[0] - o[0], e[1] - o[1]) for e, o in zip(even, odd)]
    return first + second


def staged_dft(load, store, n, sign, hold):
    outer = 8 if n >= 32 else 2
    inner = n // outer
    for a in range(outer):
        ys = dft([load(a + outer * b) for b in range(inner)], sign)
        for k, y in enumerate(ys):
            re, im = turn(y, sign * a * k, n)
            hold[k * outer + a, 0] = re
            hold[k * outer + a, 1] = im
    for k in range(inner):
        zs = dft([(hold[k * outer + a, 0], hold[k * outer + a, 1]) for a in range(outer)], sign)
        for b, z in enumerate(zs):
            store(k + inner * b, z)


def split(x):
    high = x.astype(jnp.bfloat16)
    return high, (x - high.astype(jnp.float32)).astype(jnp.bfloat16)


def product(left, right):
    dot = lambda a, b: jnp.dot(a, b, preferred_element_type=jnp.float32)
    return dot(left[0], right[0]) + (dot(left[1], right[0]) + dot(left[0], right[1]))


def halves(matrix):
    high = np.asarray(matrix, np.float32).astype(ml_dtypes.bfloat16)
    low = (np.asarray(matrix, np.float32) - high.astype(np.float32)).astype(ml_dtypes.bfloat16)
    return jnp.asarray(high), jnp.asarray(low)


def phases(product_of_indices, length):
    angle = 2.0 * np.pi * (np.asarray(product_of_indices) % length) / length
    return np.cos(angle), np.sin(angle)


class Plan:
    def __init__(self, devices):
        self.devices = devices
        self.tiles = 2 * devices
        n = self.n = TILE * self.tiles
        j = np.arange(TILE)
        c, s = phases(j[:, None] * j[None, :], TILE)
        back = TILE - 1 - j
        self.list_a = halves(np.block([[c, -s], [s, c]]))
        self.list_b = halves(np.block([[c[:, back], -s[:, back]], [s[:, back], c[:, back]]]))
        self.rows_forward = halves(np.block([[c, s], [-s, c]]))
        self.rows_inverse = halves(np.block([[c, -s], [s, c]]))
        scale = 1.0 / (2.0 * n * n)
        self.cols_inverse = halves(scale * np.block([[c, s], [-s, c]]))
        low = j < TILE // 2
        digit_a = np.where(low, j, j - TILE // 2)
        digit_b = np.where(low, np.where(j == 0, TILE // 2, TILE - j), TILE - 1 - (j - TILE // 2))
        ca, sa = phases(j[:, None] * digit_a[None, :], TILE)
        cb, sb = phases(j[:, None] * digit_b[None, :], TILE)
        blocks = []
        for mask in (low, ~low):
            blocks.append(np.concatenate([ca * mask, cb * mask, -sa * mask, -sb * mask], 1))
            blocks.append(np.concatenate([sa * mask, sb * mask, ca * mask, cb * mask], 1))
        self.special_forward = halves(np.concatenate(blocks, 0))
        freq = np.where(low, 0, devices) + self.tiles * digit_a
        ci, si = phases(freq[:, None] * j[None, :], n)
        first = np.concatenate([ci * low[:, None], ci * ~low[:, None]], 1)
        second = np.concatenate([-si * low[:, None], -si * ~low[:, None]], 1)
        second[0, :TILE] = 1.0 - 2.0 * (j % 2)
        second[0, TILE:] = 0.0
        self.special_inverse = halves(2.0 * scale * np.concatenate([first, second], 0))
        beta = np.arange(self.tiles)
        tc, ts = phases(beta[:, None] * j[None, :], n)
        self.col_twiddle = jnp.asarray(np.stack([tc, ts]), jnp.float32)
        self.row_twiddle = jnp.asarray(np.stack([tc.T, ts.T]), jnp.float32)
        self.low = low
        self.digit_a, self.digit_b = digit_a, digit_b

    def wave_of_lists(self, place):
        j = jnp.arange(TILE, dtype=jnp.int32)
        usual = place + self.tiles * j
        other = jnp.asarray(np.where(self.low, 0, self.devices) + self.tiles * self.digit_a, jnp.int32)
        other_b = (self.n - other) % self.n
        other_b = other_b.at[0].set(self.n // 2)
        a = jnp.where(place == 0, other, usual)
        b = jnp.where(place == 0, other_b, (self.n - usual) % self.n)
        return signed_wave(jnp.concatenate([a, b]), self.n).reshape(1, 2 * TILE)


def whole(shape):
    return pl.BlockSpec(shape, lambda *_: (0,) * len(shape))


def params():
    return pltpu.CompilerParams(vmem_limit_bytes=VMEM_LIMIT)


def remap_kernel(
    half_ref, above_ref, below_ref, slopes_ref, source_ref, row_ref, pixel_ref, fraction_ref,
    moves_ref, out_ref, window, picker, picked, moved,
):
    tiles = slopes_ref.shape[2] // TILE
    span = 2 * GROUP
    count = PAIRS * tiles * GROUP
    for t in range(tiles):
        cols = slice(t * TILE, (t + 1) * TILE)
        for p in range(2):
            lanes = slice(p * TILE, (p + 1) * TILE)
            window[t * span : t * span + GROUP, lanes] = above_ref[p, :, cols]
            window[t * span + GROUP : (t + 1) * span, lanes] = below_ref[p, :, cols]
    lane = lax.broadcasted_iota(jnp.int32, (GROUP, TILE), 1)
    down = lax.broadcasted_iota(jnp.int32, (GROUP, tiles), 0)
    per = TILE // span
    for k in range(PAIRS):
        source = source_ref[k]
        place = (source % per) * span + down + HALO + row_ref[k]
        block = source // per
        for t in range(tiles):
            here = slice((k * tiles + t) * GROUP, (k * tiles + t + 1) * GROUP)
            hit = jnp.where(place[:, t : t + 1] == lane, 1.0, 0.0).astype(jnp.bfloat16)
            blk = jnp.broadcast_to(block[:, t : t + 1], (GROUP, TILE))
            blk = blk.astype(jnp.float32).astype(jnp.bfloat16)
            for c in range(tiles * span // TILE):
                picker[here, c * TILE : (c + 1) * TILE] = jnp.where(
                    blk == jnp.bfloat16(c), hit, jnp.bfloat16(0)
                )
    picked[...] = jnp.dot(
        picker[...], window[...], preferred_element_type=jnp.float32
    ).astype(jnp.bfloat16)
    for p in range(2):
        moved[p * count : (p + 1) * count, :] = jnp.dot(
            picked[:, p * TILE : (p + 1) * TILE], moves_ref[...],
            preferred_element_type=jnp.float32,
        )
    for t in range(tiles):
        pulled = [None, None]
        for k in range(PAIRS):
            row0 = (k * tiles + t) * GROUP
            move = jnp.broadcast_to(pixel_ref[k][:, t : t + 1], (GROUP, TILE))
            blend = jnp.broadcast_to(fraction_ref[k][:, t : t + 1], (GROUP, TILE))
            rest = 1.0 - blend
            same = [move == step for step in STEPS[:-2]]
            for p in range(2):
                here = slice(p * count + row0, p * count + row0 + GROUP)
                part = [moved[here, i * TILE : (i + 1) * TILE] for i in range(len(STEPS))]
                near, far = part[-2], part[-1]
                for i in range(len(STEPS) - 2):
                    near = jnp.where(same[i], part[i], near)
                    far = jnp.where(same[i], part[i + 1], far)
                term = rest * near + blend * far
                pulled[p] = term if pulled[p] is None else pulled[p] + term
        cols = slice(t * TILE, (t + 1) * TILE)
        slopes = [slopes_ref[i, :, cols].astype(jnp.float32) for i in range(4)]
        out_ref[0, :, cols] = -(pulled[0] * slopes[0] + pulled[1] * slopes[1])
        out_ref[1, :, cols] = -(pulled[0] * slopes[2] + pulled[1] * slopes[3])


def remap_flow(half, part, parts, padded, slopes, source, row_shift, pixel_shift, fraction):
    rows, cols = slopes.shape[1:]
    tiles = cols // TILE
    run = TILE // parts
    steps = run // GROUP
    half_groups = rows // 2 // GROUP

    def group(l, i, half_ref):
        return half_ref[0] * half_groups + l * (TILE // GROUP) + part * steps + i

    here = lambda l, i, half_ref: (0, group(l, i, half_ref), 0)
    after = lambda l, i, half_ref: (0, group(l, i, half_ref) + 1, 0)
    j = np.arange(TILE)
    moves = np.concatenate([j[:, None] == j[None, :] + step for step in STEPS], axis=1)
    small = pl.BlockSpec((PAIRS, GROUP, tiles), here)
    depth = 2 * GROUP * tiles
    count = PAIRS * GROUP * tiles
    runs = rows // 2 // TILE
    return pl.pallas_call(
        remap_kernel,
        grid_spec=pltpu.PrefetchScalarGridSpec(
            num_scalar_prefetch=1,
            grid=(runs, steps),
            in_specs=[
                pl.BlockSpec((2, GROUP, cols), here),
                pl.BlockSpec((2, GROUP, cols), after),
                pl.BlockSpec((4, GROUP, cols), here),
                small, small, small, small,
                whole(moves.shape),
            ],
            out_specs=pl.BlockSpec((2, GROUP, cols), lambda l, i, _: (0, l * steps + i, 0)),
            scratch_shapes=[
                pltpu.VMEM((depth, 2 * TILE), jnp.bfloat16),
                pltpu.VMEM((count, depth), jnp.bfloat16),
                pltpu.VMEM((count, 2 * TILE), jnp.bfloat16),
                pltpu.VMEM((2 * count, len(STEPS) * TILE), jnp.float32),
            ],
        ),
        out_shape=jax.ShapeDtypeStruct((2, runs * run, cols), jnp.float32),
        compiler_params=params(),
        cost_estimate=pl.CostEstimate(
            flops=20_000_000 * runs * run, bytes_accessed=40 * runs * run * cols, transcendentals=0
        ),
        name="remap",
    )(half, padded, padded, slopes, source, row_shift, pixel_shift, fraction,
      jnp.asarray(moves, jnp.bfloat16))


def cols_forward_kernel(
    sign_ref, own_ref, got_ref, twiddle_ref, a_high, a_low, b_high, b_low, s_high, s_low,
    out_ref, xa_high, xa_low, xb_high, xb_low, hold,
):
    devices = out_ref.shape[0]
    rows = out_ref.shape[1]
    sign = sign_ref[0]

    def block(r, carry):
        at = pl.ds(pl.multiple_of(r * GROUP, GROUP), GROUP)

        def put(beta, z):
            tc, ts = twiddle_ref[0, beta : beta + 1, :], twiddle_ref[1, beta : beta + 1, :]
            re, im = z[0] * tc + z[1] * ts, z[1] * tc - z[0] * ts
            if beta < devices:
                slot, high, low = beta, xa_high, xa_low
            else:
                slot, high, low = (2 * devices - beta) % devices, xb_high, xb_low
            for i, value in enumerate((re, im)):
                h, l = split(value)
                high[slot, at, i * TILE : (i + 1) * TILE] = h
                low[slot, at, i * TILE : (i + 1) * TILE] = l

        def both(t):
            cols = slice(t * TILE, (t + 1) * TILE)
            return [(own_ref[p, at, cols], got_ref[p, at, cols]) for p in range(2)]

        def total(t):
            return tuple(a + b for a, b in both(t))

        def gap(t):
            return turn(tuple((a - b) * sign for a, b in both(t)), -t, 2 * devices)

        staged_dft(total, lambda k, z: put(2 * k, z), devices, -1, hold)
        staged_dft(gap, lambda k, z: put(2 * k + 1, z), devices, -1, hold)
        return carry

    lax.fori_loop(0, rows // GROUP, block, 0)
    flat = (devices - 1) * rows
    for i, (high, low, mh, ml) in enumerate(
        ((xa_high, xa_low, a_high, a_low), (xb_high, xb_low, b_high, b_low))
    ):
        left = tuple(x[1:].reshape(flat, 2 * TILE) for x in (high, low))
        value = product(left, (mh[...], ml[...]))
        for part in range(2):
            lanes = slice((2 * part + i) * TILE, (2 * part + i + 1) * TILE)
            out_ref[1:, :, lanes] = value[:, part * TILE : (part + 1) * TILE].reshape(
                devices - 1, rows, TILE
            )
    left = tuple(
        jnp.concatenate([xa[0], xb[0]], axis=1)
        for xa, xb in ((xa_high, xb_high), (xa_low, xb_low))
    )
    out_ref[0] = product(left, (s_high[...], s_low[...]))


def cols_forward(plan, sign, own, got):
    rows, cols = own.shape[1:]
    d = plan.devices
    step = 2 * GROUP
    data = pl.BlockSpec((2, step, cols), lambda i: (0, i, 0))
    square = whole((2 * TILE, 2 * TILE))
    wide = whole((4 * TILE, 4 * TILE))
    return pl.pallas_call(
        cols_forward_kernel,
        grid=(rows // step,),
        in_specs=[
            pl.BlockSpec(memory_space=pltpu.SMEM), data, data, whole(plan.col_twiddle.shape),
            square, square, square, square, wide, wide,
        ],
        out_specs=pl.BlockSpec((d, step, 4 * TILE), lambda i: (0, i, 0)),
        out_shape=jax.ShapeDtypeStruct((d, rows, 4 * TILE), jnp.float32),
        scratch_shapes=[pltpu.VMEM((d, step, 2 * TILE), jnp.bfloat16)] * 4
        + [pltpu.VMEM((d, 2, GROUP, TILE), jnp.float32)],
        compiler_params=params(),
        cost_estimate=pl.CostEstimate(
            flops=4096 * rows * cols, bytes_accessed=32 * rows * cols, transcendentals=0
        ),
        name="cols_forward",
    )(sign, own, got, plan.col_twiddle, *plan.list_a, *plan.list_b, *plan.special_forward)


def rows_forward_kernel(x_ref, twiddle_ref, out_ref, hold):
    tiles, _, lanes = x_ref.shape
    half = lanes // 2
    twiddle = (twiddle_ref[0], twiddle_ref[1])

    def load(s):
        return x_ref[s, :, :half], x_ref[s, :, half:]

    def store(k, z):
        tc, ts = twiddle[0][:, k : k + 1], twiddle[1][:, k : k + 1]
        out_ref[k, :, :half] = z[0] * tc + z[1] * ts
        out_ref[k, :, half:] = z[1] * tc - z[0] * ts

    staged_dft(load, store, tiles, -1, hold)


def rows_forward(plan, part, x):
    tiles, rows, lanes = x.shape
    step = 8
    return pl.pallas_call(
        rows_forward_kernel,
        grid=(rows // step,),
        in_specs=[
            pl.BlockSpec((tiles, step, lanes), lambda i: (0, i, 0)),
            pl.BlockSpec((2, step, tiles), lambda i: (0, part * (rows // step) + i, 0)),
        ],
        out_specs=pl.BlockSpec((tiles, step, lanes), lambda i: (0, i, 0)),
        out_shape=jax.ShapeDtypeStruct((tiles, rows, lanes), jnp.float32),
        scratch_shapes=[pltpu.VMEM((tiles, 2, step, lanes // 2), jnp.float32)],
        compiler_params=params(),
        cost_estimate=pl.CostEstimate(
            flops=64 * x.size, bytes_accessed=8 * x.size, transcendentals=0
        ),
        name="rows_forward",
    )(x, plan.row_twiddle)


def weigh_kernel(n, parts, *refs):
    x_refs = refs[:parts]
    f_high, f_low, g_high, g_low, wave_ref, out_ref = refs[parts:]
    batch, _, lanes = out_ref.shape
    half = lanes // 2
    tiles = n // TILE
    col_wave = wave_ref[...]
    floored = 8.0 * math.pi / n
    col_part = col_wave * col_wave + floored * floored
    digit = lax.broadcasted_iota(jnp.int32, (TILE, half), 0)
    for b in range(batch):
        x = jnp.concatenate(
            [r[b, :, :half] for r in x_refs] + [r[b, :, half:] for r in x_refs], axis=0
        )
        z = product((f_high[...], f_low[...]), split(x))
        row_wave = signed_wave(pl.program_id(0) * batch + b + tiles * digit, n)
        weight = local_weight + 1.0 / (row_wave * row_wave + col_part)
        re, im = z[:TILE], z[TILE:]
        z = jnp.concatenate(
            [weight * (col_wave * im - row_wave * re), -weight * (col_wave * re + row_wave * im)],
            axis=0,
        )
        y = product((g_high[...], g_low[...]), split(z))
        out_ref[b, :, :half] = y[:TILE]
        out_ref[b, :, half:] = y[TILE:]


def weigh(plan, wave, xs):
    tiles, rows, lanes = xs[0].shape
    parts = len(xs)
    batch = 4
    square = whole((2 * TILE, 2 * TILE))
    return pl.pallas_call(
        partial(weigh_kernel, plan.n, parts),
        grid=(tiles // batch,),
        in_specs=[pl.BlockSpec((batch, rows, lanes), lambda i: (i, 0, 0))] * parts
        + [square] * 4 + [whole(wave.shape)],
        out_specs=pl.BlockSpec((batch, parts * rows, lanes), lambda i: (i, 0, 0)),
        out_shape=jax.ShapeDtypeStruct((tiles, parts * rows, lanes), jnp.float32),
        compiler_params=params(),
        cost_estimate=pl.CostEstimate(
            flops=4096 * parts * xs[0].size, bytes_accessed=8 * parts * xs[0].size, transcendentals=0
        ),
        name="weigh",
    )(*xs, *plan.rows_forward, *plan.rows_inverse, wave)


def rows_inverse_kernel(x_ref, twiddle_ref, special_ref, out_ref, hold):
    tiles, _, lanes = x_ref.shape
    half = lanes // 2
    twiddle = (twiddle_ref[0], twiddle_ref[1])
    special = special_ref[...] > 0.5

    def load(k):
        tc, ts = twiddle[0][:, k : k + 1], twiddle[1][:, k : k + 1]
        re, im = x_ref[k, :, :half], x_ref[k, :, half:]
        return re * tc - im * ts, im * tc + re * ts

    def store(s, z):
        re_a, re_b = z[0][:, :TILE], z[0][:, TILE:]
        im_a, im_b = z[1][:, :TILE], z[1][:, TILE:]
        out_ref[s, :, :TILE] = jnp.where(special, re_a, re_a + re_b)
        out_ref[s, :, TILE:] = jnp.where(special, re_b, im_a - im_b)

    staged_dft(load, store, tiles, 1, hold)


def rows_inverse(plan, part, parts, special, x):
    tiles, rows, lanes = x.shape
    step = 8
    run = rows // parts // step
    return pl.pallas_call(
        rows_inverse_kernel,
        grid=(run,),
        in_specs=[
            pl.BlockSpec((tiles, step, lanes), lambda i: (0, part * run + i, 0)),
            pl.BlockSpec((2, step, tiles), lambda i: (0, part * run + i, 0)),
            whole(special.shape),
        ],
        out_specs=pl.BlockSpec((tiles, step, lanes // 2), lambda i: (0, i, 0)),
        out_shape=jax.ShapeDtypeStruct((tiles, rows // parts, lanes // 2), jnp.float32),
        scratch_shapes=[pltpu.VMEM((tiles, 2, step, lanes // 2), jnp.float32)],
        compiler_params=params(),
        cost_estimate=pl.CostEstimate(
            flops=64 * x.size // parts, bytes_accessed=6 * x.size // parts, transcendentals=0
        ),
        name="rows_inverse",
    )(x, plan.row_twiddle, special)


def cols_inverse_kernel(
    col_ref, sign_ref, x_ref, twiddle_ref, g_high, g_low, s_high, s_low, *rest,
):
    keep_ref, send_ref, spectrum, hold = rest[-4:]
    devices, rows, _ = x_ref.shape
    flat = (devices - 1) * rows
    value = product(split(x_ref[1:].reshape(flat, 2 * TILE)), (g_high[...], g_low[...]))
    spectrum[1:] = value.reshape(devices - 1, rows, 2 * TILE)
    spectrum[0] = product(split(x_ref[0]), (s_high[...], s_low[...]))
    sign = sign_ref[0]

    def block(r, carry):
        at = pl.ds(pl.multiple_of(r * GROUP, GROUP), GROUP)

        def point(k):
            tc, ts = twiddle_ref[0, k : k + 1, :], twiddle_ref[1, k : k + 1, :]
            if k % 2:
                tc, ts = tc * sign, ts * sign
            re, im = spectrum[k, at, :TILE], spectrum[k, at, TILE:]
            return re * tc - im * ts, im * tc + re * ts

        def load(k):
            if k == 0:
                p, q = spectrum[0, at, :TILE], spectrum[0, at, TILE:]
                return p + q, p - q
            (a, b), (c, d) = point(k), point(devices - k)
            odd = turn((a - c, b + d), k, 2 * devices)
            return a + c - odd[1], b - d + odd[0]

        def store(n, z):
            for i in range(2):
                t = 2 * n + i
                ref = keep_ref if t < devices else send_ref
                t %= devices
                ref[at, t * TILE : (t + 1) * TILE] = z[i]

        staged_dft(load, store, devices, 1, hold)
        return carry

    lax.fori_loop(0, rows // GROUP, block, 0)


def place_block(part, parts, half_rows, step):
    run = TILE // parts // step
    return lambda l, i, half_ref: (
        half_ref[0] * (half_rows // step) + l * (TILE // step) + part * run + i, 0
    )


def cols_inverse(plan, part, parts, half, sign, x, shape, image):
    d, rows, _ = x.shape
    step = min(2 * GROUP, TILE // parts)
    runs = rows * parts // TILE
    per = TILE // parts // step
    cols = shape[1]
    square = whole((2 * TILE, 2 * TILE))
    smem = pl.BlockSpec(memory_space=pltpu.SMEM)
    extra = [] if image is None else [image]
    return pl.pallas_call(
        cols_inverse_kernel,
        grid_spec=pltpu.PrefetchScalarGridSpec(
            num_scalar_prefetch=1,
            grid=(runs, per),
            in_specs=[
                smem, pl.BlockSpec((d, step, 2 * TILE), lambda l, i, _: (0, l * per + i, 0)),
                whole(plan.col_twiddle.shape), square, square, square, square,
            ] + [pl.BlockSpec(memory_space=pl.ANY)] * len(extra),
            out_specs=[
                pl.BlockSpec((step, cols), place_block(part, parts, shape[0] // 2, step)),
                pl.BlockSpec((step, cols), lambda l, i, _: (l * per + i, 0)),
            ],
            scratch_shapes=[
                pltpu.VMEM((d, step, 2 * TILE), jnp.float32),
                pltpu.VMEM((d, 2, GROUP, TILE), jnp.float32),
            ],
        ),
        out_shape=[
            jax.ShapeDtypeStruct(shape, jnp.float32),
            jax.ShapeDtypeStruct((rows, cols), jnp.float32),
        ],
        input_output_aliases={8: 0} if extra else {},
        compiler_params=params(),
        cost_estimate=pl.CostEstimate(
            flops=2048 * x.size, bytes_accessed=8 * x.size, transcendentals=0
        ),
        name="cols_inverse",
    )(half, sign, x, plan.col_twiddle, *plan.cols_inverse, *plan.special_inverse, *extra)


def place_kernel(half_ref, got_ref, image_ref, out_ref):
    out_ref[...] = got_ref[...]


def place_rows(part, parts, half, got, image):
    rows, cols = got.shape
    step = min(2 * GROUP, TILE // parts)
    runs = rows * parts // TILE
    per = TILE // parts // step
    return pl.pallas_call(
        place_kernel,
        grid_spec=pltpu.PrefetchScalarGridSpec(
            num_scalar_prefetch=1,
            grid=(runs, per),
            in_specs=[
                pl.BlockSpec((step, cols), lambda l, i, _: (l * per + i, 0)),
                pl.BlockSpec(memory_space=pl.ANY),
            ],
            out_specs=pl.BlockSpec(
                (step, cols), place_block(part, parts, image.shape[0] // 2, step)
            ),
        ),
        out_shape=jax.ShapeDtypeStruct(image.shape, jnp.float32),
        input_output_aliases={2: 0},
        compiler_params=params(),
        cost_estimate=pl.CostEstimate(flops=0, bytes_accessed=8 * got.size, transcendentals=0),
        name="place_rows",
    )(half, got, image)


def paired(residual, field_slopes, source_tile, row_shift, pixel_shift, fraction):
    rows_dev, cols_dev = residual.shape[1:]
    devices = lax.axis_size("rows") * lax.axis_size("cols")
    plan = Plan(devices)
    parts = SLICES
    col = lax.axis_index("cols").astype(jnp.int32)
    place = lax.axis_index("rows").astype(jnp.int32) * 2 + col
    mine, other = col.reshape(1), (1 - col).reshape(1)
    sign = (1 - 2 * col).astype(jnp.float32).reshape(1)
    swap = [(0, 1), (1, 0)]
    both = ("rows", "cols")
    padded = with_halo(residual, (("rows", 1),), HALO)
    args = (padded, field_slopes, source_tile, row_shift, pixel_shift, fraction)
    lane = jnp.arange(TILE, dtype=jnp.int32).reshape(1, TILE)
    special = jnp.where((lane == 0) & (place == 0), 1.0, 0.0)
    wave = plan.wave_of_lists(place)
    spectra = []
    for m in range(parts):
        away = remap_flow(other, m, parts, *args)
        got = lax.ppermute(away, "cols", swap)
        own = remap_flow(mine, m, parts, *args)
        lists = cols_forward(plan, sign, own, got)
        lists = lax.all_to_all(lists, both, split_axis=0, concat_axis=0, tiled=True)
        rows = lists.shape[1]
        lists = lists.reshape(2 * devices, rows // 2, 4 * TILE)
        spectra.append(rows_forward(plan, m, lists))
    mixed = weigh(plan, wave, spectra)
    image = None
    sent = []
    for m in range(parts):
        folded = rows_inverse(plan, m, parts, special, mixed)
        folded = folded.reshape(devices, 2 * folded.shape[1], 2 * TILE)
        folded = lax.all_to_all(folded, both, split_axis=0, concat_axis=0, tiled=True)
        image, away = cols_inverse(
            plan, m, parts, mine, sign, folded, (rows_dev, cols_dev), image
        )
        sent.append(lax.ppermute(away, "cols", swap))
    for m in range(parts):
        image = place_rows(m, parts, other, sent[m], image)
    return image


def general(residual, field_slopes, source_tile, row_shift, pixel_shift, fraction):
    padded = with_halo(residual, (("rows", 1),), HALO)
    pulled = remap_tiles(padded, source_tile, row_shift, pixel_shift, fraction)
    slopes = field_slopes.astype(jnp.float32)
    flow_across = -(pulled[0] * slopes[0] + pulled[1] * slopes[1])
    downward_flow = -(pulled[0] * slopes[2] + pulled[1] * slopes[3])
    rows_dev = residual.shape[1]
    cols_dev = residual.shape[2]
    rows_count = lax.axis_size("rows")
    cols_count = lax.axis_size("cols")
    part_rows = rows_dev // cols_count
    n = rows_dev * rows_count
    spread = rows_count // cols_count
    col_index = lax.axis_index("cols")
    row_place = lax.axis_index("rows")
    compact_forward_transform = fourier_matrix(rows_count, -1)
    large_forward = fourier_matrix(rows_dev, -1)
    compact_inverse_transform = fourier_matrix(rows_count, 1)
    large_inverse = fourier_matrix(rows_dev, 1)
    wave_index = jnp.arange(rows_count, dtype=jnp.int32)
    pixel_index = jnp.arange(rows_dev, dtype=jnp.int32)
    band = col_index * part_rows + jnp.arange(part_rows, dtype=jnp.int32)
    stacked_planes = jnp.stack([flow_across, downward_flow]).reshape(2, rows_dev, 1, cols_dev)
    stacked_planes = across_columns(stacked_planes).reshape(2, part_rows, rows_count, rows_dev)
    power_spectra = contract_indices("pibc,pbqk->qikc", stacked_planes, compact_forward_transform)[
        :, None
    ]
    cosine, sine_part = phase_pair(wave_index[:, None] * pixel_index[None, :], n, -1)
    power_spectra = rotate(power_spectra, cosine, sine_part)
    power_spectra = contract_indices("pfikc,pcql->qfikl", power_spectra, large_forward)
    fields = power_spectra.shape[1]
    back_cos, back_sin = phase_pair(wave_index[:, None] * pixel_index[None, :], n, 1)
    power_spectra = across_rows(power_spectra)
    power_spectra = power_spectra.reshape(2, fields, rows_count, part_rows, rows_dev)
    power_spectra = contract_indices("pfrik,prqm->qfmik", power_spectra, compact_forward_transform)
    band_cos, band_sin = phase_pair(wave_index[:, None] * band[None, :], n, -1)
    power_spectra = rotate(power_spectra, band_cos[:, :, None], band_sin[:, :, None])
    power_spectra = across_columns(
        power_spectra.reshape(2 * fields, rows_count, part_rows, rows_dev)
    )
    power_spectra = power_spectra.reshape(2, fields, spread, rows_dev, rows_dev)
    power_spectra = contract_indices("pfmsk,psql->qfmlk", power_spectra, large_forward)
    row_freq = (
        rows_count * pixel_index[None, :]
        + (col_index * spread + jnp.arange(spread, dtype=jnp.int32))[:, None]
    )
    row_wave = signed_wave(row_freq, n)[:, :, None]
    col_wave = signed_wave(rows_count * pixel_index + row_place, n)
    mixed = weigh_spectra(power_spectra, row_wave, col_wave, n)
    mixed = contract_indices("pmlk,plqs->qsmk", mixed, large_inverse)
    mixed = across_columns(mixed)
    band_cos, band_sin = phase_pair(band[:, None] * wave_index[None, :], n, 1)
    mixed = rotate(mixed, band_cos[:, :, None], band_sin[:, :, None])
    mixed = contract_indices("pimk,pmqr->qirk", mixed, compact_inverse_transform)
    mixed = across_rows(mixed.reshape(2, 1, part_rows, rows_count, rows_dev))
    mixed = mixed.reshape(2, rows_count, part_rows, rows_dev)
    mixed = contract_indices("pnik,pkqa->qina", mixed, large_inverse)
    mixed = rotate(mixed, back_cos, back_sin)
    image = jnp.einsum(
        "pina,pnb->iba",
        mixed,
        compact_inverse_transform[:, :, 0, :],
        precision=highest,
        preferred_element_type=jnp.float32,
    )
    image = image.reshape(part_rows, cols_count, cols_dev) * (1.0 / (n * n))
    return lax.all_to_all(image, "cols", split_axis=1, concat_axis=0, tiled=True).reshape(
        rows_dev, cols_dev
    )


def per_device(*arrays):
    rows_dev, cols_dev = arrays[0].shape[1:]
    rows_count, cols_count = lax.axis_size("rows"), lax.axis_size("cols")
    devices = rows_count * cols_count
    if cols_count == 2 and rows_dev * rows_count == cols_dev * cols_count == 2 * TILE * devices:
        return paired(*arrays)
    return general(*arrays)


def solution(mesh):
    return jax.shard_map(
        per_device,
        mesh=mesh,
        in_specs=(
            P(None, "rows", "cols"),
            P(None, "rows", "cols"),
            P(None, "rows", "cols"),
            P(None, "rows", "cols"),
            P(None, "rows", "cols"),
            P(None, "rows", "cols"),
        ),
        out_specs=P("rows", "cols"),
        check_vma=False,
    )
```

```python
import math
from functools import partial

import jax
import jax.numpy as jnp
import ml_dtypes
import numpy as np
from jax import lax
from jax.experimental import pallas as pl
from jax.experimental.pallas import tpu as pltpu
from jax.sharding import PartitionSpec as P

TILE = 128
PAIRS = 2
HALO = 8
SHIFT = 2


local_weight = 0.5
highest = lax.Precision.HIGHEST


def with_halo(x, sides, width):
    for axis, dim in sides:
        peers, length = (lax.axis_size(axis), x.shape[dim])
        up = [(i, (i + 1) % peers) for i in range(peers - 1)]
        down = [(j, i) for i, j in up]
        last = lax.slice_in_dim(x, length - width, length, axis=dim)
        first = lax.slice_in_dim(x, 0, width, axis=dim)
        before = lax.ppermute(last, axis, up)
        after = lax.ppermute(first, axis, down)
        x = jnp.concatenate([before, x, after], axis=dim)
    return x


def phase_pair(phases, length, direction):
    angles = phases.astype(jnp.float32) * (direction * 2.0 * math.pi / length)
    return (jnp.cos(angles), jnp.sin(angles))


def fourier_matrix(length, direction):
    counter = jnp.arange(length, dtype=jnp.int32)
    cosine, sine_part = phase_pair(counter[:, None] * counter[None, :] % length, length, direction)
    return jnp.stack([jnp.stack([cosine, sine_part], 1), jnp.stack([-sine_part, cosine], 1)], 0)


def rotate(values, cosine, sine_part):
    real_part = values[0] * cosine - values[1] * sine_part
    imag_part = values[0] * sine_part + values[1] * cosine
    return jnp.stack([real_part, imag_part])


def contract_indices(formula, values, matrix):
    return jnp.einsum(
        formula, values, matrix, precision=highest, preferred_element_type=jnp.float32
    )


def signed_wave(counter, n):
    middle = n // 2
    shifted = jnp.where(counter > middle, counter - n, counter)
    shifted = jnp.where(counter == middle, 0, shifted)
    return shifted.astype(jnp.float32) * (2.0 * math.pi / n)


def across_columns(values):
    return lax.all_to_all(values, "cols", split_axis=1, concat_axis=2, tiled=True)


def across_rows(values):
    return lax.all_to_all(values, "rows", split_axis=3, concat_axis=1, tiled=True)


def remap_tiles(padded, source_tile, row_shift, pixel_shift, fraction):
    rows_dev = padded.shape[1] - 2 * HALO
    tiles_dev = padded.shape[2] // TILE
    tile_rows = padded.reshape(2, (rows_dev + 2 * HALO) * tiles_dev, TILE)
    row_index = jnp.arange(rows_dev, dtype=jnp.int32)[None, :, None]
    flat_index = (row_index + HALO + row_shift) * tiles_dev + source_tile
    picked = jnp.take(tile_rows, flat_index.reshape(-1), axis=1)
    picked = picked.reshape(2, PAIRS, rows_dev, tiles_dev, TILE)
    widened = jnp.pad(picked, ((0, 0), (0, 0), (0, 0), (0, 0), (SHIFT + 1, SHIFT + 1)))
    pulled = jnp.zeros((2, rows_dev, tiles_dev, TILE), jnp.float32)
    for offset in range(-SHIFT, SHIFT + 2):
        weights = jnp.where(pixel_shift == offset, 1.0 - fraction, 0.0)
        weights = weights + jnp.where(pixel_shift + 1 == offset, fraction, 0.0)
        start_at = SHIFT + 1 + offset
        window = widened[..., start_at : start_at + TILE].astype(jnp.float32)
        pulled = pulled + jnp.sum(window * weights[None, :, :, :, None], axis=1)
    return pulled.reshape(2, rows_dev, tiles_dev * TILE)


def weigh_spectra(power_spectra, row_wave, col_wave, n):
    floored_wavenumber = 8.0 * math.pi / n
    weight = local_weight + 1.0 / (
        row_wave * row_wave + col_wave * col_wave + floored_wavenumber * floored_wavenumber
    )
    real_part = weight * (col_wave * power_spectra[1, 0] - row_wave * power_spectra[0, 0])
    imag_part = -weight * (col_wave * power_spectra[0, 0] + row_wave * power_spectra[1, 0])
    return jnp.stack([real_part, imag_part])


GROUP = 16
SLICES = 4
STEPS = tuple(range(-SHIFT, SHIFT + 2))
VMEM_LIMIT = 48 * 2**20


def turn(x, numerator, denominator):
    numerator %= denominator
    re, im = x
    if numerator == 0:
        return x
    if 4 * numerator == denominator:
        return (-im, re)
    if 2 * numerator == denominator:
        return (-re, -im)
    if 4 * numerator == 3 * denominator:
        return (im, -re)
    if 8 * numerator % denominator == 0:
        half = math.sqrt(0.5)
        a, b = half * re, half * im
        return {1: (a - b, a + b), 3: (-a - b, a - b), 5: (b - a, -a - b), 7: (a + b, b - a)}[
            8 * numerator // denominator
        ]
    angle = 2.0 * math.pi * numerator / denominator
    c, s = math.cos(angle), math.sin(angle)
    return (re * c - im * s, re * s + im * c)


def dft(xs, sign):
    n = len(xs)
    if n == 1:
        return xs
    even, odd = dft(xs[0::2], sign), dft(xs[1::2], sign)
    odd = [turn(x, sign * k, n) for k, x in enumerate(odd)]
    first = [(e[0] + o[0], e[1] + o[1]) for e, o in zip(even, odd)]
    second = [(e[0] - o[0], e[1] - o[1]) for e, o in zip(even, odd)]
    return first + second


def staged_dft(load, store, n, sign, hold):
    outer = 8 if n >= 32 else 2
    inner = n // outer
    for a in range(outer):
        ys = dft([load(a + outer * b) for b in range(inner)], sign)
        for k, y in enumerate(ys):
            re, im = turn(y, sign * a * k, n)
            hold[k * outer + a, 0] = re
            hold[k * outer + a, 1] = im
    for k in range(inner):
        zs = dft([(hold[k * outer + a, 0], hold[k * outer + a, 1]) for a in range(outer)], sign)
        for b, z in enumerate(zs):
            store(k + inner * b, z)


def split(x):
    high = x.astype(jnp.bfloat16)
    return high, (x - high.astype(jnp.float32)).astype(jnp.bfloat16)


def product(left, right):
    dot = lambda a, b: jnp.dot(a, b, preferred_element_type=jnp.float32)
    return dot(left[0], right[0]) + (dot(left[1], right[0]) + dot(left[0], right[1]))


LOG_STEP = math.log(2.0) / 1024.0
TOP = 32767.0


def scale_code(largest):
    return jnp.floor(jnp.log(jnp.maximum(largest, 1e-33)) / LOG_STEP).astype(jnp.int32) + 2


def unit_of(code):
    return jnp.exp(code.astype(jnp.float32) * LOG_STEP) * (1.0 / TOP)


def pack(first, second, code):
    inverse = 1.0 / unit_of(code)
    a, b = (
        jnp.clip(jnp.floor(x * inverse + 0.5), -TOP, TOP).astype(jnp.int32)
        for x in (first, second)
    )
    return (a << 16) | (b & 0xFFFF)


def unpack(packed, unit):
    first, second = packed >> 16, (packed << 16) >> 16
    return first.astype(jnp.float32) * unit, second.astype(jnp.float32) * unit


def largest_of(first, second, axis):
    return jnp.max(jnp.maximum(jnp.abs(first), jnp.abs(second)), axis=axis, keepdims=True)


def put_row(ref, where, row, value):
    old = ref[where]
    lane_row = lax.broadcasted_iota(jnp.int32, old.shape, old.ndim - 2)
    ref[where] = jnp.where(lane_row == row, value, jnp.where(row == 0, 0, old))


def take_row(tile, row):
    rows = lax.broadcasted_iota(jnp.int32, tile.shape, tile.ndim - 2)
    return jnp.sum(jnp.where(rows == row, tile, 0), axis=tile.ndim - 2, keepdims=True)


def scale_rows(count):
    return -(-count // 8) * 8


def halves(matrix):
    high = np.asarray(matrix, np.float32).astype(ml_dtypes.bfloat16)
    low = (np.asarray(matrix, np.float32) - high.astype(np.float32)).astype(ml_dtypes.bfloat16)
    return jnp.asarray(high), jnp.asarray(low)


def phases(product_of_indices, length):
    angle = 2.0 * np.pi * (np.asarray(product_of_indices) % length) / length
    return np.cos(angle), np.sin(angle)


class Plan:
    def __init__(self, devices):
        self.devices = devices
        self.tiles = 2 * devices
        n = self.n = TILE * self.tiles
        j = np.arange(TILE)
        c, s = phases(j[:, None] * j[None, :], TILE)
        back = TILE - 1 - j
        self.list_a = halves(np.block([[c, -s], [s, c]]))
        self.list_b = halves(np.block([[c[:, back], -s[:, back]], [s[:, back], c[:, back]]]))
        self.rows_forward = halves(np.block([[c, s], [-s, c]]))
        self.rows_inverse = halves(np.block([[c, -s], [s, c]]))
        scale = 1.0 / (2.0 * n * n)
        self.cols_inverse = halves(scale * np.block([[c, s], [-s, c]]))
        low = j < TILE // 2
        digit_a = np.where(low, j, j - TILE // 2)
        digit_b = np.where(low, np.where(j == 0, TILE // 2, TILE - j), TILE - 1 - (j - TILE // 2))
        ca, sa = phases(j[:, None] * digit_a[None, :], TILE)
        cb, sb = phases(j[:, None] * digit_b[None, :], TILE)
        blocks = []
        for mask in (low, ~low):
            blocks.append(np.concatenate([ca * mask, cb * mask, -sa * mask, -sb * mask], 1))
            blocks.append(np.concatenate([sa * mask, sb * mask, ca * mask, cb * mask], 1))
        self.special_forward = halves(np.concatenate(blocks, 0))
        freq = np.where(low, 0, devices) + self.tiles * digit_a
        ci, si = phases(freq[:, None] * j[None, :], n)
        first = np.concatenate([ci * low[:, None], ci * ~low[:, None]], 1)
        second = np.concatenate([-si * low[:, None], -si * ~low[:, None]], 1)
        second[0, :TILE] = 1.0 - 2.0 * (j % 2)
        second[0, TILE:] = 0.0
        self.special_inverse = halves(2.0 * scale * np.concatenate([first, second], 0))
        beta = np.arange(self.tiles)
        tc, ts = phases(beta[:, None] * j[None, :], n)
        self.col_twiddle = jnp.asarray(np.stack([tc, ts]), jnp.float32)
        self.row_twiddle = jnp.asarray(np.stack([tc.T, ts.T]), jnp.float32)
        self.low = low
        self.digit_a, self.digit_b = digit_a, digit_b

    def wave_of_lists(self, place):
        j = jnp.arange(TILE, dtype=jnp.int32)
        usual = place + self.tiles * j
        other = jnp.asarray(np.where(self.low, 0, self.devices) + self.tiles * self.digit_a, jnp.int32)
        other_b = (self.n - other) % self.n
        other_b = other_b.at[0].set(self.n // 2)
        a = jnp.where(place == 0, other, usual)
        b = jnp.where(place == 0, other_b, (self.n - usual) % self.n)
        return signed_wave(jnp.concatenate([a, b]), self.n).reshape(1, 2 * TILE)


def whole(shape):
    return pl.BlockSpec(shape, lambda *_: (0,) * len(shape))


def params():
    return pltpu.CompilerParams(vmem_limit_bytes=VMEM_LIMIT)


def remap_kernel(
    coded, group, last, half_ref, above_ref, here_ref, below_ref, edge_ref, slopes_ref, source_ref,
    row_ref, pixel_ref, fraction_ref, moves_ref, past_ref, out_ref, window, picker, picked, moved,
):
    tiles = slopes_ref.shape[2] // TILE
    span = 2 * GROUP
    count = PAIRS * tiles * GROUP
    here = group(pl.program_id(0), pl.program_id(1), half_ref)
    upper = lax.broadcasted_iota(jnp.int32, (GROUP, TILE), 0) < GROUP // 2

    def fill(after_ref, before_ref):
        for t in range(tiles):
            cols = slice(t * TILE, (t + 1) * TILE)
            for p in range(2):
                lanes = slice(p * TILE, (p + 1) * TILE)
                window[t * span : t * span + GROUP, lanes] = here_ref[p, :, cols]
                window[t * span + GROUP : (t + 1) * span, lanes] = jnp.where(
                    upper, after_ref[p, :, cols], before_ref[p, :, cols]
                )

    @pl.when((here > 0) & (here < last))
    def _():
        fill(below_ref, above_ref)

    @pl.when(here == 0)
    def _():
        fill(below_ref, edge_ref)

    @pl.when(here == last)
    def _():
        fill(edge_ref, above_ref)

    lane = lax.broadcasted_iota(jnp.int32, (GROUP, TILE), 1)
    down = lax.broadcasted_iota(jnp.int32, (GROUP, tiles), 0)
    per = TILE // span
    for k in range(PAIRS):
        source = source_ref[k]
        place = (source % per) * span + ((down + row_ref[k]) & (span - 1))
        block = source // per
        for t in range(tiles):
            here = slice((k * tiles + t) * GROUP, (k * tiles + t + 1) * GROUP)
            hit = jnp.where(place[:, t : t + 1] == lane, 1.0, 0.0).astype(jnp.bfloat16)
            blk = jnp.broadcast_to(block[:, t : t + 1], (GROUP, TILE))
            blk = blk.astype(jnp.float32).astype(jnp.bfloat16)
            for c in range(tiles * span // TILE):
                picker[here, c * TILE : (c + 1) * TILE] = jnp.where(
                    blk == jnp.bfloat16(c), hit, jnp.bfloat16(0)
                )
    picked[...] = jnp.dot(
        picker[...], window[...], preferred_element_type=jnp.float32
    ).astype(jnp.bfloat16)
    for p in range(2):
        moved[p * count : (p + 1) * count, :] = jnp.dot(
            picked[:, p * TILE : (p + 1) * TILE], moves_ref[...],
            preferred_element_type=jnp.float32,
        )
    for t in range(tiles):
        pulled = [None, None]
        for k in range(PAIRS):
            row0 = (k * tiles + t) * GROUP
            move = jnp.broadcast_to(pixel_ref[k][:, t : t + 1], (GROUP, TILE))
            blend = jnp.broadcast_to(fraction_ref[k][:, t : t + 1], (GROUP, TILE))
            rest = 1.0 - blend
            same = [move == step for step in STEPS[:-2]]
            for p in range(2):
                here = slice(p * count + row0, p * count + row0 + GROUP)
                part = [moved[here, i * TILE : (i + 1) * TILE] for i in range(len(STEPS))]
                near, far = part[-2], part[-1]
                for i in range(len(STEPS) - 2):
                    near = jnp.where(same[i], part[i], near)
                    far = jnp.where(same[i], part[i + 1], far)
                term = rest * near + blend * far
                pulled[p] = term if pulled[p] is None else pulled[p] + term
        cols = slice(t * TILE, (t + 1) * TILE)
        slopes = [slopes_ref[i, :, cols].astype(jnp.float32) for i in range(4)]
        across = -(pulled[0] * slopes[0] + pulled[1] * slopes[1])
        downward = -(pulled[0] * slopes[2] + pulled[1] * slopes[3])
        if coded:
            code = scale_code(largest_of(across, downward, 0))
            step = pl.program_id(0) * pl.num_programs(1) + pl.program_id(1)
            at = pl.ds(pl.multiple_of(step * GROUP, GROUP), GROUP)
            out_ref[at, cols] = pack(across, downward, code)
            put_row(out_ref, (slice(-8, None), cols), step, code)
        else:
            out_ref[0, :, cols] = across
            out_ref[1, :, cols] = downward


def remap_flow(
    half, part, parts, coded, past, residual, edge, slopes, source, row_shift, pixel_shift, fraction
):
    rows, cols = slopes.shape[1:]
    tiles = cols // TILE
    run = TILE // parts
    steps = run // GROUP
    half_groups = rows // 2 // GROUP

    def group(l, i, half_ref):
        return half_ref[0] * half_groups + l * (TILE // GROUP) + part * steps + i

    last = rows // GROUP - 1
    here = lambda l, i, half_ref: (0, group(l, i, half_ref), 0)
    before = lambda l, i, half_ref: (0, jnp.maximum(group(l, i, half_ref) - 1, 0), 0)
    after = lambda l, i, half_ref: (0, jnp.minimum(group(l, i, half_ref) + 1, last), 0)
    j = np.arange(TILE)
    moves = np.concatenate([j[:, None] == j[None, :] + step for step in STEPS], axis=1)
    small = pl.BlockSpec((PAIRS, GROUP, tiles), here)
    depth = 2 * GROUP * tiles
    count = PAIRS * GROUP * tiles
    runs = rows // 2 // TILE
    if coded:
        shape = (runs * run + scale_rows(runs * steps), cols)
        out = jax.ShapeDtypeStruct(shape, jnp.int32)
        out_spec = whole(shape)
    else:
        out = jax.ShapeDtypeStruct((2, runs * run, cols), jnp.float32)
        out_spec = pl.BlockSpec((2, GROUP, cols), lambda l, i, _: (0, l * steps + i, 0))
    return pl.pallas_call(
        partial(remap_kernel, coded, group, last),
        grid_spec=pltpu.PrefetchScalarGridSpec(
            num_scalar_prefetch=1,
            grid=(runs, steps),
            in_specs=[
                pl.BlockSpec((2, GROUP, cols), before),
                pl.BlockSpec((2, GROUP, cols), here),
                pl.BlockSpec((2, GROUP, cols), after),
                whole(edge.shape),
                pl.BlockSpec((4, GROUP, cols), here),
                small, small, small, small,
                whole(moves.shape),
                pl.BlockSpec(memory_space=pl.ANY),
            ],
            out_specs=out_spec,
            scratch_shapes=[
                pltpu.VMEM((depth, 2 * TILE), jnp.bfloat16),
                pltpu.VMEM((count, depth), jnp.bfloat16),
                pltpu.VMEM((count, 2 * TILE), jnp.bfloat16),
                pltpu.VMEM((2 * count, len(STEPS) * TILE), jnp.float32),
            ],
        ),
        out_shape=out,
        compiler_params=params(),
        cost_estimate=pl.CostEstimate(
            flops=1000 if coded or part == 0 else 2 * 10**10, bytes_accessed=0, transcendentals=0
        ),
        name="remap",
    )(half, residual, residual, residual, edge, slopes, source, row_shift, pixel_shift, fraction,
      jnp.asarray(moves, jnp.bfloat16), past)


def cols_forward_kernel(
    sign_ref, own_ref, got_ref, code_ref, next_ref, twiddle_ref, a_high, a_low, b_high, b_low, s_high, s_low,
    out_ref, xa_high, xa_low, xb_high, xb_low, hold,
):
    devices, rows, _ = xa_high.shape
    total_rows = rows * pl.num_programs(0)
    now = pl.program_id(0)
    sign = sign_ref[0]

    def block(r, carry):
        at = pl.ds(pl.multiple_of(r * GROUP, GROUP), GROUP)

        def put(beta, z):
            tc, ts = twiddle_ref[0, beta : beta + 1, :], twiddle_ref[1, beta : beta + 1, :]
            re, im = z[0] * tc + z[1] * ts, z[1] * tc - z[0] * ts
            if beta < devices:
                slot, high, low = beta, xa_high, xa_low
            else:
                slot, high, low = (2 * devices - beta) % devices, xb_high, xb_low
            for i, value in enumerate((re, im)):
                h, l = split(value)
                high[slot, at, i * TILE : (i + 1) * TILE] = h
                low[slot, at, i * TILE : (i + 1) * TILE] = l

        def both(t):
            cols = slice(t * TILE, (t + 1) * TILE)
            unit = unit_of(take_row(code_ref[:, cols], now * (rows // GROUP) + r))
            got = unpack(got_ref[at, cols], unit)
            return [(own_ref[p, at, cols], got[p]) for p in range(2)]

        def total(t):
            return tuple(a + b for a, b in both(t))

        def gap(t):
            return turn(tuple((a - b) * sign for a, b in both(t)), -t, 2 * devices)

        staged_dft(total, lambda k, z: put(2 * k, z), devices, -1, hold)
        staged_dft(gap, lambda k, z: put(2 * k + 1, z), devices, -1, hold)
        return carry

    lax.fori_loop(0, rows // GROUP, block, 0)
    flat = (devices - 1) * rows

    def put_out(slots, which, re, im):
        code = scale_code(largest_of(re, im, 1))
        at = pl.ds(pl.multiple_of(which * total_rows + now * rows, GROUP), rows)
        out_ref[slots, at, :] = pack(re, im, code)
        put_row(out_ref, (slots, slice(-8, None)), 2 * now + which, code)

    for i, (high, low, mh, ml) in enumerate(
        ((xa_high, xa_low, a_high, a_low), (xb_high, xb_low, b_high, b_low))
    ):
        left = tuple(x[1:].reshape(flat, 2 * TILE) for x in (high, low))
        value = product(left, (mh[...], ml[...])).reshape(devices - 1, rows, 2 * TILE)
        put_out(slice(1, devices), i, value[:, :, :TILE], value[:, :, TILE:])
    left = tuple(
        jnp.concatenate([xa[0], xb[0]], axis=1)
        for xa, xb in ((xa_high, xb_high), (xa_low, xb_low))
    )
    value = product(left, (s_high[...], s_low[...])).reshape(1, rows, 4 * TILE)
    for i in range(2):
        put_out(
            slice(0, 1), i, value[:, :, i * TILE : (i + 1) * TILE],
            value[:, :, (i + 2) * TILE : (i + 3) * TILE],
        )


def cols_forward(plan, sign, own, got, later):
    rows, cols = own.shape[1:]
    d = plan.devices
    step = 2 * GROUP
    data = pl.BlockSpec((2, step, cols), lambda i: (0, i, 0))
    codes = got.shape[0] - rows
    shape = (d, 2 * rows + scale_rows(2 * rows // step), TILE)
    square = whole((2 * TILE, 2 * TILE))
    wide = whole((4 * TILE, 4 * TILE))
    return pl.pallas_call(
        cols_forward_kernel,
        grid=(rows // step,),
        in_specs=[
            pl.BlockSpec(memory_space=pltpu.SMEM), data,
            pl.BlockSpec((step, cols), lambda i: (i, 0)),
            pl.BlockSpec((codes, cols), lambda i: (rows // codes, 0)),
            pl.BlockSpec(memory_space=pl.ANY), whole(plan.col_twiddle.shape),
            square, square, square, square, wide, wide,
        ],
        out_specs=whole(shape),
        out_shape=jax.ShapeDtypeStruct(shape, jnp.int32),
        scratch_shapes=[pltpu.VMEM((d, step, 2 * TILE), jnp.bfloat16)] * 4
        + [pltpu.VMEM((d, 2, GROUP, TILE), jnp.float32)],
        compiler_params=params(),
        cost_estimate=pl.CostEstimate(
            flops=2 * 10**10, bytes_accessed=0, transcendentals=0
        ),
        name="cols_forward",
    )(sign, own, got, got, later, plan.col_twiddle, *plan.list_a, *plan.list_b, *plan.special_forward)


def rows_forward_kernel(
    run, a0_ref, a1_ref, b0_ref, b1_ref, code_ref, twiddle_ref, past_ref, out_ref, hold, unit
):
    tiles, step, lanes = out_ref.shape
    half = lanes // 2
    twiddle = (twiddle_ref[0], twiddle_ref[1])
    unit[...] = unit_of(code_ref[...])
    block = pl.program_id(0) * step // (2 * GROUP)

    def load(s):
        g, l = s // 2, s % 2
        at = 2 * (l * (run // (2 * GROUP)) + block)
        a = unpack((a0_ref, a1_ref)[l][g], take_row(unit[g], at))
        b = unpack((b0_ref, b1_ref)[l][g], take_row(unit[g], at + 1))
        return tuple(jnp.concatenate(pair, axis=1) for pair in zip(a, b))

    def store(k, z):
        tc, ts = twiddle[0][:, k : k + 1], twiddle[1][:, k : k + 1]
        out_ref[k, :, :half] = z[0] * tc + z[1] * ts
        out_ref[k, :, half:] = z[1] * tc - z[0] * ts

    staged_dft(load, store, tiles, -1, hold)


def rows_forward(plan, part, parts, x, past):
    d = plan.devices
    tiles = 2 * d
    run = TILE // parts
    lanes = 4 * TILE
    step = 8
    codes = x.shape[1] - 4 * run
    data = lambda k: pl.BlockSpec((d, step, TILE), lambda i: (0, k * (run // step) + i, 0))
    return pl.pallas_call(
        partial(rows_forward_kernel, run),
        grid=(run // step,),
        in_specs=[data(k) for k in range(4)]
        + [
            pl.BlockSpec((d, codes, TILE), lambda i: (0, 4 * run // codes, 0)),
            pl.BlockSpec((2, step, tiles), lambda i: (0, part * (run // step) + i, 0)),
            pl.BlockSpec(memory_space=pl.ANY),
        ],
        out_specs=pl.BlockSpec((tiles, step, lanes), lambda i: (0, i, 0)),
        out_shape=jax.ShapeDtypeStruct((tiles, run, lanes), jnp.float32),
        scratch_shapes=[
            pltpu.VMEM((tiles, 2, step, lanes // 2), jnp.float32),
            pltpu.VMEM((d, codes, TILE), jnp.float32),
        ],
        compiler_params=params(),
        cost_estimate=pl.CostEstimate(
            flops=128 * x.size, bytes_accessed=12 * x.size, transcendentals=0
        ),
        name="rows_forward",
    )(x, x, x, x, x, plan.row_twiddle, past)


def weigh_kernel(n, parts, *refs):
    x_refs = refs[:parts]
    f_high, f_low, g_high, g_low, wave_ref, out_ref = refs[parts:]
    batch, _, lanes = out_ref.shape
    half = lanes // 2
    tiles = n // TILE
    col_wave = wave_ref[...]
    floored = 8.0 * math.pi / n
    col_part = col_wave * col_wave + floored * floored
    digit = lax.broadcasted_iota(jnp.int32, (TILE, half), 0)
    for b in range(batch):
        x = jnp.concatenate(
            [r[b, :, :half] for r in x_refs] + [r[b, :, half:] for r in x_refs], axis=0
        )
        z = product((f_high[...], f_low[...]), split(x))
        row_wave = signed_wave(pl.program_id(0) * batch + b + tiles * digit, n)
        weight = local_weight + 1.0 / (row_wave * row_wave + col_part)
        re, im = z[:TILE], z[TILE:]
        z = jnp.concatenate(
            [weight * (col_wave * im - row_wave * re), -weight * (col_wave * re + row_wave * im)],
            axis=0,
        )
        y = product((g_high[...], g_low[...]), split(z))
        out_ref[b, :, :half] = y[:TILE]
        out_ref[b, :, half:] = y[TILE:]


def weigh(plan, wave, xs):
    tiles, rows, lanes = xs[0].shape
    parts = len(xs)
    batch = 4
    square = whole((2 * TILE, 2 * TILE))
    return pl.pallas_call(
        partial(weigh_kernel, plan.n, parts),
        grid=(tiles // batch,),
        in_specs=[pl.BlockSpec((batch, rows, lanes), lambda i: (i, 0, 0))] * parts
        + [square] * 4 + [whole(wave.shape)],
        out_specs=pl.BlockSpec((batch, parts * rows, lanes), lambda i: (i, 0, 0)),
        out_shape=jax.ShapeDtypeStruct((tiles, parts * rows, lanes), jnp.float32),
        compiler_params=params(),
        cost_estimate=pl.CostEstimate(
            flops=4096 * parts * xs[0].size, bytes_accessed=8 * parts * xs[0].size, transcendentals=0
        ),
        name="weigh",
    )(*xs, *plan.rows_forward, *plan.rows_inverse, wave)


def rows_inverse_kernel(run, x_ref, twiddle_ref, special_ref, past_ref, out_ref, hold, folded):
    tiles, step, lanes = x_ref.shape
    now = pl.program_id(0)
    half = lanes // 2
    twiddle = (twiddle_ref[0], twiddle_ref[1])
    special = special_ref[...] > 0.5

    def load(k):
        tc, ts = twiddle[0][:, k : k + 1], twiddle[1][:, k : k + 1]
        re, im = x_ref[k, :, :half], x_ref[k, :, half:]
        return re * tc - im * ts, im * tc + re * ts

    def store(s, z):
        re_a, re_b = z[0][:, :TILE], z[0][:, TILE:]
        im_a, im_b = z[1][:, :TILE], z[1][:, TILE:]
        folded[s, 0] = jnp.where(special, re_a, re_a + re_b)
        folded[s, 1] = jnp.where(special, re_b, im_a - im_b)

    staged_dft(load, store, tiles, 1, hold)
    for g in range(tiles // 2):
        re, im = folded[2 * g : 2 * g + 2, 0], folded[2 * g : 2 * g + 2, 1]
        code = scale_code(jnp.max(largest_of(re, im, 1), axis=0))
        for l in range(2):
            at = pl.ds(pl.multiple_of(l * run + now * step, 8), step)
            out_ref[g, at, :] = pack(re[l], im[l], code)
        put_row(out_ref, (g, slice(-8, None)), now, code)


def rows_inverse(plan, part, parts, special, x, past):
    tiles, rows, lanes = x.shape
    step = 8
    run = rows // parts // step
    shape = (tiles // 2, 2 * run * step + scale_rows(run), TILE)
    return pl.pallas_call(
        partial(rows_inverse_kernel, run * step),
        grid=(run,),
        in_specs=[
            pl.BlockSpec((tiles, step, lanes), lambda i: (0, part * run + i, 0)),
            pl.BlockSpec((2, step, tiles), lambda i: (0, part * run + i, 0)),
            whole(special.shape),
            pl.BlockSpec(memory_space=pl.ANY),
        ],
        out_specs=whole(shape),
        out_shape=jax.ShapeDtypeStruct(shape, jnp.int32),
        scratch_shapes=[
            pltpu.VMEM((tiles, 2, step, lanes // 2), jnp.float32),
            pltpu.VMEM((tiles, 2, step, TILE), jnp.float32),
        ],
        compiler_params=params(),
        cost_estimate=pl.CostEstimate(
            flops=64 * x.size // parts, bytes_accessed=6 * x.size // parts, transcendentals=0
        ),
        name="rows_inverse",
    )(x, plan.row_twiddle, special, past)


def cols_inverse_kernel(
    col_ref, sign_ref, x_ref, code_ref, twiddle_ref, g_high, g_low, s_high, s_low, *rest,
):
    keep_ref, send_ref, spectrum, hold = rest[-4:]
    devices, rows, _ = x_ref.shape
    flat = (devices - 1) * rows
    per = pl.num_programs(1)
    for j in range(rows // 8):
        at = slice(8 * j, 8 * j + 8)
        unit = unit_of(take_row(code_ref[...], pl.program_id(1) * (rows // 8) + j))
        re, im = unpack(x_ref[:, at, :], unit)
        spectrum[:, at, :TILE] = re
        spectrum[:, at, TILE:] = im
    value = product(split(spectrum[1:].reshape(flat, 2 * TILE)), (g_high[...], g_low[...]))
    first = product(split(spectrum[0]), (s_high[...], s_low[...]))
    spectrum[1:] = value.reshape(devices - 1, rows, 2 * TILE)
    spectrum[0] = first
    sign = sign_ref[0]
    step = pl.program_id(0) * per + pl.program_id(1)

    def block(r, carry):
        at = pl.ds(pl.multiple_of(r * GROUP, GROUP), GROUP)

        def point(k):
            tc, ts = twiddle_ref[0, k : k + 1, :], twiddle_ref[1, k : k + 1, :]
            if k % 2:
                tc, ts = tc * sign, ts * sign
            re, im = spectrum[k, at, :TILE], spectrum[k, at, TILE:]
            return re * tc - im * ts, im * tc + re * ts

        def load(k):
            if k == 0:
                p, q = spectrum[0, at, :TILE], spectrum[0, at, TILE:]
                return p + q, p - q
            (a, b), (c, d) = point(k), point(devices - k)
            odd = turn((a - c, b + d), k, 2 * devices)
            return a + c - odd[1], b - d + odd[0]

        def store(n, z):
            if 2 * n < devices:
                for i in range(2):
                    keep_ref[at, (2 * n + i) * TILE : (2 * n + i + 1) * TILE] = z[i]
                return
            cols = slice((n - devices // 2) * TILE, (n - devices // 2 + 1) * TILE)
            code = scale_code(largest_of(z[0], z[1], 0))
            down = pl.ds(pl.multiple_of(step * rows + r * GROUP, GROUP), GROUP)
            send_ref[down, cols] = pack(z[0], z[1], code)
            put_row(send_ref, (slice(-8, None), cols), step * (rows // GROUP) + r, code)

        staged_dft(load, store, devices, 1, hold)
        return carry

    lax.fori_loop(0, rows // GROUP, block, 0)


def place_block(part, parts, half_rows, step):
    run = TILE // parts // step
    return lambda l, i, half_ref: (
        half_ref[0] * (half_rows // step) + l * (TILE // step) + part * run + i, 0
    )


def cols_inverse(plan, part, parts, half, sign, x, shape, image):
    d = plan.devices
    step = min(2 * GROUP, TILE // parts)
    runs = shape[0] // 2 // TILE
    rows = runs * TILE // parts
    codes = x.shape[1] - rows
    sent = (rows + scale_rows(rows // GROUP), shape[1] // 2)
    per = TILE // parts // step
    cols = shape[1]
    square = whole((2 * TILE, 2 * TILE))
    smem = pl.BlockSpec(memory_space=pltpu.SMEM)
    extra = [] if image is None else [image]
    return pl.pallas_call(
        cols_inverse_kernel,
        grid_spec=pltpu.PrefetchScalarGridSpec(
            num_scalar_prefetch=1,
            grid=(runs, per),
            in_specs=[
                smem, pl.BlockSpec((d, step, TILE), lambda l, i, _: (0, l * per + i, 0)),
                pl.BlockSpec((d, codes, TILE), lambda l, i, _: (0, rows // codes, 0)),
                whole(plan.col_twiddle.shape), square, square, square, square,
            ] + [pl.BlockSpec(memory_space=pl.ANY)] * len(extra),
            out_specs=[
                pl.BlockSpec((step, cols), place_block(part, parts, shape[0] // 2, step)),
                whole(sent),
            ],
            scratch_shapes=[
                pltpu.VMEM((d, step, 2 * TILE), jnp.float32),
                pltpu.VMEM((d, 2, GROUP, TILE), jnp.float32),
            ],
        ),
        out_shape=[
            jax.ShapeDtypeStruct(shape, jnp.float32),
            jax.ShapeDtypeStruct(sent, jnp.int32),
        ],
        input_output_aliases={9: 0} if extra else {},
        compiler_params=params(),
        cost_estimate=pl.CostEstimate(
            flops=2048 * x.size, bytes_accessed=8 * x.size, transcendentals=0
        ),
        name="cols_inverse",
    )(half, sign, x, x, plan.col_twiddle, *plan.cols_inverse, *plan.special_inverse, *extra)


def place_kernel(half_ref, got_ref, code_ref, image_ref, out_ref):
    rows, cols = got_ref.shape
    step = pl.program_id(0) * pl.num_programs(1) + pl.program_id(1)
    for r in range(rows // GROUP):
        at = slice(r * GROUP, (r + 1) * GROUP)
        for n in range(cols // TILE):
            lanes = slice(n * TILE, (n + 1) * TILE)
            unit = unit_of(take_row(code_ref[:, lanes], step * (rows // GROUP) + r))
            for i, value in enumerate(unpack(got_ref[at, lanes], unit)):
                out_ref[at, (2 * n + i) * TILE : (2 * n + i + 1) * TILE] = value


def place_rows(part, parts, half, got, image):
    cols = image.shape[1]
    step = min(2 * GROUP, TILE // parts)
    runs = image.shape[0] // 2 // TILE
    rows = runs * TILE // parts
    codes = got.shape[0] - rows
    per = TILE // parts // step
    return pl.pallas_call(
        place_kernel,
        grid_spec=pltpu.PrefetchScalarGridSpec(
            num_scalar_prefetch=1,
            grid=(runs, per),
            in_specs=[
                pl.BlockSpec((step, cols // 2), lambda l, i, _: (l * per + i, 0)),
                pl.BlockSpec((codes, cols // 2), lambda l, i, _: (rows // codes, 0)),
                pl.BlockSpec(memory_space=pl.ANY),
            ],
            out_specs=pl.BlockSpec(
                (step, cols), place_block(part, parts, image.shape[0] // 2, step)
            ),
        ),
        out_shape=jax.ShapeDtypeStruct(image.shape, jnp.float32),
        input_output_aliases={3: 0},
        compiler_params=params(),
        cost_estimate=pl.CostEstimate(flops=0, bytes_accessed=8 * got.size, transcendentals=0),
        name="place_rows",
    )(half, got, got, image)


def paired(residual, field_slopes, source_tile, row_shift, pixel_shift, fraction):
    rows_dev, cols_dev = residual.shape[1:]
    devices = lax.axis_size("rows") * lax.axis_size("cols")
    plan = Plan(devices)
    parts = SLICES
    col = lax.axis_index("cols").astype(jnp.int32)
    place = lax.axis_index("rows").astype(jnp.int32) * 2 + col
    mine, other = col.reshape(1), (1 - col).reshape(1)
    sign = (1 - 2 * col).astype(jnp.float32).reshape(1)
    swap = [(0, 1), (1, 0)]
    both = ("rows", "cols")
    before = lax.ppermute(
        residual[:, rows_dev - HALO :], "rows", [(k, k + 1) for k in range(devices // 2 - 1)]
    )
    after = lax.ppermute(
        residual[:, :HALO], "rows", [(k + 1, k) for k in range(devices // 2 - 1)]
    )
    edge = jnp.concatenate([after, before], axis=1)
    args = (residual, edge, field_slopes, source_tile, row_shift, pixel_shift, fraction)
    lane = jnp.arange(TILE, dtype=jnp.int32).reshape(1, TILE)
    special = jnp.where((lane == 0) & (place == 0), 1.0, 0.0)
    wave = plan.wave_of_lists(place)
    spectra = []
    spectra, lists, aways, gots = [], [], [], []

    def send(m, past):
        aways.append(remap_flow(other, m, parts, True, past, *args))
        gots.append(lax.ppermute(aways[m], "cols", swap))

    send(0, special)
    if parts > 1:
        send(1, aways[0])
    for m in range(parts):
        past = gots[m] if m or parts == 1 else aways[1]
        own = remap_flow(mine, m, parts, False, past, *args)
        past = spectra[m - 2] if m > 1 else special
        lists.append(cols_forward(plan, sign, own, gots[m], past))
        if m + 2 < parts:
            send(m + 2, lists[m])
        swapped = lax.all_to_all(lists[m], both, split_axis=0, concat_axis=0, tiled=True)
        past = spectra[m - 1] if m else special
        spectra.append(rows_forward(plan, m, parts, swapped, past))
    mixed = weigh(plan, wave, spectra)
    image = None
    sent = []
    past = [special, special]
    for m in range(parts):
        folded = rows_inverse(plan, m, parts, special, mixed, past[m])
        folded = lax.all_to_all(folded, both, split_axis=0, concat_axis=0, tiled=True)
        if m > 1:
            image = place_rows(m - 2, parts, other, sent[m - 2], image)
        image, away = cols_inverse(
            plan, m, parts, mine, sign, folded, (rows_dev, cols_dev), image
        )
        past.append(away)
        sent.append(lax.ppermute(away, "cols", swap))
    for m in range(max(parts - 2, 0), parts):
        image = place_rows(m, parts, other, sent[m], image)
    return image


def general(residual, field_slopes, source_tile, row_shift, pixel_shift, fraction):
    padded = with_halo(residual, (("rows", 1),), HALO)
    pulled = remap_tiles(padded, source_tile, row_shift, pixel_shift, fraction)
    slopes = field_slopes.astype(jnp.float32)
    flow_across = -(pulled[0] * slopes[0] + pulled[1] * slopes[1])
    downward_flow = -(pulled[0] * slopes[2] + pulled[1] * slopes[3])
    rows_dev = residual.shape[1]
    cols_dev = residual.shape[2]
    rows_count = lax.axis_size("rows")
    cols_count = lax.axis_size("cols")
    part_rows = rows_dev // cols_count
    n = rows_dev * rows_count
    spread = rows_count // cols_count
    col_index = lax.axis_index("cols")
    row_place = lax.axis_index("rows")
    compact_forward_transform = fourier_matrix(rows_count, -1)
    large_forward = fourier_matrix(rows_dev, -1)
    compact_inverse_transform = fourier_matrix(rows_count, 1)
    large_inverse = fourier_matrix(rows_dev, 1)
    wave_index = jnp.arange(rows_count, dtype=jnp.int32)
    pixel_index = jnp.arange(rows_dev, dtype=jnp.int32)
    band = col_index * part_rows + jnp.arange(part_rows, dtype=jnp.int32)
    stacked_planes = jnp.stack([flow_across, downward_flow]).reshape(2, rows_dev, 1, cols_dev)
    stacked_planes = across_columns(stacked_planes).reshape(2, part_rows, rows_count, rows_dev)
    power_spectra = contract_indices("pibc,pbqk->qikc", stacked_planes, compact_forward_transform)[
        :, None
    ]
    cosine, sine_part = phase_pair(wave_index[:, None] * pixel_index[None, :], n, -1)
    power_spectra = rotate(power_spectra, cosine, sine_part)
    power_spectra = contract_indices("pfikc,pcql->qfikl", power_spectra, large_forward)
    fields = power_spectra.shape[1]
    back_cos, back_sin = phase_pair(wave_index[:, None] * pixel_index[None, :], n, 1)
    power_spectra = across_rows(power_spectra)
    power_spectra = power_spectra.reshape(2, fields, rows_count, part_rows, rows_dev)
    power_spectra = contract_indices("pfrik,prqm->qfmik", power_spectra, compact_forward_transform)
    band_cos, band_sin = phase_pair(wave_index[:, None] * band[None, :], n, -1)
    power_spectra = rotate(power_spectra, band_cos[:, :, None], band_sin[:, :, None])
    power_spectra = across_columns(
        power_spectra.reshape(2 * fields, rows_count, part_rows, rows_dev)
    )
    power_spectra = power_spectra.reshape(2, fields, spread, rows_dev, rows_dev)
    power_spectra = contract_indices("pfmsk,psql->qfmlk", power_spectra, large_forward)
    row_freq = (
        rows_count * pixel_index[None, :]
        + (col_index * spread + jnp.arange(spread, dtype=jnp.int32))[:, None]
    )
    row_wave = signed_wave(row_freq, n)[:, :, None]
    col_wave = signed_wave(rows_count * pixel_index + row_place, n)
    mixed = weigh_spectra(power_spectra, row_wave, col_wave, n)
    mixed = contract_indices("pmlk,plqs->qsmk", mixed, large_inverse)
    mixed = across_columns(mixed)
    band_cos, band_sin = phase_pair(band[:, None] * wave_index[None, :], n, 1)
    mixed = rotate(mixed, band_cos[:, :, None], band_sin[:, :, None])
    mixed = contract_indices("pimk,pmqr->qirk", mixed, compact_inverse_transform)
    mixed = across_rows(mixed.reshape(2, 1, part_rows, rows_count, rows_dev))
    mixed = mixed.reshape(2, rows_count, part_rows, rows_dev)
    mixed = contract_indices("pnik,pkqa->qina", mixed, large_inverse)
    mixed = rotate(mixed, back_cos, back_sin)
    image = jnp.einsum(
        "pina,pnb->iba",
        mixed,
        compact_inverse_transform[:, :, 0, :],
        precision=highest,
        preferred_element_type=jnp.float32,
    )
    image = image.reshape(part_rows, cols_count, cols_dev) * (1.0 / (n * n))
    return lax.all_to_all(image, "cols", split_axis=1, concat_axis=0, tiled=True).reshape(
        rows_dev, cols_dev
    )


def per_device(*arrays):
    rows_dev, cols_dev = arrays[0].shape[1:]
    rows_count, cols_count = lax.axis_size("rows"), lax.axis_size("cols")
    devices = rows_count * cols_count
    if cols_count == 2 and rows_dev * rows_count == cols_dev * cols_count == 2 * TILE * devices:
        return paired(*arrays)
    return general(*arrays)


def solution(mesh):
    return jax.shard_map(
        per_device,
        mesh=mesh,
        in_specs=(
            P(None, "rows", "cols"),
            P(None, "rows", "cols"),
            P(None, "rows", "cols"),
            P(None, "rows", "cols"),
            P(None, "rows", "cols"),
            P(None, "rows", "cols"),
        ),
        out_specs=P("rows", "cols"),
        check_vma=False,
    )
```

```python
import math
from functools import partial

import jax
import jax.numpy as jnp
import ml_dtypes
import numpy as np
from jax import lax
from jax.experimental import pallas as pl
from jax.experimental.pallas import tpu as pltpu
from jax.sharding import PartitionSpec as P

TILE = 128
PAIRS = 2
HALO = 8
SHIFT = 2


local_weight = 0.5
highest = lax.Precision.HIGHEST


def with_halo(x, sides, width):
    for axis, dim in sides:
        peers, length = (lax.axis_size(axis), x.shape[dim])
        up = [(i, (i + 1) % peers) for i in range(peers - 1)]
        down = [(j, i) for i, j in up]
        last = lax.slice_in_dim(x, length - width, length, axis=dim)
        first = lax.slice_in_dim(x, 0, width, axis=dim)
        before = lax.ppermute(last, axis, up)
        after = lax.ppermute(first, axis, down)
        x = jnp.concatenate([before, x, after], axis=dim)
    return x


def phase_pair(phases, length, direction):
    angles = phases.astype(jnp.float32) * (direction * 2.0 * math.pi / length)
    return (jnp.cos(angles), jnp.sin(angles))


def fourier_matrix(length, direction):
    counter = jnp.arange(length, dtype=jnp.int32)
    cosine, sine_part = phase_pair(counter[:, None] * counter[None, :] % length, length, direction)
    return jnp.stack([jnp.stack([cosine, sine_part], 1), jnp.stack([-sine_part, cosine], 1)], 0)


def rotate(values, cosine, sine_part):
    real_part = values[0] * cosine - values[1] * sine_part
    imag_part = values[0] * sine_part + values[1] * cosine
    return jnp.stack([real_part, imag_part])


def contract_indices(formula, values, matrix):
    return jnp.einsum(
        formula, values, matrix, precision=highest, preferred_element_type=jnp.float32
    )


def signed_wave(counter, n):
    middle = n // 2
    shifted = jnp.where(counter > middle, counter - n, counter)
    shifted = jnp.where(counter == middle, 0, shifted)
    return shifted.astype(jnp.float32) * (2.0 * math.pi / n)


def across_columns(values):
    return lax.all_to_all(values, "cols", split_axis=1, concat_axis=2, tiled=True)


def across_rows(values):
    return lax.all_to_all(values, "rows", split_axis=3, concat_axis=1, tiled=True)


def remap_tiles(padded, source_tile, row_shift, pixel_shift, fraction):
    rows_dev = padded.shape[1] - 2 * HALO
    tiles_dev = padded.shape[2] // TILE
    tile_rows = padded.reshape(2, (rows_dev + 2 * HALO) * tiles_dev, TILE)
    row_index = jnp.arange(rows_dev, dtype=jnp.int32)[None, :, None]
    flat_index = (row_index + HALO + row_shift) * tiles_dev + source_tile
    picked = jnp.take(tile_rows, flat_index.reshape(-1), axis=1)
    picked = picked.reshape(2, PAIRS, rows_dev, tiles_dev, TILE)
    widened = jnp.pad(picked, ((0, 0), (0, 0), (0, 0), (0, 0), (SHIFT + 1, SHIFT + 1)))
    pulled = jnp.zeros((2, rows_dev, tiles_dev, TILE), jnp.float32)
    for offset in range(-SHIFT, SHIFT + 2):
        weights = jnp.where(pixel_shift == offset, 1.0 - fraction, 0.0)
        weights = weights + jnp.where(pixel_shift + 1 == offset, fraction, 0.0)
        start_at = SHIFT + 1 + offset
        window = widened[..., start_at : start_at + TILE].astype(jnp.float32)
        pulled = pulled + jnp.sum(window * weights[None, :, :, :, None], axis=1)
    return pulled.reshape(2, rows_dev, tiles_dev * TILE)


def weigh_spectra(power_spectra, row_wave, col_wave, n):
    floored_wavenumber = 8.0 * math.pi / n
    weight = local_weight + 1.0 / (
        row_wave * row_wave + col_wave * col_wave + floored_wavenumber * floored_wavenumber
    )
    real_part = weight * (col_wave * power_spectra[1, 0] - row_wave * power_spectra[0, 0])
    imag_part = -weight * (col_wave * power_spectra[0, 0] + row_wave * power_spectra[1, 0])
    return jnp.stack([real_part, imag_part])


GROUP = 16
SLICES = 4
STEPS = tuple(range(-SHIFT, SHIFT + 2))
MATRIX_STEPS = (STEPS[0], STEPS[-1])
VMEM_LIMIT = 48 * 2**20


def turn(x, numerator, denominator):
    numerator %= denominator
    re, im = x
    if numerator == 0:
        return x
    if 4 * numerator == denominator:
        return (-im, re)
    if 2 * numerator == denominator:
        return (-re, -im)
    if 4 * numerator == 3 * denominator:
        return (im, -re)
    if 8 * numerator % denominator == 0:
        half = math.sqrt(0.5)
        a, b = half * re, half * im
        return {1: (a - b, a + b), 3: (-a - b, a - b), 5: (b - a, -a - b), 7: (a + b, b - a)}[
            8 * numerator // denominator
        ]
    angle = 2.0 * math.pi * numerator / denominator
    c, s = math.cos(angle), math.sin(angle)
    return (re * c - im * s, re * s + im * c)


def dft(xs, sign):
    n = len(xs)
    if n == 1:
        return xs
    even, odd = dft(xs[0::2], sign), dft(xs[1::2], sign)
    odd = [turn(x, sign * k, n) for k, x in enumerate(odd)]
    first = [(e[0] + o[0], e[1] + o[1]) for e, o in zip(even, odd)]
    second = [(e[0] - o[0], e[1] - o[1]) for e, o in zip(even, odd)]
    return first + second


def staged_dft(load, store, n, sign, hold):
    outer = 8 if n >= 32 else 2
    inner = n // outer
    for a in range(outer):
        ys = dft([load(a + outer * b) for b in range(inner)], sign)
        for k, y in enumerate(ys):
            re, im = turn(y, sign * a * k, n)
            hold[k * outer + a, 0] = re
            hold[k * outer + a, 1] = im
    for k in range(inner):
        zs = dft([(hold[k * outer + a, 0], hold[k * outer + a, 1]) for a in range(outer)], sign)
        for b, z in enumerate(zs):
            store(k + inner * b, z)


def split(x):
    high = x.astype(jnp.bfloat16)
    return high, (x - high.astype(jnp.float32)).astype(jnp.bfloat16)


def product(left, right):
    dot = lambda a, b: jnp.dot(a, b, preferred_element_type=jnp.float32)
    return dot(left[0], right[0]) + (dot(left[1], right[0]) + dot(left[0], right[1]))


LOG_STEP = math.log(2.0) / 1024.0
TOP = 32767.0


def scale_code(largest):
    return jnp.floor(jnp.log(jnp.maximum(largest, 1e-33)) / LOG_STEP).astype(jnp.int32) + 2


def unit_of(code):
    return jnp.exp(code.astype(jnp.float32) * LOG_STEP) * (1.0 / TOP)


def pack(first, second, code):
    inverse = 1.0 / unit_of(code)
    a, b = (
        jnp.clip(jnp.floor(x * inverse + 0.5), -TOP, TOP).astype(jnp.int32)
        for x in (first, second)
    )
    return (a << 16) | (b & 0xFFFF)


def unpack(packed, unit):
    first, second = packed >> 16, (packed << 16) >> 16
    return first.astype(jnp.float32) * unit, second.astype(jnp.float32) * unit


def largest_of(first, second, axis):
    return jnp.max(jnp.maximum(jnp.abs(first), jnp.abs(second)), axis=axis, keepdims=True)


def put_row(ref, where, row, value):
    old = ref[where]
    lane_row = lax.broadcasted_iota(jnp.int32, old.shape, old.ndim - 2)
    ref[where] = jnp.where(lane_row == row, value, jnp.where(row == 0, 0, old))


def take_row(tile, row):
    rows = lax.broadcasted_iota(jnp.int32, tile.shape, tile.ndim - 2)
    return jnp.sum(jnp.where(rows == row, tile, 0), axis=tile.ndim - 2, keepdims=True)


def scale_rows(count):
    return -(-count // 8) * 8


def halves(matrix):
    high = np.asarray(matrix, np.float32).astype(ml_dtypes.bfloat16)
    low = (np.asarray(matrix, np.float32) - high.astype(np.float32)).astype(ml_dtypes.bfloat16)
    return jnp.asarray(high), jnp.asarray(low)


def phases(product_of_indices, length):
    angle = 2.0 * np.pi * (np.asarray(product_of_indices) % length) / length
    return np.cos(angle), np.sin(angle)


class Plan:
    def __init__(self, devices):
        self.devices = devices
        self.tiles = 2 * devices
        n = self.n = TILE * self.tiles
        j = np.arange(TILE)
        c, s = phases(j[:, None] * j[None, :], TILE)
        back = TILE - 1 - j
        self.list_a = halves(np.block([[c, -s], [s, c]]))
        self.list_b = halves(np.block([[c[:, back], -s[:, back]], [s[:, back], c[:, back]]]))
        self.rows_forward = halves(np.block([[c, s], [-s, c]]))
        self.rows_inverse = halves(np.block([[c, -s], [s, c]]))
        scale = 1.0 / (2.0 * n * n)
        self.cols_inverse = halves(scale * np.block([[c, s], [-s, c]]))
        low = j < TILE // 2
        digit_a = np.where(low, j, j - TILE // 2)
        digit_b = np.where(low, np.where(j == 0, TILE // 2, TILE - j), TILE - 1 - (j - TILE // 2))
        ca, sa = phases(j[:, None] * digit_a[None, :], TILE)
        cb, sb = phases(j[:, None] * digit_b[None, :], TILE)
        blocks = []
        for mask in (low, ~low):
            blocks.append(np.concatenate([ca * mask, cb * mask, -sa * mask, -sb * mask], 1))
            blocks.append(np.concatenate([sa * mask, sb * mask, ca * mask, cb * mask], 1))
        self.special_forward = halves(np.concatenate(blocks, 0))
        freq = np.where(low, 0, devices) + self.tiles * digit_a
        ci, si = phases(freq[:, None] * j[None, :], n)
        first = np.concatenate([ci * low[:, None], ci * ~low[:, None]], 1)
        second = np.concatenate([-si * low[:, None], -si * ~low[:, None]], 1)
        second[0, :TILE] = 1.0 - 2.0 * (j % 2)
        second[0, TILE:] = 0.0
        self.special_inverse = halves(2.0 * scale * np.concatenate([first, second], 0))
        beta = np.arange(self.tiles)
        tc, ts = phases(beta[:, None] * j[None, :], n)
        self.col_twiddle = jnp.asarray(np.stack([tc, ts]), jnp.float32)
        self.row_twiddle = jnp.asarray(np.stack([tc.T, ts.T]), jnp.float32)
        self.low = low
        self.digit_a, self.digit_b = digit_a, digit_b

    def wave_of_lists(self, place):
        j = jnp.arange(TILE, dtype=jnp.int32)
        usual = place + self.tiles * j
        other = jnp.asarray(np.where(self.low, 0, self.devices) + self.tiles * self.digit_a, jnp.int32)
        other_b = (self.n - other) % self.n
        other_b = other_b.at[0].set(self.n // 2)
        a = jnp.where(place == 0, other, usual)
        b = jnp.where(place == 0, other_b, (self.n - usual) % self.n)
        return signed_wave(jnp.concatenate([a, b]), self.n).reshape(1, 2 * TILE)


def whole(shape):
    return pl.BlockSpec(shape, lambda *_: (0,) * len(shape))


def params():
    return pltpu.CompilerParams(vmem_limit_bytes=VMEM_LIMIT)


def remap_kernel(
    coded, group, last, half_ref, above_ref, here_ref, below_ref, edge_ref, slopes_ref, source_ref,
    row_ref, pixel_ref, fraction_ref, moves_ref, past_ref, out_ref, window, picker, picked, moved,
):
    tiles = slopes_ref.shape[2] // TILE
    span = 2 * GROUP
    count = PAIRS * tiles * GROUP
    here = group(pl.program_id(0), pl.program_id(1), half_ref)
    upper = lax.broadcasted_iota(jnp.int32, (GROUP, TILE), 0) < GROUP // 2

    def fill(after_ref, before_ref):
        for t in range(tiles):
            cols = slice(t * TILE, (t + 1) * TILE)
            for p in range(2):
                lanes = slice(p * TILE, (p + 1) * TILE)
                window[t * span : t * span + GROUP, lanes] = here_ref[p, :, cols]
                window[t * span + GROUP : (t + 1) * span, lanes] = jnp.where(
                    upper, after_ref[p, :, cols], before_ref[p, :, cols]
                )

    @pl.when((here > 0) & (here < last))
    def _():
        fill(below_ref, above_ref)

    @pl.when(here == 0)
    def _():
        fill(below_ref, edge_ref)

    @pl.when(here == last)
    def _():
        fill(edge_ref, above_ref)

    lane = lax.broadcasted_iota(jnp.int32, (GROUP, TILE), 1)
    down = lax.broadcasted_iota(jnp.int32, (GROUP, tiles), 0)
    per = TILE // span
    for k in range(PAIRS):
        source = source_ref[k]
        place = (source % per) * span + ((down + row_ref[k]) & (span - 1))
        block = source // per
        for t in range(tiles):
            here = slice((k * tiles + t) * GROUP, (k * tiles + t + 1) * GROUP)
            hit = jnp.where(place[:, t : t + 1] == lane, 1.0, 0.0).astype(jnp.bfloat16)
            blk = jnp.broadcast_to(block[:, t : t + 1], (GROUP, TILE))
            blk = blk.astype(jnp.float32).astype(jnp.bfloat16)
            for c in range(tiles * span // TILE):
                picker[here, c * TILE : (c + 1) * TILE] = jnp.where(
                    blk == jnp.bfloat16(c), hit, jnp.bfloat16(0)
                )
    picked[...] = jnp.dot(picker[...], window[...], preferred_element_type=jnp.float32)
    for p in range(2):
        moved[p * count : (p + 1) * count, :] = jnp.dot(
            picked[:, p * TILE : (p + 1) * TILE].astype(jnp.bfloat16), moves_ref[...],
            preferred_element_type=jnp.float32,
        )
    for t in range(tiles):
        pulled = [None, None]
        for k in range(PAIRS):
            row0 = (k * tiles + t) * GROUP
            move = jnp.broadcast_to(pixel_ref[k][:, t : t + 1], (GROUP, TILE))
            blend = jnp.broadcast_to(fraction_ref[k][:, t : t + 1], (GROUP, TILE))
            rest = 1.0 - blend
            same = [move == step for step in STEPS[:-2]]
            for p in range(2):
                here = slice(p * count + row0, p * count + row0 + GROUP)
                tile = picked[row0 : row0 + GROUP, p * TILE : (p + 1) * TILE]
                part = []
                for step in STEPS:
                    if step == 0:
                        part.append(tile)
                    elif step in MATRIX_STEPS:
                        i = MATRIX_STEPS.index(step)
                        part.append(moved[here, i * TILE : (i + 1) * TILE])
                    else:
                        inside = (lane + step >= 0) & (lane + step < TILE)
                        part.append(jnp.where(inside, pltpu.roll(tile, -step % TILE, 1), 0.0))
                near, far = part[-2], part[-1]
                for i in range(len(STEPS) - 2):
                    near = jnp.where(same[i], part[i], near)
                    far = jnp.where(same[i], part[i + 1], far)
                term = rest * near + blend * far
                pulled[p] = term if pulled[p] is None else pulled[p] + term
        cols = slice(t * TILE, (t + 1) * TILE)
        slopes = [slopes_ref[i, :, cols].astype(jnp.float32) for i in range(4)]
        across = -(pulled[0] * slopes[0] + pulled[1] * slopes[1])
        downward = -(pulled[0] * slopes[2] + pulled[1] * slopes[3])
        if coded:
            code = scale_code(largest_of(across, downward, 0))
            step = pl.program_id(0) * pl.num_programs(1) + pl.program_id(1)
            at = pl.ds(pl.multiple_of(step * GROUP, GROUP), GROUP)
            out_ref[at, cols] = pack(across, downward, code)
            put_row(out_ref, (slice(-8, None), cols), step, code)
        else:
            out_ref[0, :, cols] = across
            out_ref[1, :, cols] = downward


def remap_flow(
    half, part, parts, coded, past, residual, edge, slopes, source, row_shift, pixel_shift, fraction
):
    rows, cols = slopes.shape[1:]
    tiles = cols // TILE
    run = TILE // parts
    steps = run // GROUP
    half_groups = rows // 2 // GROUP

    def group(l, i, half_ref):
        return half_ref[0] * half_groups + l * (TILE // GROUP) + part * steps + i

    last = rows // GROUP - 1
    here = lambda l, i, half_ref: (0, group(l, i, half_ref), 0)
    before = lambda l, i, half_ref: (0, jnp.maximum(group(l, i, half_ref) - 1, 0), 0)
    after = lambda l, i, half_ref: (0, jnp.minimum(group(l, i, half_ref) + 1, last), 0)
    j = np.arange(TILE)
    moves = np.concatenate([j[:, None] == j[None, :] + step for step in MATRIX_STEPS], axis=1)
    small = pl.BlockSpec((PAIRS, GROUP, tiles), here)
    depth = 2 * GROUP * tiles
    count = PAIRS * GROUP * tiles
    runs = rows // 2 // TILE
    if coded:
        shape = (runs * run + scale_rows(runs * steps), cols)
        out = jax.ShapeDtypeStruct(shape, jnp.int32)
        out_spec = whole(shape)
    else:
        out = jax.ShapeDtypeStruct((2, runs * run, cols), jnp.float32)
        out_spec = pl.BlockSpec((2, GROUP, cols), lambda l, i, _: (0, l * steps + i, 0))
    return pl.pallas_call(
        partial(remap_kernel, coded, group, last),
        grid_spec=pltpu.PrefetchScalarGridSpec(
            num_scalar_prefetch=1,
            grid=(runs, steps),
            in_specs=[
                pl.BlockSpec((2, GROUP, cols), before),
                pl.BlockSpec((2, GROUP, cols), here),
                pl.BlockSpec((2, GROUP, cols), after),
                whole(edge.shape),
                pl.BlockSpec((4, GROUP, cols), here),
                small, small, small, small,
                whole(moves.shape),
                pl.BlockSpec(memory_space=pl.ANY),
            ],
            out_specs=out_spec,
            scratch_shapes=[
                pltpu.VMEM((depth, 2 * TILE), jnp.bfloat16),
                pltpu.VMEM((count, depth), jnp.bfloat16),
                pltpu.VMEM((count, 2 * TILE), jnp.float32),
                pltpu.VMEM((2 * count, len(MATRIX_STEPS) * TILE), jnp.float32),
            ],
        ),
        out_shape=out,
        compiler_params=params(),
        cost_estimate=pl.CostEstimate(
            flops=1000 if coded or part == 0 else 2 * 10**10, bytes_accessed=0, transcendentals=0
        ),
        name="remap",
    )(half, residual, residual, residual, edge, slopes, source, row_shift, pixel_shift, fraction,
      jnp.asarray(moves, jnp.bfloat16), past)


def cols_forward_kernel(
    sign_ref, own_ref, got_ref, code_ref, next_ref, twiddle_ref, a_high, a_low, b_high, b_low, s_high, s_low,
    out_ref, xa_high, xa_low, xb_high, xb_low, hold,
):
    devices, rows, _ = xa_high.shape
    total_rows = rows * pl.num_programs(0)
    now = pl.program_id(0)
    sign = sign_ref[0]

    def block(r, carry):
        at = pl.ds(pl.multiple_of(r * GROUP, GROUP), GROUP)

        def put(beta, z):
            tc, ts = twiddle_ref[0, beta : beta + 1, :], twiddle_ref[1, beta : beta + 1, :]
            re, im = z[0] * tc + z[1] * ts, z[1] * tc - z[0] * ts
            if beta < devices:
                slot, high, low = beta, xa_high, xa_low
            else:
                slot, high, low = (2 * devices - beta) % devices, xb_high, xb_low
            for i, value in enumerate((re, im)):
                h, l = split(value)
                high[slot, at, i * TILE : (i + 1) * TILE] = h
                low[slot, at, i * TILE : (i + 1) * TILE] = l

        def both(t):
            cols = slice(t * TILE, (t + 1) * TILE)
            unit = unit_of(take_row(code_ref[:, cols], now * (rows // GROUP) + r))
            got = unpack(got_ref[at, cols], unit)
            return [(own_ref[p, at, cols], got[p]) for p in range(2)]

        def total(t):
            return tuple(a + b for a, b in both(t))

        def gap(t):
            return turn(tuple((a - b) * sign for a, b in both(t)), -t, 2 * devices)

        staged_dft(total, lambda k, z: put(2 * k, z), devices, -1, hold)
        staged_dft(gap, lambda k, z: put(2 * k + 1, z), devices, -1, hold)
        return carry

    lax.fori_loop(0, rows // GROUP, block, 0)
    flat = (devices - 1) * rows

    def put_out(slots, which, re, im):
        code = scale_code(largest_of(re, im, 1))
        at = pl.ds(pl.multiple_of(which * total_rows + now * rows, GROUP), rows)
        out_ref[slots, at, :] = pack(re, im, code)
        put_row(out_ref, (slots, slice(-8, None)), 2 * now + which, code)

    for i, (high, low, mh, ml) in enumerate(
        ((xa_high, xa_low, a_high, a_low), (xb_high, xb_low, b_high, b_low))
    ):
        left = tuple(x[1:].reshape(flat, 2 * TILE) for x in (high, low))
        value = product(left, (mh[...], ml[...])).reshape(devices - 1, rows, 2 * TILE)
        put_out(slice(1, devices), i, value[:, :, :TILE], value[:, :, TILE:])
    left = tuple(
        jnp.concatenate([xa[0], xb[0]], axis=1)
        for xa, xb in ((xa_high, xb_high), (xa_low, xb_low))
    )
    value = product(left, (s_high[...], s_low[...])).reshape(1, rows, 4 * TILE)
    for i in range(2):
        put_out(
            slice(0, 1), i, value[:, :, i * TILE : (i + 1) * TILE],
            value[:, :, (i + 2) * TILE : (i + 3) * TILE],
        )


def cols_forward(plan, sign, own, got, later):
    rows, cols = own.shape[1:]
    d = plan.devices
    step = 2 * GROUP
    data = pl.BlockSpec((2, step, cols), lambda i: (0, i, 0))
    codes = got.shape[0] - rows
    shape = (d, 2 * rows + scale_rows(2 * rows // step), TILE)
    square = whole((2 * TILE, 2 * TILE))
    wide = whole((4 * TILE, 4 * TILE))
    return pl.pallas_call(
        cols_forward_kernel,
        grid=(rows // step,),
        in_specs=[
            pl.BlockSpec(memory_space=pltpu.SMEM), data,
            pl.BlockSpec((step, cols), lambda i: (i, 0)),
            pl.BlockSpec((codes, cols), lambda i: (rows // codes, 0)),
            pl.BlockSpec(memory_space=pl.ANY), whole(plan.col_twiddle.shape),
            square, square, square, square, wide, wide,
        ],
        out_specs=whole(shape),
        out_shape=jax.ShapeDtypeStruct(shape, jnp.int32),
        scratch_shapes=[pltpu.VMEM((d, step, 2 * TILE), jnp.bfloat16)] * 4
        + [pltpu.VMEM((d, 2, GROUP, TILE), jnp.float32)],
        compiler_params=params(),
        cost_estimate=pl.CostEstimate(
            flops=2 * 10**10, bytes_accessed=0, transcendentals=0
        ),
        name="cols_forward",
    )(sign, own, got, got, later, plan.col_twiddle, *plan.list_a, *plan.list_b, *plan.special_forward)


def rows_forward_kernel(
    run, a0_ref, a1_ref, b0_ref, b1_ref, code_ref, twiddle_ref, past_ref, out_ref, hold, unit
):
    tiles, step, lanes = out_ref.shape
    half = lanes // 2
    twiddle = (twiddle_ref[0], twiddle_ref[1])
    unit[...] = unit_of(code_ref[...])
    block = pl.program_id(0) * step // (2 * GROUP)

    def load(s):
        g, l = s // 2, s % 2
        at = 2 * (l * (run // (2 * GROUP)) + block)
        a = unpack((a0_ref, a1_ref)[l][g], take_row(unit[g], at))
        b = unpack((b0_ref, b1_ref)[l][g], take_row(unit[g], at + 1))
        return tuple(jnp.concatenate(pair, axis=1) for pair in zip(a, b))

    def store(k, z):
        tc, ts = twiddle[0][:, k : k + 1], twiddle[1][:, k : k + 1]
        out_ref[k, :, :half] = z[0] * tc + z[1] * ts
        out_ref[k, :, half:] = z[1] * tc - z[0] * ts

    staged_dft(load, store, tiles, -1, hold)


def rows_forward(plan, part, parts, x, past):
    d = plan.devices
    tiles = 2 * d
    run = TILE // parts
    lanes = 4 * TILE
    step = 8
    codes = x.shape[1] - 4 * run
    data = lambda k: pl.BlockSpec((d, step, TILE), lambda i: (0, k * (run // step) + i, 0))
    return pl.pallas_call(
        partial(rows_forward_kernel, run),
        grid=(run // step,),
        in_specs=[data(k) for k in range(4)]
        + [
            pl.BlockSpec((d, codes, TILE), lambda i: (0, 4 * run // codes, 0)),
            pl.BlockSpec((2, step, tiles), lambda i: (0, part * (run // step) + i, 0)),
            pl.BlockSpec(memory_space=pl.ANY),
        ],
        out_specs=pl.BlockSpec((tiles, step, lanes), lambda i: (0, i, 0)),
        out_shape=jax.ShapeDtypeStruct((tiles, run, lanes), jnp.float32),
        scratch_shapes=[
            pltpu.VMEM((tiles, 2, step, lanes // 2), jnp.float32),
            pltpu.VMEM((d, codes, TILE), jnp.float32),
        ],
        compiler_params=params(),
        cost_estimate=pl.CostEstimate(
            flops=128 * x.size, bytes_accessed=12 * x.size, transcendentals=0
        ),
        name="rows_forward",
    )(x, x, x, x, x, plan.row_twiddle, past)


def weigh_kernel(n, parts, *refs):
    x_refs = refs[:parts]
    f_high, f_low, g_high, g_low, wave_ref, out_ref = refs[parts:]
    batch, _, lanes = out_ref.shape
    half = lanes // 2
    tiles = n // TILE
    col_wave = wave_ref[...]
    floored = 8.0 * math.pi / n
    col_part = col_wave * col_wave + floored * floored
    digit = lax.broadcasted_iota(jnp.int32, (TILE, half), 0)
    for b in range(batch):
        x = jnp.concatenate(
            [r[b, :, :half] for r in x_refs] + [r[b, :, half:] for r in x_refs], axis=0
        )
        z = product((f_high[...], f_low[...]), split(x))
        row_wave = signed_wave(pl.program_id(0) * batch + b + tiles * digit, n)
        weight = local_weight + 1.0 / (row_wave * row_wave + col_part)
        re, im = z[:TILE], z[TILE:]
        z = jnp.concatenate(
            [weight * (col_wave * im - row_wave * re), -weight * (col_wave * re + row_wave * im)],
            axis=0,
        )
        y = product((g_high[...], g_low[...]), split(z))
        out_ref[b, :, :half] = y[:TILE]
        out_ref[b, :, half:] = y[TILE:]


def weigh(plan, wave, xs):
    tiles, rows, lanes = xs[0].shape
    parts = len(xs)
    batch = 8
    square = whole((2 * TILE, 2 * TILE))
    return pl.pallas_call(
        partial(weigh_kernel, plan.n, parts),
        grid=(tiles // batch,),
        in_specs=[pl.BlockSpec((batch, rows, lanes), lambda i: (i, 0, 0))] * parts
        + [square] * 4 + [whole(wave.shape)],
        out_specs=pl.BlockSpec((batch, parts * rows, lanes), lambda i: (i, 0, 0)),
        out_shape=jax.ShapeDtypeStruct((tiles, parts * rows, lanes), jnp.float32),
        compiler_params=params(),
        cost_estimate=pl.CostEstimate(
            flops=4096 * parts * xs[0].size, bytes_accessed=8 * parts * xs[0].size, transcendentals=0
        ),
        name="weigh",
    )(*xs, *plan.rows_forward, *plan.rows_inverse, wave)


def rows_inverse_kernel(run, x_ref, twiddle_ref, special_ref, past_ref, out_ref, hold, folded):
    tiles, step, lanes = x_ref.shape
    now = pl.program_id(0)
    half = lanes // 2
    twiddle = (twiddle_ref[0], twiddle_ref[1])
    special = special_ref[...] > 0.5

    def load(k):
        tc, ts = twiddle[0][:, k : k + 1], twiddle[1][:, k : k + 1]
        re, im = x_ref[k, :, :half], x_ref[k, :, half:]
        return re * tc - im * ts, im * tc + re * ts

    def store(s, z):
        re_a, re_b = z[0][:, :TILE], z[0][:, TILE:]
        im_a, im_b = z[1][:, :TILE], z[1][:, TILE:]
        folded[s, 0] = jnp.where(special, re_a, re_a + re_b)
        folded[s, 1] = jnp.where(special, re_b, im_a - im_b)

    staged_dft(load, store, tiles, 1, hold)
    for g in range(tiles // 2):
        re, im = folded[2 * g : 2 * g + 2, 0], folded[2 * g : 2 * g + 2, 1]
        code = scale_code(jnp.max(largest_of(re, im, 1), axis=0))
        for l in range(2):
            at = pl.ds(pl.multiple_of(l * run + now * step, 8), step)
            out_ref[g, at, :] = pack(re[l], im[l], code)
        put_row(out_ref, (g, slice(-8, None)), now, code)


def rows_inverse(plan, part, parts, special, x, past):
    tiles, rows, lanes = x.shape
    step = 8
    run = rows // parts // step
    shape = (tiles // 2, 2 * run * step + scale_rows(run), TILE)
    return pl.pallas_call(
        partial(rows_inverse_kernel, run * step),
        grid=(run,),
        in_specs=[
            pl.BlockSpec((tiles, step, lanes), lambda i: (0, part * run + i, 0)),
            pl.BlockSpec((2, step, tiles), lambda i: (0, part * run + i, 0)),
            whole(special.shape),
            pl.BlockSpec(memory_space=pl.ANY),
        ],
        out_specs=whole(shape),
        out_shape=jax.ShapeDtypeStruct(shape, jnp.int32),
        scratch_shapes=[
            pltpu.VMEM((tiles, 2, step, lanes // 2), jnp.float32),
            pltpu.VMEM((tiles, 2, step, TILE), jnp.float32),
        ],
        compiler_params=params(),
        cost_estimate=pl.CostEstimate(
            flops=2 * 10**10 if part > 2 else 1000, bytes_accessed=0, transcendentals=0
        ),
        name="rows_inverse",
    )(x, plan.row_twiddle, special, past)


def cols_inverse_kernel(
    col_ref, sign_ref, x_ref, code_ref, twiddle_ref, g_high, g_low, s_high, s_low, *rest,
):
    keep_ref, send_ref, spectrum, hold = rest[-4:]
    devices, rows, _ = x_ref.shape
    flat = (devices - 1) * rows
    per = pl.num_programs(1)
    for j in range(rows // 8):
        at = slice(8 * j, 8 * j + 8)
        unit = unit_of(take_row(code_ref[...], pl.program_id(1) * (rows // 8) + j))
        re, im = unpack(x_ref[:, at, :], unit)
        spectrum[:, at, :TILE] = re
        spectrum[:, at, TILE:] = im
    value = product(split(spectrum[1:].reshape(flat, 2 * TILE)), (g_high[...], g_low[...]))
    first = product(split(spectrum[0]), (s_high[...], s_low[...]))
    spectrum[1:] = value.reshape(devices - 1, rows, 2 * TILE)
    spectrum[0] = first
    sign = sign_ref[0]
    step = pl.program_id(0) * per + pl.program_id(1)

    def block(r, carry):
        at = pl.ds(pl.multiple_of(r * GROUP, GROUP), GROUP)

        def point(k):
            tc, ts = twiddle_ref[0, k : k + 1, :], twiddle_ref[1, k : k + 1, :]
            if k % 2:
                tc, ts = tc * sign, ts * sign
            re, im = spectrum[k, at, :TILE], spectrum[k, at, TILE:]
            return re * tc - im * ts, im * tc + re * ts

        def load(k):
            if k == 0:
                p, q = spectrum[0, at, :TILE], spectrum[0, at, TILE:]
                return p + q, p - q
            (a, b), (c, d) = point(k), point(devices - k)
            odd = turn((a - c, b + d), k, 2 * devices)
            return a + c - odd[1], b - d + odd[0]

        def store(n, z):
            if 2 * n < devices:
                for i in range(2):
                    keep_ref[at, (2 * n + i) * TILE : (2 * n + i + 1) * TILE] = z[i]
                return
            cols = slice((n - devices // 2) * TILE, (n - devices // 2 + 1) * TILE)
            code = scale_code(largest_of(z[0], z[1], 0))
            down = pl.ds(pl.multiple_of(step * rows + r * GROUP, GROUP), GROUP)
            send_ref[down, cols] = pack(z[0], z[1], code)
            put_row(send_ref, (slice(-8, None), cols), step * (rows // GROUP) + r, code)

        staged_dft(load, store, devices, 1, hold)
        return carry

    lax.fori_loop(0, rows // GROUP, block, 0)


def place_block(part, parts, half_rows, step):
    run = TILE // parts // step
    return lambda l, i, half_ref: (
        half_ref[0] * (half_rows // step) + l * (TILE // step) + part * run + i, 0
    )


def cols_inverse(plan, part, parts, half, sign, x, shape, image):
    d = plan.devices
    step = min(2 * GROUP, TILE // parts)
    runs = shape[0] // 2 // TILE
    rows = runs * TILE // parts
    codes = x.shape[1] - rows
    sent = (rows + scale_rows(rows // GROUP), shape[1] // 2)
    per = TILE // parts // step
    cols = shape[1]
    square = whole((2 * TILE, 2 * TILE))
    smem = pl.BlockSpec(memory_space=pltpu.SMEM)
    extra = [] if image is None else [image]
    return pl.pallas_call(
        cols_inverse_kernel,
        grid_spec=pltpu.PrefetchScalarGridSpec(
            num_scalar_prefetch=1,
            grid=(runs, per),
            in_specs=[
                smem, pl.BlockSpec((d, step, TILE), lambda l, i, _: (0, l * per + i, 0)),
                pl.BlockSpec((d, codes, TILE), lambda l, i, _: (0, rows // codes, 0)),
                whole(plan.col_twiddle.shape), square, square, square, square,
            ] + [pl.BlockSpec(memory_space=pl.ANY)] * len(extra),
            out_specs=[
                pl.BlockSpec((step, cols), place_block(part, parts, shape[0] // 2, step)),
                whole(sent),
            ],
            scratch_shapes=[
                pltpu.VMEM((d, step, 2 * TILE), jnp.float32),
                pltpu.VMEM((d, 2, GROUP, TILE), jnp.float32),
            ],
        ),
        out_shape=[
            jax.ShapeDtypeStruct(shape, jnp.float32),
            jax.ShapeDtypeStruct(sent, jnp.int32),
        ],
        input_output_aliases={9: 0} if extra else {},
        compiler_params=params(),
        cost_estimate=pl.CostEstimate(
            flops=2048 * x.size, bytes_accessed=8 * x.size, transcendentals=0
        ),
        name="cols_inverse",
    )(half, sign, x, x, plan.col_twiddle, *plan.cols_inverse, *plan.special_inverse, *extra)


def place_kernel(half_ref, got_ref, code_ref, image_ref, out_ref, token_ref):
    token_ref[...] = jnp.zeros_like(token_ref)
    rows, cols = got_ref.shape
    step = pl.program_id(0) * pl.num_programs(1) + pl.program_id(1)
    for r in range(rows // GROUP):
        at = slice(r * GROUP, (r + 1) * GROUP)
        for n in range(cols // TILE):
            lanes = slice(n * TILE, (n + 1) * TILE)
            unit = unit_of(take_row(code_ref[:, lanes], step * (rows // GROUP) + r))
            for i, value in enumerate(unpack(got_ref[at, lanes], unit)):
                out_ref[at, (2 * n + i) * TILE : (2 * n + i + 1) * TILE] = value


def place_rows(part, parts, half, got, image):
    cols = image.shape[1]
    step = min(2 * GROUP, TILE // parts)
    runs = image.shape[0] // 2 // TILE
    rows = runs * TILE // parts
    codes = got.shape[0] - rows
    per = TILE // parts // step
    return pl.pallas_call(
        place_kernel,
        grid_spec=pltpu.PrefetchScalarGridSpec(
            num_scalar_prefetch=1,
            grid=(runs, per),
            in_specs=[
                pl.BlockSpec((step, cols // 2), lambda l, i, _: (l * per + i, 0)),
                pl.BlockSpec((codes, cols // 2), lambda l, i, _: (rows // codes, 0)),
                pl.BlockSpec(memory_space=pl.ANY),
            ],
            out_specs=[
                pl.BlockSpec((step, cols), place_block(part, parts, image.shape[0] // 2, step)),
                whole((8, TILE)),
            ],
        ),
        out_shape=[
            jax.ShapeDtypeStruct(image.shape, jnp.float32),
            jax.ShapeDtypeStruct((8, TILE), jnp.float32),
        ],
        input_output_aliases={3: 0},
        compiler_params=params(),
        cost_estimate=pl.CostEstimate(flops=2 * 10**10, bytes_accessed=0, transcendentals=0),
        name="place_rows",
    )(half, got, got, image)


def paired(residual, field_slopes, source_tile, row_shift, pixel_shift, fraction):
    rows_dev, cols_dev = residual.shape[1:]
    devices = lax.axis_size("rows") * lax.axis_size("cols")
    plan = Plan(devices)
    parts = SLICES
    col = lax.axis_index("cols").astype(jnp.int32)
    place = lax.axis_index("rows").astype(jnp.int32) * 2 + col
    mine, other = col.reshape(1), (1 - col).reshape(1)
    sign = (1 - 2 * col).astype(jnp.float32).reshape(1)
    swap = [(0, 1), (1, 0)]
    both = ("rows", "cols")
    before = lax.ppermute(
        residual[:, rows_dev - HALO :], "rows", [(k, k + 1) for k in range(devices // 2 - 1)]
    )
    after = lax.ppermute(
        residual[:, :HALO], "rows", [(k + 1, k) for k in range(devices // 2 - 1)]
    )
    edge = jnp.concatenate([after, before], axis=1)
    args = (residual, edge, field_slopes, source_tile, row_shift, pixel_shift, fraction)
    lane = jnp.arange(TILE, dtype=jnp.int32).reshape(1, TILE)
    special = jnp.where((lane == 0) & (place == 0), 1.0, 0.0)
    wave = plan.wave_of_lists(place)
    spectra = []
    spectra, lists, aways, gots = [], [], [], []

    def send(m, past):
        aways.append(remap_flow(other, m, parts, True, past, *args))
        gots.append(lax.ppermute(aways[m], "cols", swap))

    send(0, special)
    if parts > 1:
        send(1, aways[0])
    for m in range(parts):
        past = gots[m] if m or parts == 1 else aways[1]
        own = remap_flow(mine, m, parts, False, past, *args)
        past = spectra[m - 2] if m > 1 else special
        lists.append(cols_forward(plan, sign, own, gots[m], past))
        if m + 2 < parts:
            send(m + 2, lists[m])
        swapped = lax.all_to_all(lists[m], both, split_axis=0, concat_axis=0, tiled=True)
        past = spectra[m - 1] if m else special
        spectra.append(rows_forward(plan, m, parts, swapped, past))
    mixed = weigh(plan, wave, spectra)
    image = None
    sent = []
    past = [special, special]
    for m in range(parts):
        folded = rows_inverse(plan, m, parts, special, mixed, past[m])
        folded = lax.all_to_all(folded, both, split_axis=0, concat_axis=0, tiled=True)
        if m > 1:
            image, token = place_rows(m - 2, parts, other, sent[m - 2], image)
            past.append(token)
        image, away = cols_inverse(
            plan, m, parts, mine, sign, folded, (rows_dev, cols_dev), image
        )
        if m == 0:
            past.append(away)
        sent.append(lax.ppermute(away, "cols", swap))
    for m in range(max(parts - 2, 0), parts):
        image, _ = place_rows(m, parts, other, sent[m], image)
    return image


def general(residual, field_slopes, source_tile, row_shift, pixel_shift, fraction):
    padded = with_halo(residual, (("rows", 1),), HALO)
    pulled = remap_tiles(padded, source_tile, row_shift, pixel_shift, fraction)
    slopes = field_slopes.astype(jnp.float32)
    flow_across = -(pulled[0] * slopes[0] + pulled[1] * slopes[1])
    downward_flow = -(pulled[0] * slopes[2] + pulled[1] * slopes[3])
    rows_dev = residual.shape[1]
    cols_dev = residual.shape[2]
    rows_count = lax.axis_size("rows")
    cols_count = lax.axis_size("cols")
    part_rows = rows_dev // cols_count
    n = rows_dev * rows_count
    spread = rows_count // cols_count
    col_index = lax.axis_index("cols")
    row_place = lax.axis_index("rows")
    compact_forward_transform = fourier_matrix(rows_count, -1)
    large_forward = fourier_matrix(rows_dev, -1)
    compact_inverse_transform = fourier_matrix(rows_count, 1)
    large_inverse = fourier_matrix(rows_dev, 1)
    wave_index = jnp.arange(rows_count, dtype=jnp.int32)
    pixel_index = jnp.arange(rows_dev, dtype=jnp.int32)
    band = col_index * part_rows + jnp.arange(part_rows, dtype=jnp.int32)
    stacked_planes = jnp.stack([flow_across, downward_flow]).reshape(2, rows_dev, 1, cols_dev)
    stacked_planes = across_columns(stacked_planes).reshape(2, part_rows, rows_count, rows_dev)
    power_spectra = contract_indices("pibc,pbqk->qikc", stacked_planes, compact_forward_transform)[
        :, None
    ]
    cosine, sine_part = phase_pair(wave_index[:, None] * pixel_index[None, :], n, -1)
    power_spectra = rotate(power_spectra, cosine, sine_part)
    power_spectra = contract_indices("pfikc,pcql->qfikl", power_spectra, large_forward)
    fields = power_spectra.shape[1]
    back_cos, back_sin = phase_pair(wave_index[:, None] * pixel_index[None, :], n, 1)
    power_spectra = across_rows(power_spectra)
    power_spectra = power_spectra.reshape(2, fields, rows_count, part_rows, rows_dev)
    power_spectra = contract_indices("pfrik,prqm->qfmik", power_spectra, compact_forward_transform)
    band_cos, band_sin = phase_pair(wave_index[:, None] * band[None, :], n, -1)
    power_spectra = rotate(power_spectra, band_cos[:, :, None], band_sin[:, :, None])
    power_spectra = across_columns(
        power_spectra.reshape(2 * fields, rows_count, part_rows, rows_dev)
    )
    power_spectra = power_spectra.reshape(2, fields, spread, rows_dev, rows_dev)
    power_spectra = contract_indices("pfmsk,psql->qfmlk", power_spectra, large_forward)
    row_freq = (
        rows_count * pixel_index[None, :]
        + (col_index * spread + jnp.arange(spread, dtype=jnp.int32))[:, None]
    )
    row_wave = signed_wave(row_freq, n)[:, :, None]
    col_wave = signed_wave(rows_count * pixel_index + row_place, n)
    mixed = weigh_spectra(power_spectra, row_wave, col_wave, n)
    mixed = contract_indices("pmlk,plqs->qsmk", mixed, large_inverse)
    mixed = across_columns(mixed)
    band_cos, band_sin = phase_pair(band[:, None] * wave_index[None, :], n, 1)
    mixed = rotate(mixed, band_cos[:, :, None], band_sin[:, :, None])
    mixed = contract_indices("pimk,pmqr->qirk", mixed, compact_inverse_transform)
    mixed = across_rows(mixed.reshape(2, 1, part_rows, rows_count, rows_dev))
    mixed = mixed.reshape(2, rows_count, part_rows, rows_dev)
    mixed = contract_indices("pnik,pkqa->qina", mixed, large_inverse)
    mixed = rotate(mixed, back_cos, back_sin)
    image = jnp.einsum(
        "pina,pnb->iba",
        mixed,
        compact_inverse_transform[:, :, 0, :],
        precision=highest,
        preferred_element_type=jnp.float32,
    )
    image = image.reshape(part_rows, cols_count, cols_dev) * (1.0 / (n * n))
    return lax.all_to_all(image, "cols", split_axis=1, concat_axis=0, tiled=True).reshape(
        rows_dev, cols_dev
    )


def per_device(*arrays):
    rows_dev, cols_dev = arrays[0].shape[1:]
    rows_count, cols_count = lax.axis_size("rows"), lax.axis_size("cols")
    devices = rows_count * cols_count
    if cols_count == 2 and rows_dev * rows_count == cols_dev * cols_count == 2 * TILE * devices:
        return paired(*arrays)
    return general(*arrays)


def solution(mesh):
    return jax.shard_map(
        per_device,
        mesh=mesh,
        in_specs=(
            P(None, "rows", "cols"),
            P(None, "rows", "cols"),
            P(None, "rows", "cols"),
            P(None, "rows", "cols"),
            P(None, "rows", "cols"),
            P(None, "rows", "cols"),
        ),
        out_specs=P("rows", "cols"),
        check_vma=False,
    )
```

```python
import math
from functools import partial

import jax
import jax.numpy as jnp
import ml_dtypes
import numpy as np
from jax import lax
from jax.experimental import pallas as pl
from jax.experimental.pallas import tpu as pltpu
from jax.sharding import PartitionSpec as P

TILE = 128
PAIRS = 2
HALO = 8
SHIFT = 2


local_weight = 0.5
highest = lax.Precision.HIGHEST


def with_halo(x, sides, width):
    for axis, dim in sides:
        peers, length = (lax.axis_size(axis), x.shape[dim])
        up = [(i, (i + 1) % peers) for i in range(peers - 1)]
        down = [(j, i) for i, j in up]
        last = lax.slice_in_dim(x, length - width, length, axis=dim)
        first = lax.slice_in_dim(x, 0, width, axis=dim)
        before = lax.ppermute(last, axis, up)
        after = lax.ppermute(first, axis, down)
        x = jnp.concatenate([before, x, after], axis=dim)
    return x


def phase_pair(phases, length, direction):
    angles = phases.astype(jnp.float32) * (direction * 2.0 * math.pi / length)
    return (jnp.cos(angles), jnp.sin(angles))


def fourier_matrix(length, direction):
    counter = jnp.arange(length, dtype=jnp.int32)
    cosine, sine_part = phase_pair(counter[:, None] * counter[None, :] % length, length, direction)
    return jnp.stack([jnp.stack([cosine, sine_part], 1), jnp.stack([-sine_part, cosine], 1)], 0)


def rotate(values, cosine, sine_part):
    real_part = values[0] * cosine - values[1] * sine_part
    imag_part = values[0] * sine_part + values[1] * cosine
    return jnp.stack([real_part, imag_part])


def contract_indices(formula, values, matrix):
    return jnp.einsum(
        formula, values, matrix, precision=highest, preferred_element_type=jnp.float32
    )


def signed_wave(counter, n):
    middle = n // 2
    shifted = jnp.where(counter > middle, counter - n, counter)
    shifted = jnp.where(counter == middle, 0, shifted)
    return shifted.astype(jnp.float32) * (2.0 * math.pi / n)


def across_columns(values):
    return lax.all_to_all(values, "cols", split_axis=1, concat_axis=2, tiled=True)


def across_rows(values):
    return lax.all_to_all(values, "rows", split_axis=3, concat_axis=1, tiled=True)


def remap_tiles(padded, source_tile, row_shift, pixel_shift, fraction):
    rows_dev = padded.shape[1] - 2 * HALO
    tiles_dev = padded.shape[2] // TILE
    tile_rows = padded.reshape(2, (rows_dev + 2 * HALO) * tiles_dev, TILE)
    row_index = jnp.arange(rows_dev, dtype=jnp.int32)[None, :, None]
    flat_index = (row_index + HALO + row_shift) * tiles_dev + source_tile
    picked = jnp.take(tile_rows, flat_index.reshape(-1), axis=1)
    picked = picked.reshape(2, PAIRS, rows_dev, tiles_dev, TILE)
    widened = jnp.pad(picked, ((0, 0), (0, 0), (0, 0), (0, 0), (SHIFT + 1, SHIFT + 1)))
    pulled = jnp.zeros((2, rows_dev, tiles_dev, TILE), jnp.float32)
    for offset in range(-SHIFT, SHIFT + 2):
        weights = jnp.where(pixel_shift == offset, 1.0 - fraction, 0.0)
        weights = weights + jnp.where(pixel_shift + 1 == offset, fraction, 0.0)
        start_at = SHIFT + 1 + offset
        window = widened[..., start_at : start_at + TILE].astype(jnp.float32)
        pulled = pulled + jnp.sum(window * weights[None, :, :, :, None], axis=1)
    return pulled.reshape(2, rows_dev, tiles_dev * TILE)


def weigh_spectra(power_spectra, row_wave, col_wave, n):
    floored_wavenumber = 8.0 * math.pi / n
    weight = local_weight + 1.0 / (
        row_wave * row_wave + col_wave * col_wave + floored_wavenumber * floored_wavenumber
    )
    real_part = weight * (col_wave * power_spectra[1, 0] - row_wave * power_spectra[0, 0])
    imag_part = -weight * (col_wave * power_spectra[0, 0] + row_wave * power_spectra[1, 0])
    return jnp.stack([real_part, imag_part])


GROUP = 16
SLICES = 4
STEPS = tuple(range(-SHIFT, SHIFT + 2))
MATRIX_STEPS = (STEPS[0], STEPS[-1])
VMEM_LIMIT = 48 * 2**20


def turn(x, numerator, denominator):
    numerator %= denominator
    re, im = x
    if numerator == 0:
        return x
    if 4 * numerator == denominator:
        return (-im, re)
    if 2 * numerator == denominator:
        return (-re, -im)
    if 4 * numerator == 3 * denominator:
        return (im, -re)
    if 8 * numerator % denominator == 0:
        half = math.sqrt(0.5)
        a, b = half * re, half * im
        return {1: (a - b, a + b), 3: (-a - b, a - b), 5: (b - a, -a - b), 7: (a + b, b - a)}[
            8 * numerator // denominator
        ]
    angle = 2.0 * math.pi * numerator / denominator
    c, s = math.cos(angle), math.sin(angle)
    return (re * c - im * s, re * s + im * c)


def dft(xs, sign):
    n = len(xs)
    if n == 1:
        return xs
    even, odd = dft(xs[0::2], sign), dft(xs[1::2], sign)
    odd = [turn(x, sign * k, n) for k, x in enumerate(odd)]
    first = [(e[0] + o[0], e[1] + o[1]) for e, o in zip(even, odd)]
    second = [(e[0] - o[0], e[1] - o[1]) for e, o in zip(even, odd)]
    return first + second


def staged_dft(load, store, n, sign, hold):
    outer = 8 if n >= 32 else 2
    inner = n // outer
    for a in range(outer):
        ys = dft([load(a + outer * b) for b in range(inner)], sign)
        for k, y in enumerate(ys):
            re, im = turn(y, sign * a * k, n)
            hold[k * outer + a, 0] = re
            hold[k * outer + a, 1] = im
    for k in range(inner):
        zs = dft([(hold[k * outer + a, 0], hold[k * outer + a, 1]) for a in range(outer)], sign)
        for b, z in enumerate(zs):
            store(k + inner * b, z)


def split(x):
    high = x.astype(jnp.bfloat16)
    return high, (x - high.astype(jnp.float32)).astype(jnp.bfloat16)


def product(left, right):
    dot = lambda a, b: jnp.dot(a, b, preferred_element_type=jnp.float32)
    return dot(left[0], right[0]) + (dot(left[1], right[0]) + dot(left[0], right[1]))


LOG_STEP = math.log(2.0) / 1024.0
TOP = 32767.0


def scale_code(largest):
    return jnp.floor(jnp.log(jnp.maximum(largest, 1e-33)) / LOG_STEP).astype(jnp.int32) + 2


def unit_of(code):
    return jnp.exp(code.astype(jnp.float32) * LOG_STEP) * (1.0 / TOP)


def pack(first, second, code):
    inverse = 1.0 / unit_of(code)
    a, b = (
        jnp.clip(jnp.floor(x * inverse + 0.5), -TOP, TOP).astype(jnp.int32)
        for x in (first, second)
    )
    return (a << 16) | (b & 0xFFFF)


def unpack(packed, unit):
    first, second = packed >> 16, (packed << 16) >> 16
    return first.astype(jnp.float32) * unit, second.astype(jnp.float32) * unit


def largest_of(first, second, axis):
    return jnp.max(jnp.maximum(jnp.abs(first), jnp.abs(second)), axis=axis, keepdims=True)


def put_row(ref, where, row, value):
    old = ref[where]
    lane_row = lax.broadcasted_iota(jnp.int32, old.shape, old.ndim - 2)
    ref[where] = jnp.where(lane_row == row, value, jnp.where(row == 0, 0, old))


def take_row(tile, row):
    rows = lax.broadcasted_iota(jnp.int32, tile.shape, tile.ndim - 2)
    return jnp.sum(jnp.where(rows == row, tile, 0), axis=tile.ndim - 2, keepdims=True)


def scale_rows(count):
    return -(-count // 8) * 8


def halves(matrix):
    high = np.asarray(matrix, np.float32).astype(ml_dtypes.bfloat16)
    low = (np.asarray(matrix, np.float32) - high.astype(np.float32)).astype(ml_dtypes.bfloat16)
    return jnp.asarray(high), jnp.asarray(low)


def phases(product_of_indices, length):
    angle = 2.0 * np.pi * (np.asarray(product_of_indices) % length) / length
    return np.cos(angle), np.sin(angle)


class Plan:
    def __init__(self, devices):
        self.devices = devices
        self.tiles = 2 * devices
        n = self.n = TILE * self.tiles
        j = np.arange(TILE)
        c, s = phases(j[:, None] * j[None, :], TILE)
        back = TILE - 1 - j
        self.list_a = halves(np.block([[c, -s], [s, c]]))
        self.list_b = halves(np.block([[c[:, back], -s[:, back]], [s[:, back], c[:, back]]]))
        self.rows_forward = np.block([[c, s], [-s, c]])
        self.rows_inverse = np.block([[c, -s], [s, c]])
        scale = 1.0 / (2.0 * n * n)
        self.cols_inverse = halves(scale * np.block([[c, s], [-s, c]]))
        low = j < TILE // 2
        digit_a = np.where(low, j, j - TILE // 2)
        digit_b = np.where(low, np.where(j == 0, TILE // 2, TILE - j), TILE - 1 - (j - TILE // 2))
        ca, sa = phases(j[:, None] * digit_a[None, :], TILE)
        cb, sb = phases(j[:, None] * digit_b[None, :], TILE)
        blocks = []
        for mask in (low, ~low):
            blocks.append(np.concatenate([ca * mask, cb * mask, -sa * mask, -sb * mask], 1))
            blocks.append(np.concatenate([sa * mask, sb * mask, ca * mask, cb * mask], 1))
        self.special_forward = halves(np.concatenate(blocks, 0))
        freq = np.where(low, 0, devices) + self.tiles * digit_a
        ci, si = phases(freq[:, None] * j[None, :], n)
        first = np.concatenate([ci * low[:, None], ci * ~low[:, None]], 1)
        second = np.concatenate([-si * low[:, None], -si * ~low[:, None]], 1)
        second[0, :TILE] = 1.0 - 2.0 * (j % 2)
        second[0, TILE:] = 0.0
        self.special_inverse = halves(2.0 * scale * np.concatenate([first, second], 0))
        beta = np.arange(self.tiles)
        tc, ts = phases(beta[:, None] * j[None, :], n)
        self.col_twiddle = jnp.asarray(np.stack([tc, ts]), jnp.float32)
        self.row_twiddle = jnp.asarray(np.stack([tc.T, ts.T]), jnp.float32)
        self.low = low
        self.digit_a, self.digit_b = digit_a, digit_b

    def wave_of_lists(self, place):
        j = jnp.arange(TILE, dtype=jnp.int32)
        usual = place + self.tiles * j
        other = jnp.asarray(np.where(self.low, 0, self.devices) + self.tiles * self.digit_a, jnp.int32)
        other_b = (self.n - other) % self.n
        other_b = other_b.at[0].set(self.n // 2)
        a = jnp.where(place == 0, other, usual)
        b = jnp.where(place == 0, other_b, (self.n - usual) % self.n)
        return signed_wave(jnp.concatenate([a, b]), self.n).reshape(1, 2 * TILE)


def whole(shape):
    return pl.BlockSpec(shape, lambda *_: (0,) * len(shape))


def params():
    return pltpu.CompilerParams(vmem_limit_bytes=VMEM_LIMIT)


def remap_kernel(
    coded, group, last, half_ref, above_ref, here_ref, below_ref, edge_ref, slopes_ref, source_ref,
    row_ref, pixel_ref, fraction_ref, moves_ref, past_ref, out_ref, window, picker, picked, moved,
):
    tiles = slopes_ref.shape[2] // TILE
    span = 2 * GROUP
    count = PAIRS * tiles * GROUP
    here = group(pl.program_id(0), pl.program_id(1), half_ref)
    upper = lax.broadcasted_iota(jnp.int32, (GROUP, TILE), 0) < GROUP // 2

    def fill(after_ref, before_ref):
        for t in range(tiles):
            cols = slice(t * TILE, (t + 1) * TILE)
            for p in range(2):
                lanes = slice(p * TILE, (p + 1) * TILE)
                window[t * span : t * span + GROUP, lanes] = here_ref[p, :, cols]
                window[t * span + GROUP : (t + 1) * span, lanes] = jnp.where(
                    upper, after_ref[p, :, cols], before_ref[p, :, cols]
                )

    @pl.when((here > 0) & (here < last))
    def _():
        fill(below_ref, above_ref)

    @pl.when(here == 0)
    def _():
        fill(below_ref, edge_ref)

    @pl.when(here == last)
    def _():
        fill(edge_ref, above_ref)

    lane = lax.broadcasted_iota(jnp.int32, (GROUP, TILE), 1)
    down = lax.broadcasted_iota(jnp.int32, (GROUP, tiles), 0)
    per = TILE // span
    for k in range(PAIRS):
        source = source_ref[k]
        place = (source % per) * span + ((down + row_ref[k]) & (span - 1))
        block = source // per
        for t in range(tiles):
            here = slice((k * tiles + t) * GROUP, (k * tiles + t + 1) * GROUP)
            hit = jnp.where(place[:, t : t + 1] == lane, 1.0, 0.0).astype(jnp.bfloat16)
            blk = jnp.broadcast_to(block[:, t : t + 1], (GROUP, TILE))
            blk = blk.astype(jnp.float32).astype(jnp.bfloat16)
            for c in range(tiles * span // TILE):
                picker[here, c * TILE : (c + 1) * TILE] = jnp.where(
                    blk == jnp.bfloat16(c), hit, jnp.bfloat16(0)
                )
    picked[...] = jnp.dot(picker[...], window[...], preferred_element_type=jnp.float32)
    for p in range(2):
        moved[p * count : (p + 1) * count, :] = jnp.dot(
            picked[:, p * TILE : (p + 1) * TILE].astype(jnp.bfloat16), moves_ref[...],
            preferred_element_type=jnp.float32,
        )
    for t in range(tiles):
        pulled = [None, None]
        for k in range(PAIRS):
            row0 = (k * tiles + t) * GROUP
            move = jnp.broadcast_to(pixel_ref[k][:, t : t + 1], (GROUP, TILE))
            blend = jnp.broadcast_to(fraction_ref[k][:, t : t + 1], (GROUP, TILE))
            rest = 1.0 - blend
            same = [move == step for step in STEPS[:-2]]
            for p in range(2):
                here = slice(p * count + row0, p * count + row0 + GROUP)
                tile = picked[row0 : row0 + GROUP, p * TILE : (p + 1) * TILE]
                part = []
                for step in STEPS:
                    if step == 0:
                        part.append(tile)
                    elif step in MATRIX_STEPS:
                        i = MATRIX_STEPS.index(step)
                        part.append(moved[here, i * TILE : (i + 1) * TILE])
                    else:
                        inside = (lane + step >= 0) & (lane + step < TILE)
                        part.append(jnp.where(inside, pltpu.roll(tile, -step % TILE, 1), 0.0))
                near, far = part[-2], part[-1]
                for i in range(len(STEPS) - 2):
                    near = jnp.where(same[i], part[i], near)
                    far = jnp.where(same[i], part[i + 1], far)
                term = rest * near + blend * far
                pulled[p] = term if pulled[p] is None else pulled[p] + term
        cols = slice(t * TILE, (t + 1) * TILE)
        slopes = [slopes_ref[i, :, cols].astype(jnp.float32) for i in range(4)]
        across = -(pulled[0] * slopes[0] + pulled[1] * slopes[1])
        downward = -(pulled[0] * slopes[2] + pulled[1] * slopes[3])
        if coded:
            code = scale_code(largest_of(across, downward, 0))
            step = pl.program_id(0) * pl.num_programs(1) + pl.program_id(1)
            at = pl.ds(pl.multiple_of(step * GROUP, GROUP), GROUP)
            out_ref[at, cols] = pack(across, downward, code)
            put_row(out_ref, (slice(-8, None), cols), step, code)
        else:
            out_ref[0, :, cols] = across
            out_ref[1, :, cols] = downward


def remap_flow(
    half, part, parts, coded, past, residual, edge, slopes, source, row_shift, pixel_shift, fraction
):
    rows, cols = slopes.shape[1:]
    tiles = cols // TILE
    run = TILE // parts
    steps = run // GROUP
    half_groups = rows // 2 // GROUP

    def group(l, i, half_ref):
        return half_ref[0] * half_groups + l * (TILE // GROUP) + part * steps + i

    last = rows // GROUP - 1
    here = lambda l, i, half_ref: (0, group(l, i, half_ref), 0)
    before = lambda l, i, half_ref: (0, jnp.maximum(group(l, i, half_ref) - 1, 0), 0)
    after = lambda l, i, half_ref: (0, jnp.minimum(group(l, i, half_ref) + 1, last), 0)
    j = np.arange(TILE)
    moves = np.concatenate([j[:, None] == j[None, :] + step for step in MATRIX_STEPS], axis=1)
    small = pl.BlockSpec((PAIRS, GROUP, tiles), here)
    depth = 2 * GROUP * tiles
    count = PAIRS * GROUP * tiles
    runs = rows // 2 // TILE
    if coded:
        shape = (runs * run + scale_rows(runs * steps), cols)
        out = jax.ShapeDtypeStruct(shape, jnp.int32)
        out_spec = whole(shape)
    else:
        out = jax.ShapeDtypeStruct((2, runs * run, cols), jnp.float32)
        out_spec = pl.BlockSpec((2, GROUP, cols), lambda l, i, _: (0, l * steps + i, 0))
    return pl.pallas_call(
        partial(remap_kernel, coded, group, last),
        grid_spec=pltpu.PrefetchScalarGridSpec(
            num_scalar_prefetch=1,
            grid=(runs, steps),
            in_specs=[
                pl.BlockSpec((2, GROUP, cols), before),
                pl.BlockSpec((2, GROUP, cols), here),
                pl.BlockSpec((2, GROUP, cols), after),
                whole(edge.shape),
                pl.BlockSpec((4, GROUP, cols), here),
                small, small, small, small,
                whole(moves.shape),
                pl.BlockSpec(memory_space=pl.ANY),
            ],
            out_specs=out_spec,
            scratch_shapes=[
                pltpu.VMEM((depth, 2 * TILE), jnp.bfloat16),
                pltpu.VMEM((count, depth), jnp.bfloat16),
                pltpu.VMEM((count, 2 * TILE), jnp.float32),
                pltpu.VMEM((2 * count, len(MATRIX_STEPS) * TILE), jnp.float32),
            ],
        ),
        out_shape=out,
        compiler_params=params(),
        cost_estimate=pl.CostEstimate(
            flops=1000 if coded or part == 0 else 2 * 10**10, bytes_accessed=0, transcendentals=0
        ),
        name="remap",
    )(half, residual, residual, residual, edge, slopes, source, row_shift, pixel_shift, fraction,
      jnp.asarray(moves, jnp.bfloat16), past)


def cols_forward_kernel(
    sign_ref, own_ref, got_ref, code_ref, next_ref, twiddle_ref, a_high, a_low, b_high, b_low, s_high, s_low,
    out_ref, xa_high, xa_low, xb_high, xb_low, hold,
):
    devices, rows, _ = xa_high.shape
    total_rows = rows * pl.num_programs(0)
    now = pl.program_id(0)
    sign = sign_ref[0]

    def block(r, carry):
        at = pl.ds(pl.multiple_of(r * GROUP, GROUP), GROUP)

        def put(beta, z):
            tc, ts = twiddle_ref[0, beta : beta + 1, :], twiddle_ref[1, beta : beta + 1, :]
            re, im = z[0] * tc + z[1] * ts, z[1] * tc - z[0] * ts
            if beta < devices:
                slot, high, low = beta, xa_high, xa_low
            else:
                slot, high, low = (2 * devices - beta) % devices, xb_high, xb_low
            for i, value in enumerate((re, im)):
                h, l = split(value)
                high[slot, at, i * TILE : (i + 1) * TILE] = h
                low[slot, at, i * TILE : (i + 1) * TILE] = l

        def both(t):
            cols = slice(t * TILE, (t + 1) * TILE)
            unit = unit_of(take_row(code_ref[:, cols], now * (rows // GROUP) + r))
            got = unpack(got_ref[at, cols], unit)
            return [(own_ref[p, at, cols], got[p]) for p in range(2)]

        def total(t):
            return tuple(a + b for a, b in both(t))

        def gap(t):
            return turn(tuple((a - b) * sign for a, b in both(t)), -t, 2 * devices)

        staged_dft(total, lambda k, z: put(2 * k, z), devices, -1, hold)
        staged_dft(gap, lambda k, z: put(2 * k + 1, z), devices, -1, hold)
        return carry

    lax.fori_loop(0, rows // GROUP, block, 0)
    flat = (devices - 1) * rows

    def put_out(slots, which, re, im):
        code = scale_code(largest_of(re, im, 1))
        at = pl.ds(pl.multiple_of(which * total_rows + now * rows, GROUP), rows)
        out_ref[slots, at, :] = pack(re, im, code)
        put_row(out_ref, (slots, slice(-8, None)), 2 * now + which, code)

    for i, (high, low, mh, ml) in enumerate(
        ((xa_high, xa_low, a_high, a_low), (xb_high, xb_low, b_high, b_low))
    ):
        left = tuple(x[1:].reshape(flat, 2 * TILE) for x in (high, low))
        value = product(left, (mh[...], ml[...])).reshape(devices - 1, rows, 2 * TILE)
        put_out(slice(1, devices), i, value[:, :, :TILE], value[:, :, TILE:])
    left = tuple(
        jnp.concatenate([xa[0], xb[0]], axis=1)
        for xa, xb in ((xa_high, xb_high), (xa_low, xb_low))
    )
    value = product(left, (s_high[...], s_low[...])).reshape(1, rows, 4 * TILE)
    for i in range(2):
        put_out(
            slice(0, 1), i, value[:, :, i * TILE : (i + 1) * TILE],
            value[:, :, (i + 2) * TILE : (i + 3) * TILE],
        )


def cols_forward(plan, sign, own, got, later):
    rows, cols = own.shape[1:]
    d = plan.devices
    step = 2 * GROUP
    data = pl.BlockSpec((2, step, cols), lambda i: (0, i, 0))
    codes = got.shape[0] - rows
    shape = (d, 2 * rows + scale_rows(2 * rows // step), TILE)
    square = whole((2 * TILE, 2 * TILE))
    wide = whole((4 * TILE, 4 * TILE))
    return pl.pallas_call(
        cols_forward_kernel,
        grid=(rows // step,),
        in_specs=[
            pl.BlockSpec(memory_space=pltpu.SMEM), data,
            pl.BlockSpec((step, cols), lambda i: (i, 0)),
            pl.BlockSpec((codes, cols), lambda i: (rows // codes, 0)),
            pl.BlockSpec(memory_space=pl.ANY), whole(plan.col_twiddle.shape),
            square, square, square, square, wide, wide,
        ],
        out_specs=whole(shape),
        out_shape=jax.ShapeDtypeStruct(shape, jnp.int32),
        scratch_shapes=[pltpu.VMEM((d, step, 2 * TILE), jnp.bfloat16)] * 4
        + [pltpu.VMEM((d, 2, GROUP, TILE), jnp.float32)],
        compiler_params=params(),
        cost_estimate=pl.CostEstimate(
            flops=2 * 10**10, bytes_accessed=0, transcendentals=0
        ),
        name="cols_forward",
    )(sign, own, got, got, later, plan.col_twiddle, *plan.list_a, *plan.list_b, *plan.special_forward)


def rows_forward_kernel(
    run, a0_ref, a1_ref, b0_ref, b1_ref, code_ref, twiddle_ref, past_ref, out_ref, hold, unit
):
    tiles, step, lanes = out_ref.shape
    half = lanes // 2
    twiddle = (twiddle_ref[0], twiddle_ref[1])
    unit[...] = unit_of(code_ref[...])
    block = pl.program_id(0) * step // (2 * GROUP)

    def load(s):
        g, l = s // 2, s % 2
        at = 2 * (l * (run // (2 * GROUP)) + block)
        a = unpack((a0_ref, a1_ref)[l][g], take_row(unit[g], at))
        b = unpack((b0_ref, b1_ref)[l][g], take_row(unit[g], at + 1))
        return tuple(jnp.concatenate(pair, axis=1) for pair in zip(a, b))

    def store(k, z):
        tc, ts = twiddle[0][:, k : k + 1], twiddle[1][:, k : k + 1]
        out_ref[k, :, :half] = z[0] * tc + z[1] * ts
        out_ref[k, :, half:] = z[1] * tc - z[0] * ts

    staged_dft(load, store, tiles, -1, hold)


def rows_forward(plan, part, parts, x, past):
    d = plan.devices
    tiles = 2 * d
    run = TILE // parts
    lanes = 4 * TILE
    step = 8
    codes = x.shape[1] - 4 * run
    data = lambda k: pl.BlockSpec((d, step, TILE), lambda i: (0, k * (run // step) + i, 0))
    return pl.pallas_call(
        partial(rows_forward_kernel, run),
        grid=(run // step,),
        in_specs=[data(k) for k in range(4)]
        + [
            pl.BlockSpec((d, codes, TILE), lambda i: (0, 4 * run // codes, 0)),
            pl.BlockSpec((2, step, tiles), lambda i: (0, part * (run // step) + i, 0)),
            pl.BlockSpec(memory_space=pl.ANY),
        ],
        out_specs=pl.BlockSpec((tiles, step, lanes), lambda i: (0, i, 0)),
        out_shape=jax.ShapeDtypeStruct((tiles, run, lanes), jnp.float32),
        scratch_shapes=[
            pltpu.VMEM((tiles, 2, step, lanes // 2), jnp.float32),
            pltpu.VMEM((d, codes, TILE), jnp.float32),
        ],
        compiler_params=params(),
        cost_estimate=pl.CostEstimate(
            flops=128 * x.size, bytes_accessed=12 * x.size, transcendentals=0
        ),
        name="rows_forward",
    )(x, x, x, x, x, plan.row_twiddle, past)


def run_index(first, last):
    return np.r_[first:last, TILE + first : TILE + last]


def gather_kernel(parts, *refs):
    x_refs = refs[:parts]
    f_high, f_low, out_ref = refs[parts:]
    batch, _, half = out_ref.shape
    for b in range(batch):
        x = jnp.concatenate(
            [r[b, :, :half] for r in x_refs] + [r[b, :, half:] for r in x_refs], axis=0
        )
        out_ref[b] = product((f_high[...], f_low[...]), split(x))


def gather_rows(plan, xs):
    tiles, rows, lanes = xs[0].shape
    parts = len(xs)
    batch = 8
    matrix = halves(plan.rows_forward[:, run_index(0, parts * rows)])
    return pl.pallas_call(
        partial(gather_kernel, parts),
        grid=(tiles // batch,),
        in_specs=[pl.BlockSpec((batch, rows, lanes), lambda i: (i, 0, 0))] * parts
        + [whole(matrix[0].shape)] * 2,
        out_specs=pl.BlockSpec((batch, 2 * TILE, lanes // 2), lambda i: (i, 0, 0)),
        out_shape=jax.ShapeDtypeStruct((tiles, 2 * TILE, lanes // 2), jnp.float32),
        compiler_params=params(),
        cost_estimate=pl.CostEstimate(flops=10**10, bytes_accessed=0, transcendentals=0),
        name="gather_rows",
    )(*xs, *matrix)


def weigh_kernel(
    n, sum_ref, x_ref, f_high, f_low, g_high, g_low, wave_ref, out_ref, high_ref, low_ref
):
    batch, rows, lanes = out_ref.shape
    half = lanes // 2
    tiles = n // TILE
    col_wave = wave_ref[...]
    floored = 8.0 * math.pi / n
    col_part = col_wave * col_wave + floored * floored
    digit = lax.broadcasted_iota(jnp.int32, (TILE, half), 0)
    for b in range(batch):
        x = jnp.concatenate([x_ref[b, :, :half], x_ref[b, :, half:]], axis=0)
        z = sum_ref[b] + product((f_high[...], f_low[...]), split(x))
        row_wave = signed_wave(pl.program_id(0) * batch + b + tiles * digit, n)
        weight = local_weight + 1.0 / (row_wave * row_wave + col_part)
        re, im = z[:TILE], z[TILE:]
        z = jnp.concatenate(
            [weight * (col_wave * im - row_wave * re), -weight * (col_wave * re + row_wave * im)],
            axis=0,
        )
        high, low = split(z)
        high_ref[b] = high
        low_ref[b] = low
        y = product((g_high[...], g_low[...]), (high, low))
        out_ref[b, :, :half] = y[:rows]
        out_ref[b, :, half:] = y[rows:]


def weigh(plan, wave, summed, x):
    tiles, rows, lanes = x.shape
    batch = 8
    forward = halves(plan.rows_forward[:, run_index(TILE - rows, TILE)])
    inverse = halves(plan.rows_inverse[run_index(0, rows)])
    block = lambda *dims: pl.BlockSpec((batch,) + dims, lambda i: (i, 0, 0))
    square = (2 * TILE, lanes // 2)
    return pl.pallas_call(
        partial(weigh_kernel, plan.n),
        grid=(tiles // batch,),
        in_specs=[block(*square), block(rows, lanes)]
        + [whole(forward[0].shape)] * 2
        + [whole(inverse[0].shape)] * 2
        + [whole(wave.shape)],
        out_specs=[block(rows, lanes), block(*square), block(*square)],
        out_shape=[jax.ShapeDtypeStruct((tiles, rows, lanes), jnp.float32)]
        + [jax.ShapeDtypeStruct((tiles,) + square, jnp.bfloat16)] * 2,
        compiler_params=params(),
        cost_estimate=pl.CostEstimate(flops=10**10, bytes_accessed=0, transcendentals=0),
        name="weigh",
    )(summed, x, *forward, *inverse, wave)


def spread_kernel(high_ref, low_ref, g_high, g_low, out_ref):
    batch, rows, lanes = out_ref.shape
    half = lanes // 2
    for b in range(batch):
        y = product((g_high[...], g_low[...]), (high_ref[b], low_ref[b]))
        out_ref[b, :, :half] = y[:rows]
        out_ref[b, :, half:] = y[rows:]


def spread_rows(plan, first, high, low):
    tiles, _, half = high.shape
    batch = 8
    rows = TILE - first
    inverse = halves(plan.rows_inverse[run_index(first, TILE)])
    block = lambda *dims: pl.BlockSpec((batch,) + dims, lambda i: (i, 0, 0))
    return pl.pallas_call(
        spread_kernel,
        grid=(tiles // batch,),
        in_specs=[block(2 * TILE, half)] * 2 + [whole(inverse[0].shape)] * 2,
        out_specs=block(rows, 2 * half),
        out_shape=jax.ShapeDtypeStruct((tiles, rows, 2 * half), jnp.float32),
        compiler_params=params(),
        cost_estimate=pl.CostEstimate(flops=10**10, bytes_accessed=0, transcendentals=0),
        name="spread_rows",
    )(high, low, *inverse)


def rows_inverse_kernel(run, x_ref, twiddle_ref, special_ref, past_ref, out_ref, hold, folded):
    tiles, step, lanes = x_ref.shape
    now = pl.program_id(0)
    half = lanes // 2
    twiddle = (twiddle_ref[0], twiddle_ref[1])
    special = special_ref[...] > 0.5

    def load(k):
        tc, ts = twiddle[0][:, k : k + 1], twiddle[1][:, k : k + 1]
        re, im = x_ref[k, :, :half], x_ref[k, :, half:]
        return re * tc - im * ts, im * tc + re * ts

    def store(s, z):
        re_a, re_b = z[0][:, :TILE], z[0][:, TILE:]
        im_a, im_b = z[1][:, :TILE], z[1][:, TILE:]
        folded[s, 0] = jnp.where(special, re_a, re_a + re_b)
        folded[s, 1] = jnp.where(special, re_b, im_a - im_b)

    staged_dft(load, store, tiles, 1, hold)
    for g in range(tiles // 2):
        re, im = folded[2 * g : 2 * g + 2, 0], folded[2 * g : 2 * g + 2, 1]
        code = scale_code(jnp.max(largest_of(re, im, 1), axis=0))
        for l in range(2):
            at = pl.ds(pl.multiple_of(l * run + now * step, 8), step)
            out_ref[g, at, :] = pack(re[l], im[l], code)
        put_row(out_ref, (g, slice(-8, None)), now, code)


def rows_inverse(plan, part, parts, first, special, x, past):
    tiles, rows, lanes = x.shape
    step = 8
    run = TILE // parts // step
    shape = (tiles // 2, 2 * run * step + scale_rows(run), TILE)
    return pl.pallas_call(
        partial(rows_inverse_kernel, run * step),
        grid=(run,),
        in_specs=[
            pl.BlockSpec((tiles, step, lanes), lambda i: (0, (part - first) * run + i, 0)),
            pl.BlockSpec((2, step, tiles), lambda i: (0, part * run + i, 0)),
            whole(special.shape),
            pl.BlockSpec(memory_space=pl.ANY),
        ],
        out_specs=whole(shape),
        out_shape=jax.ShapeDtypeStruct(shape, jnp.int32),
        scratch_shapes=[
            pltpu.VMEM((tiles, 2, step, lanes // 2), jnp.float32),
            pltpu.VMEM((tiles, 2, step, TILE), jnp.float32),
        ],
        compiler_params=params(),
        cost_estimate=pl.CostEstimate(
            flops=2 * 10**10 if part > 2 else 1000, bytes_accessed=0, transcendentals=0
        ),
        name="rows_inverse",
    )(x, plan.row_twiddle, special, past)


def cols_inverse_kernel(
    col_ref, sign_ref, x_ref, code_ref, twiddle_ref, g_high, g_low, s_high, s_low, *rest,
):
    keep_ref, send_ref, spectrum, hold = rest[-4:]
    devices, rows, _ = x_ref.shape
    flat = (devices - 1) * rows
    per = pl.num_programs(1)
    for j in range(rows // 8):
        at = slice(8 * j, 8 * j + 8)
        unit = unit_of(take_row(code_ref[...], pl.program_id(1) * (rows // 8) + j))
        re, im = unpack(x_ref[:, at, :], unit)
        spectrum[:, at, :TILE] = re
        spectrum[:, at, TILE:] = im
    value = product(split(spectrum[1:].reshape(flat, 2 * TILE)), (g_high[...], g_low[...]))
    first = product(split(spectrum[0]), (s_high[...], s_low[...]))
    spectrum[1:] = value.reshape(devices - 1, rows, 2 * TILE)
    spectrum[0] = first
    sign = sign_ref[0]
    step = pl.program_id(0) * per + pl.program_id(1)

    def block(r, carry):
        at = pl.ds(pl.multiple_of(r * GROUP, GROUP), GROUP)

        def point(k):
            tc, ts = twiddle_ref[0, k : k + 1, :], twiddle_ref[1, k : k + 1, :]
            if k % 2:
                tc, ts = tc * sign, ts * sign
            re, im = spectrum[k, at, :TILE], spectrum[k, at, TILE:]
            return re * tc - im * ts, im * tc + re * ts

        def load(k):
            if k == 0:
                p, q = spectrum[0, at, :TILE], spectrum[0, at, TILE:]
                return p + q, p - q
            (a, b), (c, d) = point(k), point(devices - k)
            odd = turn((a - c, b + d), k, 2 * devices)
            return a + c - odd[1], b - d + odd[0]

        def store(n, z):
            if 2 * n < devices:
                for i in range(2):
                    keep_ref[at, (2 * n + i) * TILE : (2 * n + i + 1) * TILE] = z[i]
                return
            cols = slice((n - devices // 2) * TILE, (n - devices // 2 + 1) * TILE)
            code = scale_code(largest_of(z[0], z[1], 0))
            down = pl.ds(pl.multiple_of(step * rows + r * GROUP, GROUP), GROUP)
            send_ref[down, cols] = pack(z[0], z[1], code)
            put_row(send_ref, (slice(-8, None), cols), step * (rows // GROUP) + r, code)

        staged_dft(load, store, devices, 1, hold)
        return carry

    lax.fori_loop(0, rows // GROUP, block, 0)


def place_block(part, parts, half_rows, step):
    run = TILE // parts // step
    return lambda l, i, half_ref: (
        half_ref[0] * (half_rows // step) + l * (TILE // step) + part * run + i, 0
    )


def cols_inverse(plan, part, parts, half, sign, x, shape, image):
    d = plan.devices
    step = min(2 * GROUP, TILE // parts)
    runs = shape[0] // 2 // TILE
    rows = runs * TILE // parts
    codes = x.shape[1] - rows
    sent = (rows + scale_rows(rows // GROUP), shape[1] // 2)
    per = TILE // parts // step
    cols = shape[1]
    square = whole((2 * TILE, 2 * TILE))
    smem = pl.BlockSpec(memory_space=pltpu.SMEM)
    extra = [] if image is None else [image]
    return pl.pallas_call(
        cols_inverse_kernel,
        grid_spec=pltpu.PrefetchScalarGridSpec(
            num_scalar_prefetch=1,
            grid=(runs, per),
            in_specs=[
                smem, pl.BlockSpec((d, step, TILE), lambda l, i, _: (0, l * per + i, 0)),
                pl.BlockSpec((d, codes, TILE), lambda l, i, _: (0, rows // codes, 0)),
                whole(plan.col_twiddle.shape), square, square, square, square,
            ] + [pl.BlockSpec(memory_space=pl.ANY)] * len(extra),
            out_specs=[
                pl.BlockSpec((step, cols), place_block(part, parts, shape[0] // 2, step)),
                whole(sent),
            ],
            scratch_shapes=[
                pltpu.VMEM((d, step, 2 * TILE), jnp.float32),
                pltpu.VMEM((d, 2, GROUP, TILE), jnp.float32),
            ],
        ),
        out_shape=[
            jax.ShapeDtypeStruct(shape, jnp.float32),
            jax.ShapeDtypeStruct(sent, jnp.int32),
        ],
        input_output_aliases={9: 0} if extra else {},
        compiler_params=params(),
        cost_estimate=pl.CostEstimate(
            flops=2048 * x.size, bytes_accessed=8 * x.size, transcendentals=0
        ),
        name="cols_inverse",
    )(half, sign, x, x, plan.col_twiddle, *plan.cols_inverse, *plan.special_inverse, *extra)


def place_kernel(half_ref, got_ref, code_ref, image_ref, out_ref, token_ref):
    token_ref[...] = jnp.zeros_like(token_ref)
    rows, cols = got_ref.shape
    step = pl.program_id(0) * pl.num_programs(1) + pl.program_id(1)
    for r in range(rows // GROUP):
        at = slice(r * GROUP, (r + 1) * GROUP)
        for n in range(cols // TILE):
            lanes = slice(n * TILE, (n + 1) * TILE)
            unit = unit_of(take_row(code_ref[:, lanes], step * (rows // GROUP) + r))
            for i, value in enumerate(unpack(got_ref[at, lanes], unit)):
                out_ref[at, (2 * n + i) * TILE : (2 * n + i + 1) * TILE] = value


def place_rows(part, parts, half, got, image):
    cols = image.shape[1]
    step = min(2 * GROUP, TILE // parts)
    runs = image.shape[0] // 2 // TILE
    rows = runs * TILE // parts
    codes = got.shape[0] - rows
    per = TILE // parts // step
    return pl.pallas_call(
        place_kernel,
        grid_spec=pltpu.PrefetchScalarGridSpec(
            num_scalar_prefetch=1,
            grid=(runs, per),
            in_specs=[
                pl.BlockSpec((step, cols // 2), lambda l, i, _: (l * per + i, 0)),
                pl.BlockSpec((codes, cols // 2), lambda l, i, _: (rows // codes, 0)),
                pl.BlockSpec(memory_space=pl.ANY),
            ],
            out_specs=[
                pl.BlockSpec((step, cols), place_block(part, parts, image.shape[0] // 2, step)),
                whole((8, TILE)),
            ],
        ),
        out_shape=[
            jax.ShapeDtypeStruct(image.shape, jnp.float32),
            jax.ShapeDtypeStruct((8, TILE), jnp.float32),
        ],
        input_output_aliases={3: 0},
        compiler_params=params(),
        cost_estimate=pl.CostEstimate(flops=2 * 10**10, bytes_accessed=0, transcendentals=0),
        name="place_rows",
    )(half, got, got, image)


def paired(residual, field_slopes, source_tile, row_shift, pixel_shift, fraction):
    rows_dev, cols_dev = residual.shape[1:]
    devices = lax.axis_size("rows") * lax.axis_size("cols")
    plan = Plan(devices)
    parts = SLICES
    col = lax.axis_index("cols").astype(jnp.int32)
    place = lax.axis_index("rows").astype(jnp.int32) * 2 + col
    mine, other = col.reshape(1), (1 - col).reshape(1)
    sign = (1 - 2 * col).astype(jnp.float32).reshape(1)
    swap = [(0, 1), (1, 0)]
    both = ("rows", "cols")
    before = lax.ppermute(
        residual[:, rows_dev - HALO :], "rows", [(k, k + 1) for k in range(devices // 2 - 1)]
    )
    after = lax.ppermute(
        residual[:, :HALO], "rows", [(k + 1, k) for k in range(devices // 2 - 1)]
    )
    edge = jnp.concatenate([after, before], axis=1)
    args = (residual, edge, field_slopes, source_tile, row_shift, pixel_shift, fraction)
    lane = jnp.arange(TILE, dtype=jnp.int32).reshape(1, TILE)
    special = jnp.where((lane == 0) & (place == 0), 1.0, 0.0)
    wave = plan.wave_of_lists(place)
    spectra = []
    spectra, lists, aways, gots = [], [], [], []

    def send(m, past):
        aways.append(remap_flow(other, m, parts, True, past, *args))
        gots.append(lax.ppermute(aways[m], "cols", swap))

    send(0, special)
    if parts > 1:
        send(1, aways[0])
    for m in range(parts):
        past = gots[m] if m or parts == 1 else aways[1]
        own = remap_flow(mine, m, parts, False, past, *args)
        past = spectra[m - 2] if m > 1 else special
        lists.append(cols_forward(plan, sign, own, gots[m], past))
        if m + 2 < parts:
            send(m + 2, lists[m])
        swapped = lax.all_to_all(lists[m], both, split_axis=0, concat_axis=0, tiled=True)
        past = spectra[m - 1] if m else special
        spectra.append(rows_forward(plan, m, parts, swapped, past))
    summed = gather_rows(plan, spectra[:-1])
    mixed, high, low = weigh(plan, wave, summed, spectra[-1])
    others = spread_rows(plan, TILE // parts, high, low)
    image = None
    sent = []
    past = [special, special]
    for m in range(parts):
        mixed = others if m else mixed
        folded = rows_inverse(plan, m, parts, min(m, 1), special, mixed, past[m])
        folded = lax.all_to_all(folded, both, split_axis=0, concat_axis=0, tiled=True)
        if m > 1:
            image, token = place_rows(m - 2, parts, other, sent[m - 2], image)
            past.append(token)
        image, away = cols_inverse(
            plan, m, parts, mine, sign, folded, (rows_dev, cols_dev), image
        )
        if m == 0:
            past.append(away)
        sent.append(lax.ppermute(away, "cols", swap))
    for m in range(max(parts - 2, 0), parts):
        image, _ = place_rows(m, parts, other, sent[m], image)
    return image


def general(residual, field_slopes, source_tile, row_shift, pixel_shift, fraction):
    padded = with_halo(residual, (("rows", 1),), HALO)
    pulled = remap_tiles(padded, source_tile, row_shift, pixel_shift, fraction)
    slopes = field_slopes.astype(jnp.float32)
    flow_across = -(pulled[0] * slopes[0] + pulled[1] * slopes[1])
    downward_flow = -(pulled[0] * slopes[2] + pulled[1] * slopes[3])
    rows_dev = residual.shape[1]
    cols_dev = residual.shape[2]
    rows_count = lax.axis_size("rows")
    cols_count = lax.axis_size("cols")
    part_rows = rows_dev // cols_count
    n = rows_dev * rows_count
    spread = rows_count // cols_count
    col_index = lax.axis_index("cols")
    row_place = lax.axis_index("rows")
    compact_forward_transform = fourier_matrix(rows_count, -1)
    large_forward = fourier_matrix(rows_dev, -1)
    compact_inverse_transform = fourier_matrix(rows_count, 1)
    large_inverse = fourier_matrix(rows_dev, 1)
    wave_index = jnp.arange(rows_count, dtype=jnp.int32)
    pixel_index = jnp.arange(rows_dev, dtype=jnp.int32)
    band = col_index * part_rows + jnp.arange(part_rows, dtype=jnp.int32)
    stacked_planes = jnp.stack([flow_across, downward_flow]).reshape(2, rows_dev, 1, cols_dev)
    stacked_planes = across_columns(stacked_planes).reshape(2, part_rows, rows_count, rows_dev)
    power_spectra = contract_indices("pibc,pbqk->qikc", stacked_planes, compact_forward_transform)[
        :, None
    ]
    cosine, sine_part = phase_pair(wave_index[:, None] * pixel_index[None, :], n, -1)
    power_spectra = rotate(power_spectra, cosine, sine_part)
    power_spectra = contract_indices("pfikc,pcql->qfikl", power_spectra, large_forward)
    fields = power_spectra.shape[1]
    back_cos, back_sin = phase_pair(wave_index[:, None] * pixel_index[None, :], n, 1)
    power_spectra = across_rows(power_spectra)
    power_spectra = power_spectra.reshape(2, fields, rows_count, part_rows, rows_dev)
    power_spectra = contract_indices("pfrik,prqm->qfmik", power_spectra, compact_forward_transform)
    band_cos, band_sin = phase_pair(wave_index[:, None] * band[None, :], n, -1)
    power_spectra = rotate(power_spectra, band_cos[:, :, None], band_sin[:, :, None])
    power_spectra = across_columns(
        power_spectra.reshape(2 * fields, rows_count, part_rows, rows_dev)
    )
    power_spectra = power_spectra.reshape(2, fields, spread, rows_dev, rows_dev)
    power_spectra = contract_indices("pfmsk,psql->qfmlk", power_spectra, large_forward)
    row_freq = (
        rows_count * pixel_index[None, :]
        + (col_index * spread + jnp.arange(spread, dtype=jnp.int32))[:, None]
    )
    row_wave = signed_wave(row_freq, n)[:, :, None]
    col_wave = signed_wave(rows_count * pixel_index + row_place, n)
    mixed = weigh_spectra(power_spectra, row_wave, col_wave, n)
    mixed = contract_indices("pmlk,plqs->qsmk", mixed, large_inverse)
    mixed = across_columns(mixed)
    band_cos, band_sin = phase_pair(band[:, None] * wave_index[None, :], n, 1)
    mixed = rotate(mixed, band_cos[:, :, None], band_sin[:, :, None])
    mixed = contract_indices("pimk,pmqr->qirk", mixed, compact_inverse_transform)
    mixed = across_rows(mixed.reshape(2, 1, part_rows, rows_count, rows_dev))
    mixed = mixed.reshape(2, rows_count, part_rows, rows_dev)
    mixed = contract_indices("pnik,pkqa->qina", mixed, large_inverse)
    mixed = rotate(mixed, back_cos, back_sin)
    image = jnp.einsum(
        "pina,pnb->iba",
        mixed,
        compact_inverse_transform[:, :, 0, :],
        precision=highest,
        preferred_element_type=jnp.float32,
    )
    image = image.reshape(part_rows, cols_count, cols_dev) * (1.0 / (n * n))
    return lax.all_to_all(image, "cols", split_axis=1, concat_axis=0, tiled=True).reshape(
        rows_dev, cols_dev
    )


def per_device(*arrays):
    rows_dev, cols_dev = arrays[0].shape[1:]
    rows_count, cols_count = lax.axis_size("rows"), lax.axis_size("cols")
    devices = rows_count * cols_count
    if cols_count == 2 and rows_dev * rows_count == cols_dev * cols_count == 2 * TILE * devices:
        return paired(*arrays)
    return general(*arrays)


def solution(mesh):
    return jax.shard_map(
        per_device,
        mesh=mesh,
        in_specs=(
            P(None, "rows", "cols"),
            P(None, "rows", "cols"),
            P(None, "rows", "cols"),
            P(None, "rows", "cols"),
            P(None, "rows", "cols"),
            P(None, "rows", "cols"),
        ),
        out_specs=P("rows", "cols"),
        check_vma=False,
    )
```

```python
import math
from functools import partial

import jax
import jax.numpy as jnp
import ml_dtypes
import numpy as np
from jax import lax
from jax.experimental import pallas as pl
from jax.experimental.pallas import tpu as pltpu
from jax.sharding import PartitionSpec as P

TILE = 128
PAIRS = 2
HALO = 8
SHIFT = 2


local_weight = 0.5
highest = lax.Precision.HIGHEST


def with_halo(x, sides, width):
    for axis, dim in sides:
        peers, length = (lax.axis_size(axis), x.shape[dim])
        up = [(i, (i + 1) % peers) for i in range(peers - 1)]
        down = [(j, i) for i, j in up]
        last = lax.slice_in_dim(x, length - width, length, axis=dim)
        first = lax.slice_in_dim(x, 0, width, axis=dim)
        before = lax.ppermute(last, axis, up)
        after = lax.ppermute(first, axis, down)
        x = jnp.concatenate([before, x, after], axis=dim)
    return x


def phase_pair(phases, length, direction):
    angles = phases.astype(jnp.float32) * (direction * 2.0 * math.pi / length)
    return (jnp.cos(angles), jnp.sin(angles))


def fourier_matrix(length, direction):
    counter = jnp.arange(length, dtype=jnp.int32)
    cosine, sine_part = phase_pair(counter[:, None] * counter[None, :] % length, length, direction)
    return jnp.stack([jnp.stack([cosine, sine_part], 1), jnp.stack([-sine_part, cosine], 1)], 0)


def rotate(values, cosine, sine_part):
    real_part = values[0] * cosine - values[1] * sine_part
    imag_part = values[0] * sine_part + values[1] * cosine
    return jnp.stack([real_part, imag_part])


def contract_indices(formula, values, matrix):
    return jnp.einsum(
        formula, values, matrix, precision=highest, preferred_element_type=jnp.float32
    )


def signed_wave(counter, n):
    middle = n // 2
    shifted = jnp.where(counter > middle, counter - n, counter)
    shifted = jnp.where(counter == middle, 0, shifted)
    return shifted.astype(jnp.float32) * (2.0 * math.pi / n)


def across_columns(values):
    return lax.all_to_all(values, "cols", split_axis=1, concat_axis=2, tiled=True)


def across_rows(values):
    return lax.all_to_all(values, "rows", split_axis=3, concat_axis=1, tiled=True)


def remap_tiles(padded, source_tile, row_shift, pixel_shift, fraction):
    rows_dev = padded.shape[1] - 2 * HALO
    tiles_dev = padded.shape[2] // TILE
    tile_rows = padded.reshape(2, (rows_dev + 2 * HALO) * tiles_dev, TILE)
    row_index = jnp.arange(rows_dev, dtype=jnp.int32)[None, :, None]
    flat_index = (row_index + HALO + row_shift) * tiles_dev + source_tile
    picked = jnp.take(tile_rows, flat_index.reshape(-1), axis=1)
    picked = picked.reshape(2, PAIRS, rows_dev, tiles_dev, TILE)
    widened = jnp.pad(picked, ((0, 0), (0, 0), (0, 0), (0, 0), (SHIFT + 1, SHIFT + 1)))
    pulled = jnp.zeros((2, rows_dev, tiles_dev, TILE), jnp.float32)
    for offset in range(-SHIFT, SHIFT + 2):
        weights = jnp.where(pixel_shift == offset, 1.0 - fraction, 0.0)
        weights = weights + jnp.where(pixel_shift + 1 == offset, fraction, 0.0)
        start_at = SHIFT + 1 + offset
        window = widened[..., start_at : start_at + TILE].astype(jnp.float32)
        pulled = pulled + jnp.sum(window * weights[None, :, :, :, None], axis=1)
    return pulled.reshape(2, rows_dev, tiles_dev * TILE)


def weigh_spectra(power_spectra, row_wave, col_wave, n):
    floored_wavenumber = 8.0 * math.pi / n
    weight = local_weight + 1.0 / (
        row_wave * row_wave + col_wave * col_wave + floored_wavenumber * floored_wavenumber
    )
    real_part = weight * (col_wave * power_spectra[1, 0] - row_wave * power_spectra[0, 0])
    imag_part = -weight * (col_wave * power_spectra[0, 0] + row_wave * power_spectra[1, 0])
    return jnp.stack([real_part, imag_part])


GROUP = 16
SLICES = 4
STEPS = tuple(range(-SHIFT, SHIFT + 2))
MATRIX_STEPS = (STEPS[0], STEPS[-1])
VMEM_LIMIT = 48 * 2**20


def turn(x, numerator, denominator):
    numerator %= denominator
    re, im = x
    if numerator == 0:
        return x
    if 4 * numerator == denominator:
        return (-im, re)
    if 2 * numerator == denominator:
        return (-re, -im)
    if 4 * numerator == 3 * denominator:
        return (im, -re)
    if 8 * numerator % denominator == 0:
        half = math.sqrt(0.5)
        a, b = half * re, half * im
        return {1: (a - b, a + b), 3: (-a - b, a - b), 5: (b - a, -a - b), 7: (a + b, b - a)}[
            8 * numerator // denominator
        ]
    angle = 2.0 * math.pi * numerator / denominator
    c, s = math.cos(angle), math.sin(angle)
    return (re * c - im * s, re * s + im * c)


def dft(xs, sign):
    n = len(xs)
    if n == 1:
        return xs
    even, odd = dft(xs[0::2], sign), dft(xs[1::2], sign)
    odd = [turn(x, sign * k, n) for k, x in enumerate(odd)]
    first = [(e[0] + o[0], e[1] + o[1]) for e, o in zip(even, odd)]
    second = [(e[0] - o[0], e[1] - o[1]) for e, o in zip(even, odd)]
    return first + second


def staged_dft(load, store, n, sign, hold):
    outer = 8 if n >= 32 else 2
    inner = n // outer
    for a in range(outer):
        ys = dft([load(a + outer * b) for b in range(inner)], sign)
        for k, y in enumerate(ys):
            re, im = turn(y, sign * a * k, n)
            hold[k * outer + a, 0] = re
            hold[k * outer + a, 1] = im
    for k in range(inner):
        zs = dft([(hold[k * outer + a, 0], hold[k * outer + a, 1]) for a in range(outer)], sign)
        for b, z in enumerate(zs):
            store(k + inner * b, z)


def split(x):
    high = x.astype(jnp.bfloat16)
    return high, (x - high.astype(jnp.float32)).astype(jnp.bfloat16)


def product(left, right):
    dot = lambda a, b: jnp.dot(a, b, preferred_element_type=jnp.float32)
    return dot(left[0], right[0]) + (dot(left[1], right[0]) + dot(left[0], right[1]))


LOG_STEP = math.log(2.0) / 1024.0
TOP = 32767.0


def scale_code(largest):
    return jnp.floor(jnp.log(jnp.maximum(largest, 1e-33)) / LOG_STEP).astype(jnp.int32) + 2


def unit_of(code):
    return jnp.exp(code.astype(jnp.float32) * LOG_STEP) * (1.0 / TOP)


def pack(first, second, code):
    inverse = 1.0 / unit_of(code)
    a, b = (
        jnp.clip(jnp.floor(x * inverse + 0.5), -TOP, TOP).astype(jnp.int32)
        for x in (first, second)
    )
    return (a << 16) | (b & 0xFFFF)


def unpack(packed, unit):
    first, second = packed >> 16, (packed << 16) >> 16
    return first.astype(jnp.float32) * unit, second.astype(jnp.float32) * unit


def largest_of(first, second, axis):
    return jnp.max(jnp.maximum(jnp.abs(first), jnp.abs(second)), axis=axis, keepdims=True)


def put_row(ref, where, row, value):
    old = ref[where]
    lane_row = lax.broadcasted_iota(jnp.int32, old.shape, old.ndim - 2)
    ref[where] = jnp.where(lane_row == row, value, jnp.where(row == 0, 0, old))


def take_row(tile, row):
    rows = lax.broadcasted_iota(jnp.int32, tile.shape, tile.ndim - 2)
    return jnp.sum(jnp.where(rows == row, tile, 0), axis=tile.ndim - 2, keepdims=True)


def scale_rows(count):
    return -(-count // 8) * 8


def halves(matrix):
    high = np.asarray(matrix, np.float32).astype(ml_dtypes.bfloat16)
    low = (np.asarray(matrix, np.float32) - high.astype(np.float32)).astype(ml_dtypes.bfloat16)
    return jnp.asarray(high), jnp.asarray(low)


def phases(product_of_indices, length):
    angle = 2.0 * np.pi * (np.asarray(product_of_indices) % length) / length
    return np.cos(angle), np.sin(angle)


class Plan:
    def __init__(self, devices):
        self.devices = devices
        self.tiles = 2 * devices
        n = self.n = TILE * self.tiles
        j = np.arange(TILE)
        c, s = phases(j[:, None] * j[None, :], TILE)
        back = TILE - 1 - j
        self.list_a = halves(np.block([[c, -s], [s, c]]))
        self.list_b = halves(np.block([[c[:, back], -s[:, back]], [s[:, back], c[:, back]]]))
        self.rows_forward = halves(np.block([[c, s], [-s, c]]))
        self.rows_inverse = halves(np.block([[c, -s], [s, c]]))
        scale = 1.0 / (2.0 * n * n)
        self.cols_inverse = halves(scale * np.block([[c, s], [-s, c]]))
        low = j < TILE // 2
        digit_a = np.where(low, j, j - TILE // 2)
        digit_b = np.where(low, np.where(j == 0, TILE // 2, TILE - j), TILE - 1 - (j - TILE // 2))
        ca, sa = phases(j[:, None] * digit_a[None, :], TILE)
        cb, sb = phases(j[:, None] * digit_b[None, :], TILE)
        blocks = []
        for mask in (low, ~low):
            blocks.append(np.concatenate([ca * mask, cb * mask, -sa * mask, -sb * mask], 1))
            blocks.append(np.concatenate([sa * mask, sb * mask, ca * mask, cb * mask], 1))
        self.special_forward = halves(np.concatenate(blocks, 0))
        freq = np.where(low, 0, devices) + self.tiles * digit_a
        ci, si = phases(freq[:, None] * j[None, :], n)
        first = np.concatenate([ci * low[:, None], ci * ~low[:, None]], 1)
        second = np.concatenate([-si * low[:, None], -si * ~low[:, None]], 1)
        second[0, :TILE] = 1.0 - 2.0 * (j % 2)
        second[0, TILE:] = 0.0
        self.special_inverse = halves(2.0 * scale * np.concatenate([first, second], 0))
        beta = np.arange(self.tiles)
        tc, ts = phases(beta[:, None] * j[None, :], n)
        self.col_twiddle = jnp.asarray(np.stack([tc, ts]), jnp.float32)
        self.row_twiddle = jnp.asarray(np.stack([tc.T, ts.T]), jnp.float32)
        self.low = low
        self.digit_a, self.digit_b = digit_a, digit_b

    def wave_of_lists(self, place):
        j = jnp.arange(TILE, dtype=jnp.int32)
        usual = place + self.tiles * j
        other = jnp.asarray(np.where(self.low, 0, self.devices) + self.tiles * self.digit_a, jnp.int32)
        other_b = (self.n - other) % self.n
        other_b = other_b.at[0].set(self.n // 2)
        a = jnp.where(place == 0, other, usual)
        b = jnp.where(place == 0, other_b, (self.n - usual) % self.n)
        return signed_wave(jnp.concatenate([a, b]), self.n).reshape(1, 2 * TILE)


def whole(shape):
    return pl.BlockSpec(shape, lambda *_: (0,) * len(shape))


def params():
    return pltpu.CompilerParams(vmem_limit_bytes=VMEM_LIMIT)


def remap_kernel(
    coded, group, last, half_ref, above_ref, here_ref, below_ref, edge_ref, slopes_ref, source_ref,
    row_ref, pixel_ref, fraction_ref, moves_ref, past_ref, out_ref, window, picker, picked, moved,
):
    tiles = slopes_ref.shape[2] // TILE
    span = 2 * GROUP
    count = PAIRS * tiles * GROUP
    here = group(pl.program_id(0), pl.program_id(1), half_ref)
    upper = lax.broadcasted_iota(jnp.int32, (GROUP, TILE), 0) < GROUP // 2

    def fill(after_ref, before_ref):
        for t in range(tiles):
            cols = slice(t * TILE, (t + 1) * TILE)
            for p in range(2):
                lanes = slice(p * TILE, (p + 1) * TILE)
                window[t * span : t * span + GROUP, lanes] = here_ref[p, :, cols]
                window[t * span + GROUP : (t + 1) * span, lanes] = jnp.where(
                    upper, after_ref[p, :, cols], before_ref[p, :, cols]
                )

    @pl.when((here > 0) & (here < last))
    def _():
        fill(below_ref, above_ref)

    @pl.when(here == 0)
    def _():
        fill(below_ref, edge_ref)

    @pl.when(here == last)
    def _():
        fill(edge_ref, above_ref)

    lane = lax.broadcasted_iota(jnp.int32, (GROUP, TILE), 1)
    down = lax.broadcasted_iota(jnp.int32, (GROUP, tiles), 0)
    per = TILE // span
    for k in range(PAIRS):
        source = source_ref[k]
        place = (source % per) * span + ((down + row_ref[k]) & (span - 1))
        block = source // per
        for t in range(tiles):
            here = slice((k * tiles + t) * GROUP, (k * tiles + t + 1) * GROUP)
            hit = jnp.where(place[:, t : t + 1] == lane, 1.0, 0.0).astype(jnp.bfloat16)
            blk = jnp.broadcast_to(block[:, t : t + 1], (GROUP, TILE))
            blk = blk.astype(jnp.float32).astype(jnp.bfloat16)
            for c in range(tiles * span // TILE):
                picker[here, c * TILE : (c + 1) * TILE] = jnp.where(
                    blk == jnp.bfloat16(c), hit, jnp.bfloat16(0)
                )
    picked[...] = jnp.dot(picker[...], window[...], preferred_element_type=jnp.float32)
    for p in range(2):
        moved[p * count : (p + 1) * count, :] = jnp.dot(
            picked[:, p * TILE : (p + 1) * TILE].astype(jnp.bfloat16), moves_ref[...],
            preferred_element_type=jnp.float32,
        )
    for t in range(tiles):
        pulled = [None, None]
        for k in range(PAIRS):
            row0 = (k * tiles + t) * GROUP
            move = jnp.broadcast_to(pixel_ref[k][:, t : t + 1], (GROUP, TILE))
            blend = jnp.broadcast_to(fraction_ref[k][:, t : t + 1], (GROUP, TILE))
            rest = 1.0 - blend
            same = [move == step for step in STEPS[:-2]]
            for p in range(2):
                here = slice(p * count + row0, p * count + row0 + GROUP)
                tile = picked[row0 : row0 + GROUP, p * TILE : (p + 1) * TILE]
                part = []
                for step in STEPS:
                    if step == 0:
                        part.append(tile)
                    elif step in MATRIX_STEPS:
                        i = MATRIX_STEPS.index(step)
                        part.append(moved[here, i * TILE : (i + 1) * TILE])
                    else:
                        inside = (lane + step >= 0) & (lane + step < TILE)
                        part.append(jnp.where(inside, pltpu.roll(tile, -step % TILE, 1), 0.0))
                near, far = part[-2], part[-1]
                for i in range(len(STEPS) - 2):
                    near = jnp.where(same[i], part[i], near)
                    far = jnp.where(same[i], part[i + 1], far)
                term = rest * near + blend * far
                pulled[p] = term if pulled[p] is None else pulled[p] + term
        cols = slice(t * TILE, (t + 1) * TILE)
        slopes = [slopes_ref[i, :, cols].astype(jnp.float32) for i in range(4)]
        across = -(pulled[0] * slopes[0] + pulled[1] * slopes[1])
        downward = -(pulled[0] * slopes[2] + pulled[1] * slopes[3])
        if coded:
            code = scale_code(largest_of(across, downward, 0))
            step = pl.program_id(0) * pl.num_programs(1) + pl.program_id(1)
            at = pl.ds(pl.multiple_of(step * GROUP, GROUP), GROUP)
            out_ref[at, cols] = pack(across, downward, code)
            put_row(out_ref, (slice(-8, None), cols), step, code)
        else:
            out_ref[0, :, cols] = across
            out_ref[1, :, cols] = downward


def remap_flow(
    half, part, parts, coded, past, residual, edge, slopes, source, row_shift, pixel_shift, fraction
):
    rows, cols = slopes.shape[1:]
    tiles = cols // TILE
    run = TILE // parts
    steps = run // GROUP
    half_groups = rows // 2 // GROUP

    def group(l, i, half_ref):
        return half_ref[0] * half_groups + l * (TILE // GROUP) + part * steps + i

    last = rows // GROUP - 1
    here = lambda l, i, half_ref: (0, group(l, i, half_ref), 0)
    before = lambda l, i, half_ref: (0, jnp.maximum(group(l, i, half_ref) - 1, 0), 0)
    after = lambda l, i, half_ref: (0, jnp.minimum(group(l, i, half_ref) + 1, last), 0)
    j = np.arange(TILE)
    moves = np.concatenate([j[:, None] == j[None, :] + step for step in MATRIX_STEPS], axis=1)
    small = pl.BlockSpec((PAIRS, GROUP, tiles), here)
    depth = 2 * GROUP * tiles
    count = PAIRS * GROUP * tiles
    runs = rows // 2 // TILE
    if coded:
        shape = (runs * run + scale_rows(runs * steps), cols)
        out = jax.ShapeDtypeStruct(shape, jnp.int32)
        out_spec = whole(shape)
    else:
        out = jax.ShapeDtypeStruct((2, runs * run, cols), jnp.float32)
        out_spec = pl.BlockSpec((2, GROUP, cols), lambda l, i, _: (0, l * steps + i, 0))
    return pl.pallas_call(
        partial(remap_kernel, coded, group, last),
        grid_spec=pltpu.PrefetchScalarGridSpec(
            num_scalar_prefetch=1,
            grid=(runs, steps),
            in_specs=[
                pl.BlockSpec((2, GROUP, cols), before),
                pl.BlockSpec((2, GROUP, cols), here),
                pl.BlockSpec((2, GROUP, cols), after),
                whole(edge.shape),
                pl.BlockSpec((4, GROUP, cols), here),
                small, small, small, small,
                whole(moves.shape),
                pl.BlockSpec(memory_space=pl.ANY),
            ],
            out_specs=out_spec,
            scratch_shapes=[
                pltpu.VMEM((depth, 2 * TILE), jnp.bfloat16),
                pltpu.VMEM((count, depth), jnp.bfloat16),
                pltpu.VMEM((count, 2 * TILE), jnp.float32),
                pltpu.VMEM((2 * count, len(MATRIX_STEPS) * TILE), jnp.float32),
            ],
        ),
        out_shape=out,
        compiler_params=params(),
        cost_estimate=pl.CostEstimate(
            flops=1000 if coded or part == 0 else 2 * 10**10, bytes_accessed=0, transcendentals=0
        ),
        name="remap",
    )(half, residual, residual, residual, edge, slopes, source, row_shift, pixel_shift, fraction,
      jnp.asarray(moves, jnp.bfloat16), past)


def cols_forward_kernel(
    sign_ref, own_ref, got_ref, code_ref, next_ref, twiddle_ref, a_high, a_low, b_high, b_low, s_high, s_low,
    out_ref, xa_high, xa_low, xb_high, xb_low, hold,
):
    devices, rows, _ = xa_high.shape
    total_rows = rows * pl.num_programs(0)
    now = pl.program_id(0)
    sign = sign_ref[0]

    def block(r, carry):
        at = pl.ds(pl.multiple_of(r * GROUP, GROUP), GROUP)

        def put(beta, z):
            tc, ts = twiddle_ref[0, beta : beta + 1, :], twiddle_ref[1, beta : beta + 1, :]
            re, im = z[0] * tc + z[1] * ts, z[1] * tc - z[0] * ts
            if beta < devices:
                slot, high, low = beta, xa_high, xa_low
            else:
                slot, high, low = (2 * devices - beta) % devices, xb_high, xb_low
            for i, value in enumerate((re, im)):
                h, l = split(value)
                high[slot, at, i * TILE : (i + 1) * TILE] = h
                low[slot, at, i * TILE : (i + 1) * TILE] = l

        def both(t):
            cols = slice(t * TILE, (t + 1) * TILE)
            unit = unit_of(take_row(code_ref[:, cols], now * (rows // GROUP) + r))
            got = unpack(got_ref[at, cols], unit)
            return [(own_ref[p, at, cols], got[p]) for p in range(2)]

        def total(t):
            return tuple(a + b for a, b in both(t))

        def gap(t):
            return turn(tuple((a - b) * sign for a, b in both(t)), -t, 2 * devices)

        staged_dft(total, lambda k, z: put(2 * k, z), devices, -1, hold)
        staged_dft(gap, lambda k, z: put(2 * k + 1, z), devices, -1, hold)
        return carry

    lax.fori_loop(0, rows // GROUP, block, 0)
    flat = (devices - 1) * rows

    def put_out(slots, which, re, im):
        code = scale_code(largest_of(re, im, 1))
        at = pl.ds(pl.multiple_of(which * total_rows + now * rows, GROUP), rows)
        out_ref[slots, at, :] = pack(re, im, code)
        put_row(out_ref, (slots, slice(-8, None)), 2 * now + which, code)

    for i, (high, low, mh, ml) in enumerate(
        ((xa_high, xa_low, a_high, a_low), (xb_high, xb_low, b_high, b_low))
    ):
        left = tuple(x[1:].reshape(flat, 2 * TILE) for x in (high, low))
        value = product(left, (mh[...], ml[...])).reshape(devices - 1, rows, 2 * TILE)
        put_out(slice(1, devices), i, value[:, :, :TILE], value[:, :, TILE:])
    left = tuple(
        jnp.concatenate([xa[0], xb[0]], axis=1)
        for xa, xb in ((xa_high, xb_high), (xa_low, xb_low))
    )
    value = product(left, (s_high[...], s_low[...])).reshape(1, rows, 4 * TILE)
    for i in range(2):
        put_out(
            slice(0, 1), i, value[:, :, i * TILE : (i + 1) * TILE],
            value[:, :, (i + 2) * TILE : (i + 3) * TILE],
        )


def cols_forward(plan, sign, own, got, later):
    rows, cols = own.shape[1:]
    d = plan.devices
    step = 2 * GROUP
    data = pl.BlockSpec((2, step, cols), lambda i: (0, i, 0))
    codes = got.shape[0] - rows
    shape = (d, 2 * rows + scale_rows(2 * rows // step), TILE)
    square = whole((2 * TILE, 2 * TILE))
    wide = whole((4 * TILE, 4 * TILE))
    return pl.pallas_call(
        cols_forward_kernel,
        grid=(rows // step,),
        in_specs=[
            pl.BlockSpec(memory_space=pltpu.SMEM), data,
            pl.BlockSpec((step, cols), lambda i: (i, 0)),
            pl.BlockSpec((codes, cols), lambda i: (rows // codes, 0)),
            pl.BlockSpec(memory_space=pl.ANY), whole(plan.col_twiddle.shape),
            square, square, square, square, wide, wide,
        ],
        out_specs=whole(shape),
        out_shape=jax.ShapeDtypeStruct(shape, jnp.int32),
        scratch_shapes=[pltpu.VMEM((d, step, 2 * TILE), jnp.bfloat16)] * 4
        + [pltpu.VMEM((d, 2, GROUP, TILE), jnp.float32)],
        compiler_params=params(),
        cost_estimate=pl.CostEstimate(
            flops=2 * 10**10, bytes_accessed=0, transcendentals=0
        ),
        name="cols_forward",
    )(sign, own, got, got, later, plan.col_twiddle, *plan.list_a, *plan.list_b, *plan.special_forward)


def rows_forward_kernel(
    run, a0_ref, a1_ref, b0_ref, b1_ref, code_ref, twiddle_ref, past_ref, out_ref, hold, unit
):
    tiles, step, lanes = out_ref.shape
    half = lanes // 2
    twiddle = (twiddle_ref[0], twiddle_ref[1])
    unit[...] = unit_of(code_ref[...])
    block = pl.program_id(0) * step // (2 * GROUP)

    def load(s):
        g, l = s // 2, s % 2
        at = 2 * (l * (run // (2 * GROUP)) + block)
        a = unpack((a0_ref, a1_ref)[l][g], take_row(unit[g], at))
        b = unpack((b0_ref, b1_ref)[l][g], take_row(unit[g], at + 1))
        return tuple(jnp.concatenate(pair, axis=1) for pair in zip(a, b))

    def store(k, z):
        tc, ts = twiddle[0][:, k : k + 1], twiddle[1][:, k : k + 1]
        out_ref[k, :, :half] = z[0] * tc + z[1] * ts
        out_ref[k, :, half:] = z[1] * tc - z[0] * ts

    staged_dft(load, store, tiles, -1, hold)


def rows_forward(plan, part, parts, x, past):
    d = plan.devices
    tiles = 2 * d
    run = TILE // parts
    lanes = 4 * TILE
    step = 8
    codes = x.shape[1] - 4 * run
    data = lambda k: pl.BlockSpec((d, step, TILE), lambda i: (0, k * (run // step) + i, 0))
    return pl.pallas_call(
        partial(rows_forward_kernel, run),
        grid=(run // step,),
        in_specs=[data(k) for k in range(4)]
        + [
            pl.BlockSpec((d, codes, TILE), lambda i: (0, 4 * run // codes, 0)),
            pl.BlockSpec((2, step, tiles), lambda i: (0, part * (run // step) + i, 0)),
            pl.BlockSpec(memory_space=pl.ANY),
        ],
        out_specs=pl.BlockSpec((tiles, step, lanes), lambda i: (0, i, 0)),
        out_shape=jax.ShapeDtypeStruct((tiles, run, lanes), jnp.float32),
        scratch_shapes=[
            pltpu.VMEM((tiles, 2, step, lanes // 2), jnp.float32),
            pltpu.VMEM((d, codes, TILE), jnp.float32),
        ],
        compiler_params=params(),
        cost_estimate=pl.CostEstimate(
            flops=128 * x.size, bytes_accessed=12 * x.size, transcendentals=0
        ),
        name="rows_forward",
    )(x, x, x, x, x, plan.row_twiddle, past)


def weigh_kernel(n, parts, *refs):
    x_refs = refs[:parts]
    f_high, f_low, g_high, g_low, wave_ref, out_ref = refs[parts:]
    batch, _, lanes = out_ref.shape
    half = lanes // 2
    tiles = n // TILE
    col_wave = wave_ref[...]
    floored = 8.0 * math.pi / n
    col_part = col_wave * col_wave + floored * floored
    digit = lax.broadcasted_iota(jnp.int32, (TILE, half), 0)
    for b in range(batch):
        x = jnp.concatenate(
            [r[b, :, :half] for r in x_refs] + [r[b, :, half:] for r in x_refs], axis=0
        )
        z = product((f_high[...], f_low[...]), split(x))
        row_wave = signed_wave(pl.program_id(0) * batch + b + tiles * digit, n)
        weight = local_weight + 1.0 / (row_wave * row_wave + col_part)
        re, im = z[:TILE], z[TILE:]
        z = jnp.concatenate(
            [weight * (col_wave * im - row_wave * re), -weight * (col_wave * re + row_wave * im)],
            axis=0,
        )
        y = product((g_high[...], g_low[...]), split(z))
        out_ref[b, :, :half] = y[:TILE]
        out_ref[b, :, half:] = y[TILE:]


def weigh(plan, wave, xs):
    tiles, rows, lanes = xs[0].shape
    parts = len(xs)
    batch = 8
    square = whole((2 * TILE, 2 * TILE))
    return pl.pallas_call(
        partial(weigh_kernel, plan.n, parts),
        grid=(tiles // batch,),
        in_specs=[pl.BlockSpec((batch, rows, lanes), lambda i: (i, 0, 0))] * parts
        + [square] * 4 + [whole(wave.shape)],
        out_specs=pl.BlockSpec((batch, parts * rows, lanes), lambda i: (i, 0, 0)),
        out_shape=jax.ShapeDtypeStruct((tiles, parts * rows, lanes), jnp.float32),
        compiler_params=params(),
        cost_estimate=pl.CostEstimate(
            flops=4096 * parts * xs[0].size, bytes_accessed=8 * parts * xs[0].size, transcendentals=0
        ),
        name="weigh",
    )(*xs, *plan.rows_forward, *plan.rows_inverse, wave)


def rows_inverse_kernel(run, x_ref, twiddle_ref, special_ref, past_ref, out_ref, hold, folded):
    tiles, step, lanes = x_ref.shape
    now = pl.program_id(0)
    half = lanes // 2
    twiddle = (twiddle_ref[0], twiddle_ref[1])
    special = special_ref[...] > 0.5

    def load(k):
        tc, ts = twiddle[0][:, k : k + 1], twiddle[1][:, k : k + 1]
        re, im = x_ref[k, :, :half], x_ref[k, :, half:]
        return re * tc - im * ts, im * tc + re * ts

    def store(s, z):
        re_a, re_b = z[0][:, :TILE], z[0][:, TILE:]
        im_a, im_b = z[1][:, :TILE], z[1][:, TILE:]
        folded[s, 0] = jnp.where(special, re_a, re_a + re_b)
        folded[s, 1] = jnp.where(special, re_b, im_a - im_b)

    staged_dft(load, store, tiles, 1, hold)
    for g in range(tiles // 2):
        re, im = folded[2 * g : 2 * g + 2, 0], folded[2 * g : 2 * g + 2, 1]
        code = scale_code(jnp.max(largest_of(re, im, 1), axis=0))
        for l in range(2):
            at = pl.ds(pl.multiple_of(l * run + now * step, 8), step)
            out_ref[g, at, :] = pack(re[l], im[l], code)
        put_row(out_ref, (g, slice(-8, None)), now, code)


def rows_inverse(plan, part, parts, special, x, past):
    tiles, rows, lanes = x.shape
    step = 8
    run = rows // parts // step
    shape = (tiles // 2, 2 * run * step + scale_rows(run), TILE)
    return pl.pallas_call(
        partial(rows_inverse_kernel, run * step),
        grid=(run,),
        in_specs=[
            pl.BlockSpec((tiles, step, lanes), lambda i: (0, part * run + i, 0)),
            pl.BlockSpec((2, step, tiles), lambda i: (0, part * run + i, 0)),
            whole(special.shape),
            pl.BlockSpec(memory_space=pl.ANY),
        ],
        out_specs=whole(shape),
        out_shape=jax.ShapeDtypeStruct(shape, jnp.int32),
        scratch_shapes=[
            pltpu.VMEM((tiles, 2, step, lanes // 2), jnp.float32),
            pltpu.VMEM((tiles, 2, step, TILE), jnp.float32),
        ],
        compiler_params=params(),
        cost_estimate=pl.CostEstimate(
            flops=1000, bytes_accessed=0, transcendentals=0
        ),
        name="rows_inverse",
    )(x, plan.row_twiddle, special, past)


def cols_inverse_kernel(
    col_ref, sign_ref, x_ref, code_ref, twiddle_ref, g_high, g_low, s_high, s_low, *rest,
):
    keep_ref, send_ref, spectrum, hold = rest[-4:]
    devices, rows, _ = x_ref.shape
    flat = (devices - 1) * rows
    per = pl.num_programs(1)
    for j in range(rows // 8):
        at = slice(8 * j, 8 * j + 8)
        unit = unit_of(take_row(code_ref[...], pl.program_id(1) * (rows // 8) + j))
        re, im = unpack(x_ref[:, at, :], unit)
        spectrum[:, at, :TILE] = re
        spectrum[:, at, TILE:] = im
    value = product(split(spectrum[1:].reshape(flat, 2 * TILE)), (g_high[...], g_low[...]))
    first = product(split(spectrum[0]), (s_high[...], s_low[...]))
    spectrum[1:] = value.reshape(devices - 1, rows, 2 * TILE)
    spectrum[0] = first
    sign = sign_ref[0]
    step = pl.program_id(0) * per + pl.program_id(1)

    def block(r, carry):
        at = pl.ds(pl.multiple_of(r * GROUP, GROUP), GROUP)

        def point(k):
            tc, ts = twiddle_ref[0, k : k + 1, :], twiddle_ref[1, k : k + 1, :]
            if k % 2:
                tc, ts = tc * sign, ts * sign
            re, im = spectrum[k, at, :TILE], spectrum[k, at, TILE:]
            return re * tc - im * ts, im * tc + re * ts

        def load(k):
            if k == 0:
                p, q = spectrum[0, at, :TILE], spectrum[0, at, TILE:]
                return p + q, p - q
            (a, b), (c, d) = point(k), point(devices - k)
            odd = turn((a - c, b + d), k, 2 * devices)
            return a + c - odd[1], b - d + odd[0]

        def store(n, z):
            if 2 * n < devices:
                for i in range(2):
                    keep_ref[at, (2 * n + i) * TILE : (2 * n + i + 1) * TILE] = z[i]
                return
            cols = slice((n - devices // 2) * TILE, (n - devices // 2 + 1) * TILE)
            code = scale_code(largest_of(z[0], z[1], 0))
            down = pl.ds(pl.multiple_of(step * rows + r * GROUP, GROUP), GROUP)
            send_ref[down, cols] = pack(z[0], z[1], code)
            put_row(send_ref, (slice(-8, None), cols), step * (rows // GROUP) + r, code)

        staged_dft(load, store, devices, 1, hold)
        return carry

    lax.fori_loop(0, rows // GROUP, block, 0)


def place_block(part, parts, half_rows, step):
    run = TILE // parts // step
    return lambda l, i, half_ref: (
        half_ref[0] * (half_rows // step) + l * (TILE // step) + part * run + i, 0
    )


def cols_inverse(plan, part, parts, half, sign, x, shape, image):
    d = plan.devices
    step = min(2 * GROUP, TILE // parts)
    runs = shape[0] // 2 // TILE
    rows = runs * TILE // parts
    codes = x.shape[1] - rows
    sent = (rows + scale_rows(rows // GROUP), shape[1] // 2)
    per = TILE // parts // step
    cols = shape[1]
    square = whole((2 * TILE, 2 * TILE))
    smem = pl.BlockSpec(memory_space=pltpu.SMEM)
    extra = [] if image is None else [image]
    return pl.pallas_call(
        cols_inverse_kernel,
        grid_spec=pltpu.PrefetchScalarGridSpec(
            num_scalar_prefetch=1,
            grid=(runs, per),
            in_specs=[
                smem, pl.BlockSpec((d, step, TILE), lambda l, i, _: (0, l * per + i, 0)),
                pl.BlockSpec((d, codes, TILE), lambda l, i, _: (0, rows // codes, 0)),
                whole(plan.col_twiddle.shape), square, square, square, square,
            ] + [pl.BlockSpec(memory_space=pl.ANY)] * len(extra),
            out_specs=[
                pl.BlockSpec((step, cols), place_block(part, parts, shape[0] // 2, step)),
                whole(sent),
            ],
            scratch_shapes=[
                pltpu.VMEM((d, step, 2 * TILE), jnp.float32),
                pltpu.VMEM((d, 2, GROUP, TILE), jnp.float32),
            ],
        ),
        out_shape=[
            jax.ShapeDtypeStruct(shape, jnp.float32),
            jax.ShapeDtypeStruct(sent, jnp.int32),
        ],
        input_output_aliases={9: 0} if extra else {},
        compiler_params=params(),
        cost_estimate=pl.CostEstimate(
            flops=2048 * x.size, bytes_accessed=8 * x.size, transcendentals=0
        ),
        name="cols_inverse",
    )(half, sign, x, x, plan.col_twiddle, *plan.cols_inverse, *plan.special_inverse, *extra)


def place_kernel(half_ref, got_ref, code_ref, image_ref, out_ref, token_ref):
    token_ref[...] = jnp.zeros_like(token_ref)
    rows, cols = got_ref.shape
    step = pl.program_id(0) * pl.num_programs(1) + pl.program_id(1)
    for r in range(rows // GROUP):
        at = slice(r * GROUP, (r + 1) * GROUP)
        for n in range(cols // TILE):
            lanes = slice(n * TILE, (n + 1) * TILE)
            unit = unit_of(take_row(code_ref[:, lanes], step * (rows // GROUP) + r))
            for i, value in enumerate(unpack(got_ref[at, lanes], unit)):
                out_ref[at, (2 * n + i) * TILE : (2 * n + i + 1) * TILE] = value


def place_rows(part, parts, half, got, image):
    cols = image.shape[1]
    step = min(2 * GROUP, TILE // parts)
    runs = image.shape[0] // 2 // TILE
    rows = runs * TILE // parts
    codes = got.shape[0] - rows
    per = TILE // parts // step
    return pl.pallas_call(
        place_kernel,
        grid_spec=pltpu.PrefetchScalarGridSpec(
            num_scalar_prefetch=1,
            grid=(runs, per),
            in_specs=[
                pl.BlockSpec((step, cols // 2), lambda l, i, _: (l * per + i, 0)),
                pl.BlockSpec((codes, cols // 2), lambda l, i, _: (rows // codes, 0)),
                pl.BlockSpec(memory_space=pl.ANY),
            ],
            out_specs=[
                pl.BlockSpec((step, cols), place_block(part, parts, image.shape[0] // 2, step)),
                whole((8, TILE)),
            ],
        ),
        out_shape=[
            jax.ShapeDtypeStruct(image.shape, jnp.float32),
            jax.ShapeDtypeStruct((8, TILE), jnp.float32),
        ],
        input_output_aliases={3: 0},
        compiler_params=params(),
        cost_estimate=pl.CostEstimate(flops=2 * 10**10, bytes_accessed=0, transcendentals=0),
        name="place_rows",
    )(half, got, got, image)


def paired(residual, field_slopes, source_tile, row_shift, pixel_shift, fraction):
    rows_dev, cols_dev = residual.shape[1:]
    devices = lax.axis_size("rows") * lax.axis_size("cols")
    plan = Plan(devices)
    parts = SLICES
    col = lax.axis_index("cols").astype(jnp.int32)
    place = lax.axis_index("rows").astype(jnp.int32) * 2 + col
    mine, other = col.reshape(1), (1 - col).reshape(1)
    sign = (1 - 2 * col).astype(jnp.float32).reshape(1)
    swap = [(0, 1), (1, 0)]
    both = ("rows", "cols")
    before = lax.ppermute(
        residual[:, rows_dev - HALO :], "rows", [(k, k + 1) for k in range(devices // 2 - 1)]
    )
    after = lax.ppermute(
        residual[:, :HALO], "rows", [(k + 1, k) for k in range(devices // 2 - 1)]
    )
    edge = jnp.concatenate([after, before], axis=1)
    args = (residual, edge, field_slopes, source_tile, row_shift, pixel_shift, fraction)
    lane = jnp.arange(TILE, dtype=jnp.int32).reshape(1, TILE)
    special = jnp.where((lane == 0) & (place == 0), 1.0, 0.0)
    wave = plan.wave_of_lists(place)
    spectra = []
    spectra, lists, aways, gots = [], [], [], []

    def send(m, past):
        aways.append(remap_flow(other, m, parts, True, past, *args))
        gots.append(lax.ppermute(aways[m], "cols", swap))

    send(0, special)
    if parts > 1:
        send(1, aways[0])
    for m in range(parts):
        past = gots[m] if m or parts == 1 else aways[1]
        own = remap_flow(mine, m, parts, False, past, *args)
        past = spectra[m - 2] if m > 1 else special
        lists.append(cols_forward(plan, sign, own, gots[m], past))
        if m + 2 < parts:
            send(m + 2, lists[m])
        swapped = lax.all_to_all(lists[m], both, split_axis=0, concat_axis=0, tiled=True)
        past = spectra[m - 1] if m else special
        spectra.append(rows_forward(plan, m, parts, swapped, past))
    mixed = weigh(plan, wave, spectra)
    image = None
    sent = []
    past = [special, special]
    for m in range(parts):
        folded = rows_inverse(plan, m, parts, special, mixed, past[m])
        folded = lax.all_to_all(folded, both, split_axis=0, concat_axis=0, tiled=True)
        if m > 1:
            image, token = place_rows(m - 2, parts, other, sent[m - 2], image)
            past.append(token)
        image, away = cols_inverse(
            plan, m, parts, mine, sign, folded, (rows_dev, cols_dev), image
        )
        if m == 0:
            past.append(away)
        sent.append(lax.ppermute(away, "cols", swap))
    for m in range(max(parts - 2, 0), parts):
        image, _ = place_rows(m, parts, other, sent[m], image)
    return image


def general(residual, field_slopes, source_tile, row_shift, pixel_shift, fraction):
    padded = with_halo(residual, (("rows", 1),), HALO)
    pulled = remap_tiles(padded, source_tile, row_shift, pixel_shift, fraction)
    slopes = field_slopes.astype(jnp.float32)
    flow_across = -(pulled[0] * slopes[0] + pulled[1] * slopes[1])
    downward_flow = -(pulled[0] * slopes[2] + pulled[1] * slopes[3])
    rows_dev = residual.shape[1]
    cols_dev = residual.shape[2]
    rows_count = lax.axis_size("rows")
    cols_count = lax.axis_size("cols")
    part_rows = rows_dev // cols_count
    n = rows_dev * rows_count
    spread = rows_count // cols_count
    col_index = lax.axis_index("cols")
    row_place = lax.axis_index("rows")
    compact_forward_transform = fourier_matrix(rows_count, -1)
    large_forward = fourier_matrix(rows_dev, -1)
    compact_inverse_transform = fourier_matrix(rows_count, 1)
    large_inverse = fourier_matrix(rows_dev, 1)
    wave_index = jnp.arange(rows_count, dtype=jnp.int32)
    pixel_index = jnp.arange(rows_dev, dtype=jnp.int32)
    band = col_index * part_rows + jnp.arange(part_rows, dtype=jnp.int32)
    stacked_planes = jnp.stack([flow_across, downward_flow]).reshape(2, rows_dev, 1, cols_dev)
    stacked_planes = across_columns(stacked_planes).reshape(2, part_rows, rows_count, rows_dev)
    power_spectra = contract_indices("pibc,pbqk->qikc", stacked_planes, compact_forward_transform)[
        :, None
    ]
    cosine, sine_part = phase_pair(wave_index[:, None] * pixel_index[None, :], n, -1)
    power_spectra = rotate(power_spectra, cosine, sine_part)
    power_spectra = contract_indices("pfikc,pcql->qfikl", power_spectra, large_forward)
    fields = power_spectra.shape[1]
    back_cos, back_sin = phase_pair(wave_index[:, None] * pixel_index[None, :], n, 1)
    power_spectra = across_rows(power_spectra)
    power_spectra = power_spectra.reshape(2, fields, rows_count, part_rows, rows_dev)
    power_spectra = contract_indices("pfrik,prqm->qfmik", power_spectra, compact_forward_transform)
    band_cos, band_sin = phase_pair(wave_index[:, None] * band[None, :], n, -1)
    power_spectra = rotate(power_spectra, band_cos[:, :, None], band_sin[:, :, None])
    power_spectra = across_columns(
        power_spectra.reshape(2 * fields, rows_count, part_rows, rows_dev)
    )
    power_spectra = power_spectra.reshape(2, fields, spread, rows_dev, rows_dev)
    power_spectra = contract_indices("pfmsk,psql->qfmlk", power_spectra, large_forward)
    row_freq = (
        rows_count * pixel_index[None, :]
        + (col_index * spread + jnp.arange(spread, dtype=jnp.int32))[:, None]
    )
    row_wave = signed_wave(row_freq, n)[:, :, None]
    col_wave = signed_wave(rows_count * pixel_index + row_place, n)
    mixed = weigh_spectra(power_spectra, row_wave, col_wave, n)
    mixed = contract_indices("pmlk,plqs->qsmk", mixed, large_inverse)
    mixed = across_columns(mixed)
    band_cos, band_sin = phase_pair(band[:, None] * wave_index[None, :], n, 1)
    mixed = rotate(mixed, band_cos[:, :, None], band_sin[:, :, None])
    mixed = contract_indices("pimk,pmqr->qirk", mixed, compact_inverse_transform)
    mixed = across_rows(mixed.reshape(2, 1, part_rows, rows_count, rows_dev))
    mixed = mixed.reshape(2, rows_count, part_rows, rows_dev)
    mixed = contract_indices("pnik,pkqa->qina", mixed, large_inverse)
    mixed = rotate(mixed, back_cos, back_sin)
    image = jnp.einsum(
        "pina,pnb->iba",
        mixed,
        compact_inverse_transform[:, :, 0, :],
        precision=highest,
        preferred_element_type=jnp.float32,
    )
    image = image.reshape(part_rows, cols_count, cols_dev) * (1.0 / (n * n))
    return lax.all_to_all(image, "cols", split_axis=1, concat_axis=0, tiled=True).reshape(
        rows_dev, cols_dev
    )


def per_device(*arrays):
    rows_dev, cols_dev = arrays[0].shape[1:]
    rows_count, cols_count = lax.axis_size("rows"), lax.axis_size("cols")
    devices = rows_count * cols_count
    if cols_count == 2 and rows_dev * rows_count == cols_dev * cols_count == 2 * TILE * devices:
        return paired(*arrays)
    return general(*arrays)


def solution(mesh):
    return jax.shard_map(
        per_device,
        mesh=mesh,
        in_specs=(
            P(None, "rows", "cols"),
            P(None, "rows", "cols"),
            P(None, "rows", "cols"),
            P(None, "rows", "cols"),
            P(None, "rows", "cols"),
            P(None, "rows", "cols"),
        ),
        out_specs=P("rows", "cols"),
        check_vma=False,
    )
```
